32 devices in a mesh: section: 4 (over x, core), space: 8 (over z, y).
Axes of the slice: x: 2, y: 2, z: 4, core: 2. Of those that a mesh axis runs over, the one named last changes fastest.
Arguments:
- volume: bfloat16 [4, 16, 8, 8, 64], P('section', 'space'), may hold values from -6 to 6
- w_first: bfloat16 [1728, 128], replicated, may hold values from -0.25 to 0.25
- w_enc: bfloat16 [3456, 128], replicated, may hold values from -0.1875 to 0.1875
- w_down: bfloat16 [1024, 256], replicated, may hold values from -0.25 to 0.25
- w_bottom: bfloat16 [6912, 256], replicated, may hold values from -0.125 to 0.125
- w_up: bfloat16 [256, 1024], replicated, may hold values from -0.375 to 0.375
- w_join: bfloat16 [6912, 128], replicated, may hold values from -0.125 to 0.125
- cotangent: bfloat16 [4, 16, 8, 8, 128], P('section', 'space'), may hold values from -6 to 6
Outputs:
- decoded: bfloat16 [4, 16, 8, 8, 128], P('section', 'space')
- grad_first: float32 [1728, 128], P(None, 'space')
- grad_enc: float32 [3456, 128], P(None, 'space')
- grad_down: float32 [1024, 256], P(None, 'space')
- grad_bottom: float32 [6912, 256], P(None, 'space')
- grad_up: float32 [256, 1024], P(None, 'space')
- grad_join: float32 [6912, 128], P(None, 'space')
The draws below stay inside these ranges and needn't reach their ends.
All inputs are finite; a program needn't handle non-finite values.
Results may differ from the reference program's by a relative error of at most 0.025.
Values may be sent and summed in bfloat16 or wider, within the bound.
No kernel may reach another device: no remote copies, remote signals or barrier semaphores. Data moves between devices by JAX's collectives and lax.ppermute only.
A program may use at most 128 MiB of HBM per device.

```python
import math
import jax
import jax.numpy as jnp
from jax import lax

C0 = 64
C1 = 128
C2 = 256
NY = 8
NZ = 8
CROPS = 4
NX = 16


def shard_levels(rng, shape, shards, low, high):
    loudness, own = 1.0, jax.random.fold_in(rng, 6)
    for position, blocks in shards:
        steps = jnp.exp(jax.random.uniform(jax.random.fold_in(own, position), (blocks,), jnp.float32, low / len(shards), high / len(shards)))
        loudness = loudness * jnp.repeat(steps, shape[position] // blocks).reshape([-1 if axis == position else 1 for axis in range(len(shape))])
    return loudness


def scatter_about(own_key, extent, scale, reach, pieces=(), kind=jnp.bfloat16):
    factor_of = shard_levels(own_key, extent, pieces, -0.22, 0.18) if pieces else 1.0
    values = jax.random.normal(own_key, extent, jnp.float32) * scale * factor_of
    return jnp.minimum(jnp.maximum(values, -reach), reach).astype(kind)


def setup_inputs(seed: int = 0) -> dict:
    key_of = jax.random.split(jax.random.key(seed), 9)
    volume = scatter_about(key_of[0], (CROPS, NX, NY, NZ, C0), 1.0, 6.0, ((0, 4), (1, 8)))
    w_first = scatter_about(key_of[1], (27 * C0, C1), (9 * C0) ** -0.5, 0.25)
    w_enc = scatter_about(key_of[2], (27 * C1, C1), (9 * C1) ** -0.5, 0.1875)
    w_down = scatter_about(key_of[3], (8 * C1, C2), (4 * C1) ** -0.5, 0.25)
    w_bottom = scatter_about(key_of[4], (27 * C2, C2), (9 * C2) ** -0.5, 0.125)
    w_up = scatter_about(key_of[5], (C2, 8 * C1), C2 ** -0.5, 0.375)
    w_join = scatter_about(key_of[6], (54 * C1, C1), (18 * C1) ** -0.5, 0.125)
    cotangent = scatter_about(key_of[7], (CROPS, NX, NY, NZ, C1), 1.0, 6.0, ((0, 4), (1, 8)))
    return {"volume": volume, "w_first": w_first, "w_enc": w_enc, "w_down": w_down, "w_bottom": w_bottom, "w_up": w_up, "w_join": w_join, "cotangent": cotangent}


def conv_full(field, weight):
    width_in = field.shape[-1]
    kernel = weight.reshape(3, 3, 3, width_in, weight.shape[-1])
    return lax.conv_general_dilated(field[None], kernel, (1, 1, 1), 'SAME', dimension_numbers=('NDHWC', 'DHWIO', 'NDHWC'), precision=lax.Precision.HIGHEST)[0]

def down_full(field, weight):
    size_x, size_y, size_z, width = field.shape
    blocks = field.reshape(size_x // 2, 2, size_y // 2, 2, size_z // 2, 2, width).transpose(0, 2, 4, 1, 3, 5, 6)
    blocks = blocks.reshape(size_x // 2, size_y // 2, size_z // 2, 8 * width)
    return jnp.dot(blocks, weight, precision=lax.Precision.HIGHEST)

def up_full(field, weight):
    size_x, size_y, size_z, wide = field.shape
    width = weight.shape[1] // 8
    spread = jnp.dot(field, weight, precision=lax.Precision.HIGHEST)
    spread = spread.reshape(size_x, size_y, size_z, 2, 2, 2, width).transpose(0, 3, 1, 4, 2, 5, 6)
    return spread.reshape(2 * size_x, 2 * size_y, 2 * size_z, width)

def silu_slope(pre):
    logistic = jax.nn.sigmoid(pre)
    return logistic * (1.0 + pre * (1.0 - logistic))

def rounded(value):
    return lax.optimization_barrier(value.astype(jnp.bfloat16)).astype(jnp.float32)

def layer(field, weight, action):
    pre = action(field.astype(jnp.float32), weight)
    return (pre, jax.nn.silu(pre).astype(jnp.bfloat16))

def reference(volume, w_first, w_enc, w_down, w_bottom, w_up, w_join, cotangent):
    weights = [item.astype(jnp.float32) for item in (w_first, w_enc, w_down, w_bottom, w_up, w_join)]
    f_first, f_enc, f_down, f_bottom, f_up, f_join = weights
    totals = [jnp.zeros(item.shape, jnp.float32) for item in weights]
    outputs = []
    for crop in range(CROPS):
        field = volume[crop]
        pre_first, act_first = layer(field, f_first, conv_full)
        pre_enc, skip_map = layer(act_first, f_enc, conv_full)
        pre_down, act_down = layer(skip_map, f_down, down_full)
        pre_bottom, act_bottom = layer(act_down, f_bottom, conv_full)
        lifted = up_full(act_bottom.astype(jnp.float32), f_up).astype(jnp.bfloat16)
        joined = jnp.concatenate([lifted, skip_map], axis=-1)
        pre_join, out_map = layer(joined, f_join, conv_full)
        outputs.append(out_map)
        step_join = rounded(cotangent[crop].astype(jnp.float32) * silu_slope(pre_join))
        unused, pull = jax.vjp(conv_full, joined.astype(jnp.float32), f_join)
        back, grad_w = pull(step_join)
        totals[5] = totals[5] + grad_w
        grad_lift = rounded(back[..., :C1])
        grad_skip = back[..., C1:]
        unused, pull = jax.vjp(up_full, act_bottom.astype(jnp.float32), f_up)
        back, grad_w = pull(grad_lift)
        totals[4] = totals[4] + grad_w
        step_bottom = rounded(rounded(back) * silu_slope(pre_bottom))
        unused, pull = jax.vjp(conv_full, act_down.astype(jnp.float32), f_bottom)
        back, grad_w = pull(step_bottom)
        totals[3] = totals[3] + grad_w
        step_down = rounded(rounded(back) * silu_slope(pre_down))
        unused, pull = jax.vjp(down_full, skip_map.astype(jnp.float32), f_down)
        back, grad_w = pull(step_down)
        totals[2] = totals[2] + grad_w
        step_enc = rounded((back + grad_skip) * silu_slope(pre_enc))
        unused, pull = jax.vjp(conv_full, act_first.astype(jnp.float32), f_enc)
        back, grad_w = pull(step_enc)
        totals[1] = totals[1] + grad_w
        step_first = rounded(rounded(back) * silu_slope(pre_first))
        unused, pull = jax.vjp(conv_full, field.astype(jnp.float32), f_first)
        back, grad_w = pull(step_first)
        totals[0] = totals[0] + grad_w
    factor = 1.0 / math.sqrt(CROPS * NX * NY * NZ)
    decoded = jnp.stack(outputs, 0)
    return (decoded, totals[0] * factor, totals[1] * factor, totals[2] * factor, totals[3] * factor, totals[4] * factor, totals[5] * factor)
```

```python
import functools
import math

import jax
import jax.numpy as jnp
import numpy as np
from jax import lax
from jax.experimental import pallas as pl
from jax.experimental.pallas import tpu as pltpu
from jax.sharding import PartitionSpec as P

BF = jnp.bfloat16
F32 = jnp.float32
LANES = 128


def dot(a, b):
    return jnp.dot(a, b, preferred_element_type=F32)


def dot_t(a, b):
    return lax.dot_general(a, b, (((1,), (1,)), ((), ())), preferred_element_type=F32)


def sigmoid(z):
    return 1.0 / (1.0 + jnp.exp(-z))


def silu(z):
    return (z * sigmoid(z)).astype(BF)


def slope(z):
    s = sigmoid(z)
    return s * (1.0 + z * (1.0 - s))


def windows(field, size_y, size_z):
    rows, width = field.shape
    place = lax.broadcasted_iota(jnp.int32, (rows, width), 0)
    at_z = lax.rem(place, size_z)
    at_y = lax.rem(lax.div(place, size_z), size_y)
    shifted = []
    for oz in (-1, 0, 1):
        part = field
        if oz:
            part = pltpu.roll(field, (-oz) % rows, 0)
            part = jnp.where(at_z == (size_z - 1 if oz > 0 else 0), 0.0, part)
        shifted.append(part)
    out = []
    for oy in (-1, 0, 1):
        for part in shifted:
            if oy:
                part = pltpu.roll(part, (-oy * size_z) % rows, 0)
                part = jnp.where(at_y == (size_y - 1 if oy > 0 else 0), 0.0, part)
            out.append(part)
    return out


def fill(u_ref, field, plane, sizes, offset=0, stride=None):
    rows, width = field.shape
    stride = width if stride is None else stride
    for t, part in enumerate(windows(field, *sizes)):
        lane = t * stride + offset
        u_ref[plane : plane + rows, lane : lane + width] = part.astype(BF)


def clear_rims(u_ref, plane):
    rows, lanes = u_ref.shape
    zero = jnp.zeros((plane, lanes), BF)
    u_ref[0:plane, :] = zero
    u_ref[rows - plane : rows, :] = zero


def conv(u_ref, w_ref, rows, plane):
    depth = u_ref.shape[1]
    total = None
    for ox in range(3):
        part = dot(u_ref[ox * plane : ox * plane + rows, :], w_ref[ox * depth : (ox + 1) * depth, :])
        total = part if total is None else total + part
    return total


def conv_back(u_ref, w_ref, rows, plane):
    width = w_ref.shape[0] // 27
    total = None
    for ox in range(3):
        taps = [(2 - ox) * 9 + 8 - t for t in range(9)]
        flipped = jnp.concatenate([w_ref[tap * width : (tap + 1) * width, :] for tap in taps], axis=1)
        part = dot_t(u_ref[ox * plane : ox * plane + rows, :], flipped)
        total = part if total is None else total + part
    return total


def own_rows(field, t_ref, count, position):
    t_ref[...] = field.T
    return t_ref[pl.ds(pl.multiple_of(position * count, count), count), :].astype(BF)


def to_blocks(shuffle, field, d_ref, pairs, plane):
    width = field.shape[1]
    for i in range(pairs):
        moved = dot(shuffle, field[i * 8 * plane : (i + 1) * 8 * plane]).astype(BF)
        for t in range(8):
            d_ref[i * plane : (i + 1) * plane, t * width : (t + 1) * width] = moved[
                t * plane : (t + 1) * plane
            ]


def from_blocks(unshuffle, flat, pairs, plane, width):
    parts = []
    for i in range(pairs):
        rows = flat[i * plane : (i + 1) * plane]
        stacked = jnp.concatenate([rows[:, t * width : (t + 1) * width] for t in range(8)], axis=0)
        parts.append(dot(unshuffle, stacked))
    return jnp.concatenate(parts, axis=0)


def step_kernel(
    geo,
    place_ref,
    near_ref,
    far_ref,
    shuffle_ref,
    unshuffle_ref,
    w_first,
    w_enc,
    w_down,
    w_bottom,
    w_up,
    w_join,
    decoded_ref,
    pack_ref,
    blocks,
    uv,
    u1,
    uj,
    ut,
    uc,
    utc,
    d_ref,
    lb_ref,
    wa,
    wb,
    out_map,
    tr_fine,
    tr_wide,
    tr_up,
    z1_ref,
    z2_ref,
):
    (n, sx, ny, nz, c0, c1, c2, masks, spots) = geo
    position = place_ref[0]
    plane, nx = ny * nz, sx * n
    rows = nx * plane
    cplane, cx = plane // 4, nx // 2
    crows = cx * cplane
    fine, coarse = (ny, nz), (ny // 2, nz // 2)
    half = n // 2 if n > 1 else 1
    for m, mask in enumerate(masks):
        source = near_ref if m < half else far_ref
        blocks[lax.bitwise_xor(position, mask)] = source[m % half]

    def emit(name, grad):
        at, _ = spots[name]
        count, width = grad.shape
        for v in range(0, width, LANES):
            piece = grad[:, v : v + LANES]
            if piece.shape[1] < LANES:
                piece = jnp.concatenate([piece, jnp.zeros((count, LANES - piece.shape[1]), F32)], 1)
            pack_ref[at : at + count, :] = piece.astype(BF)
            at += count

    lane = lax.broadcasted_iota(jnp.int32, (plane, LANES), 1)
    vol_rows = sx // 2 * plane
    pairs = [
        blocks[j, i * plane : (i + 1) * plane, :].astype(F32) for j in range(n) for i in range(sx // 2)
    ]
    turned = [pltpu.roll(p, c0, 1) for p in pairs]
    zero = jnp.zeros((plane, LANES), F32)
    beside = []
    for i in range(len(pairs) + 1):
        before = turned[i - 1] if i else zero
        after = turned[i] if i < len(pairs) else zero
        beside.append(jnp.where(lane < c0, before, after))
        if i < len(pairs):
            beside.append(pairs[i])
    fill(uv, jnp.concatenate(beside, 0), 0, fine)
    for t in range(9):
        a, b, c = [w_first[(ox * 9 + t) * c0 : (ox * 9 + t + 1) * c0, :] for ox in range(3)]
        wa[t * 2 * c0 : (t + 1) * 2 * c0, :] = jnp.concatenate([a, b], 0)
        wb[t * 2 * c0 : (t + 1) * 2 * c0, :] = jnp.concatenate([jnp.zeros_like(c), c], 0)
    z1 = dot(uv[0:rows, :], wa[...]) + dot(uv[plane : plane + rows, :], wb[...])
    z1_ref[...] = z1
    clear_rims(u1, plane)
    fill(u1, silu(z1).astype(F32), plane, fine)
    z2 = conv(u1, w_enc, rows, plane)
    z2_ref[...] = z2
    skip = silu(z2)
    clear_rims(uj, plane)
    fill(uj, skip.astype(F32), plane, fine, c1, 2 * c1)
    to_blocks(shuffle_ref[...], skip, d_ref, cx, cplane)
    z3 = dot(d_ref[...], w_down[...])
    clear_rims(uc, cplane)
    fill(uc, silu(z3).astype(F32), cplane, coarse)
    z4 = conv(uc, w_bottom, crows, cplane)
    g2 = silu(z4)
    lifted = from_blocks(unshuffle_ref[...], dot(g2, w_up[...]).astype(BF), cx, cplane, c1)
    fill(uj, lifted, plane, fine, 0, 2 * c1)
    z7 = conv(uj, w_join, rows, plane)
    out_map[...] = silu(z7)
    kept = sx * plane
    decoded_ref[...] = out_map[pl.ds(pl.multiple_of(position * kept, kept), kept), :]

    cot = jnp.concatenate([blocks[j, vol_rows:, :] for j in range(n)], 0).astype(F32)
    t7 = (cot * slope(z7)).astype(BF).astype(F32)
    clear_rims(ut, plane)
    fill(ut, t7, plane, fine)
    mine = own_rows(t7, tr_fine, c1 // n, position)
    depth = uj.shape[1]
    emit("join", jnp.concatenate([dot(mine, uj[ox * plane : ox * plane + rows, :]) for ox in range(3)], 1))
    b7 = conv_back(ut, w_join, rows, plane)
    e_lift = b7[:, :c1].astype(BF)
    e_skip = b7[:, c1:]

    to_blocks(shuffle_ref[...], e_lift, lb_ref, cx, cplane)
    mine = own_rows(lb_ref[...].astype(F32), tr_up, 8 * c1 // n, position)
    emit("up", dot(mine, g2))
    e3 = dot_t(lb_ref[...], w_up[...]).astype(BF).astype(F32)
    t4 = (e3 * slope(z4)).astype(BF).astype(F32)
    clear_rims(utc, cplane)
    fill(utc, t4, cplane, coarse)
    mine = own_rows(t4, tr_wide, c2 // n, position)
    emit("bottom", jnp.concatenate([dot(mine, uc[ox * cplane : ox * cplane + crows, :]) for ox in range(3)], 1))
    e4 = conv_back(utc, w_bottom, crows, cplane).astype(BF).astype(F32)
    t3 = (e4 * slope(z3)).astype(BF)
    mine = own_rows(t3.astype(F32), tr_wide, c2 // n, position)
    emit("down", dot(mine, d_ref[...]))
    e5 = dot_t(t3, w_down[...])
    high = e5.astype(BF)
    low = (e5 - high.astype(F32)).astype(BF)
    e5 = from_blocks(unshuffle_ref[...], high, cx, cplane, c1) + from_blocks(
        unshuffle_ref[...], low, cx, cplane, c1
    )
    t2 = ((e5 + e_skip) * slope(z2_ref[...])).astype(BF).astype(F32)
    fill(ut, t2, plane, fine)
    mine = own_rows(t2, tr_fine, c1 // n, position)
    emit("enc", jnp.concatenate([dot(mine, u1[ox * plane : ox * plane + rows, :]) for ox in range(3)], 1))
    e6 = conv_back(ut, w_enc, rows, plane).astype(BF).astype(F32)
    t1 = (e6 * slope(z1_ref[...])).astype(BF).astype(F32)
    mine = own_rows(t1, tr_fine, c1 // n, position)
    pair = dot(mine, uv[0:rows, :])
    last = dot(mine, uv[plane : plane + rows, :])
    halves = []
    for ox in range(3):
        for t in range(9):
            source = last if ox == 2 else pair
            halves.append((source[:, t * LANES : (t + 1) * LANES], ox > 0))
    if len(halves) % 2:
        halves.append((jnp.zeros_like(halves[0][0]), False))
    lane = lax.broadcasted_iota(jnp.int32, halves[0][0].shape, 1)
    packed = []
    for (a, a_high), (b, b_high) in zip(halves[::2], halves[1::2]):
        a = pltpu.roll(a, c0, 1) if a_high else a
        b = b if b_high else pltpu.roll(b, c0, 1)
        packed.append(jnp.where(lane < c0, a, b))
    emit("first", jnp.concatenate(packed, 1))


def finish_kernel(factor, order, spots, a_ref, b_ref, *outs):
    for name, out in zip(order, outs):
        at, _ = spots[name]
        count, width = out.shape
        for v in range(0, width, LANES):
            take = min(LANES, width - v)
            total = a_ref[at : at + count, :].astype(F32) + b_ref[at : at + count, :].astype(F32)
            out[:, v : v + take] = (total * factor)[:, :take]
            at += count


def exchange(array, axis, mask):
    devices = lax.axis_size(axis)
    return lax.ppermute(array, axis, [(i, i ^ mask) for i in range(devices)])


def one_hot_shuffle(ny, nz):
    plane = ny * nz
    shuffle = np.zeros((2 * plane, 2 * plane), np.float32)
    row = 0
    for ox in range(2):
        for oy in range(2):
            for oz in range(2):
                for y in range(ny // 2):
                    for z in range(nz // 2):
                        shuffle[row, ox * plane + (2 * y + oy) * nz + 2 * z + oz] = 1.0
                        row += 1
    return shuffle


def body(volume, w_first, w_enc, w_down, w_bottom, w_up, w_join, cotangent):
    n = lax.axis_size("space")
    crops = lax.axis_size("section")
    _, sx, ny, nz, c0 = volume.shape
    c1, c2 = w_enc.shape[1], w_bottom.shape[1]
    plane, nx = ny * nz, sx * n
    rows = nx * plane
    cplane, crows = plane // 4, rows // 8
    vol = volume.reshape(sx // 2, 2, plane, c0).transpose(0, 2, 1, 3).reshape(sx // 2 * plane, 2 * c0)
    near = jnp.concatenate([vol, cotangent.reshape(sx * plane, c1)], 0)[None]
    masks, step = [0], n // 2
    far = near
    while step:
        masks = masks + [m ^ step for m in masks]
        far = exchange(near, "space", step)
        step //= 2
        if step:
            near = jnp.concatenate([near, far], 0)

    order = ("first", "enc", "down", "bottom", "up", "join")
    shapes = {
        "first": (c1 // n, 27 * c0),
        "enc": (c1 // n, 27 * c1),
        "down": (c2 // n, 8 * c1),
        "bottom": (c2 // n, 27 * c2),
        "up": (8 * c1 // n, c2),
        "join": (c1 // n, 54 * c1),
    }
    spots, at = {}, 0
    for name in order:
        count, width = shapes[name]
        spots[name] = (at, count)
        at += count * -(-width // LANES)
    total_rows = -(-at // 32) * 32
    geo = (n, sx, ny, nz, c0, c1, c2, tuple(masks), spots)
    shuffle = one_hot_shuffle(ny, nz)
    position = lax.axis_index("space").astype(jnp.int32).reshape(1)
    whole = pl.BlockSpec(memory_space=pltpu.VMEM)
    decoded, pack = pl.pallas_call(
        functools.partial(step_kernel, geo),
        out_shape=(
            jax.ShapeDtypeStruct((sx * plane, c1), BF),
            jax.ShapeDtypeStruct((total_rows, LANES), BF),
        ),
        in_specs=[pl.BlockSpec(memory_space=pltpu.SMEM)] + [whole] * 10,
        out_specs=(whole, whole),
        scratch_shapes=[
            pltpu.VMEM((n,) + near.shape[1:], BF),
            pltpu.VMEM((rows + plane, 9 * 2 * c0), BF),
            pltpu.VMEM((rows + 2 * plane, 9 * c1), BF),
            pltpu.VMEM((rows + 2 * plane, 18 * c1), BF),
            pltpu.VMEM((rows + 2 * plane, 9 * c1), BF),
            pltpu.VMEM((crows + 2 * cplane, 9 * c2), BF),
            pltpu.VMEM((crows + 2 * cplane, 9 * c2), BF),
            pltpu.VMEM((crows, 8 * c1), BF),
            pltpu.VMEM((crows, 8 * c1), BF),
            pltpu.VMEM((18 * c0, c1), BF),
            pltpu.VMEM((18 * c0, c1), BF),
            pltpu.VMEM((rows, c1), BF),
            pltpu.VMEM((c1, rows), F32),
            pltpu.VMEM((c2, crows), F32),
            pltpu.VMEM((8 * c1, crows), F32),
            pltpu.VMEM((rows, c1), F32),
            pltpu.VMEM((rows, c1), F32),
        ],
        compiler_params=pltpu.CompilerParams(vmem_limit_bytes=58 * 1024 * 1024),
    )(
        position,
        near,
        far,
        jnp.asarray(shuffle, BF),
        jnp.asarray(shuffle.T, BF),
        w_first,
        w_enc,
        w_down,
        w_bottom,
        w_up,
        w_join,
    )
    mask = 1
    other = exchange(pack, "section", mask)
    while 2 * mask < crops:
        pack = (pack.astype(F32) + other.astype(F32)).astype(BF)
        mask *= 2
        other = exchange(pack, "section", mask)
    factor = 1.0 / math.sqrt(crops * rows)
    grads = pl.pallas_call(
        functools.partial(finish_kernel, factor, order, spots),
        out_shape=tuple(jax.ShapeDtypeStruct(shapes[name], F32) for name in order),
        in_specs=[whole, whole],
        out_specs=tuple(whole for _ in order),
        compiler_params=pltpu.CompilerParams(vmem_limit_bytes=40 * 1024 * 1024),
    )(pack, other)
    return (decoded.reshape((1, sx, ny, nz, c1)),) + tuple(g.T for g in grads)


def solution(mesh):
    field = P("section", "space", None, None, None)
    split = P(None, "space")
    return jax.shard_map(
        body,
        mesh=mesh,
        in_specs=(field,) + (P(),) * 6 + (field,),
        out_specs=(field,) + (split,) * 6,
        check_vma=False,
    )
```

```python
import functools
import math

import jax
import jax.numpy as jnp
import numpy as np
from jax import lax
from jax.experimental import pallas as pl
from jax.experimental.pallas import tpu as pltpu
from jax.sharding import PartitionSpec as P

BF = jnp.bfloat16
F32 = jnp.float32
LANES = 128
MIB = 1024 * 1024


def dot(a, b):
    return jnp.dot(a, b, preferred_element_type=F32)


def dot_t(a, b):
    return lax.dot_general(a, b, (((1,), (1,)), ((), ())), preferred_element_type=F32)


def sigmoid(z):
    return 1.0 / (1.0 + jnp.exp(-z))


def silu(z):
    return (z * sigmoid(z)).astype(BF)


def slope(z):
    s = sigmoid(z)
    return s * (1.0 + z * (1.0 - s))


def z_windows(field, size_z):
    rows = field.shape[0]
    at_z = lax.rem(lax.broadcasted_iota(jnp.int32, field.shape, 0), size_z)
    out = []
    for oz in (-1, 0, 1):
        part = field
        if oz:
            part = pltpu.roll(field, (-oz) % rows, 0)
            part = jnp.where(at_z == (size_z - 1 if oz > 0 else 0), 0.0, part)
        out.append(part)
    return out


def yz_windows(field, size_y, size_z):
    rows = field.shape[0]
    place = lax.broadcasted_iota(jnp.int32, field.shape, 0)
    at_y = lax.rem(lax.div(place, size_z), size_y)
    shifted = z_windows(field, size_z)
    out = []
    for oy in (-1, 0, 1):
        for part in shifted:
            if oy:
                part = pltpu.roll(part, (-oy * size_z) % rows, 0)
                part = jnp.where(at_y == (size_y - 1 if oy > 0 else 0), 0.0, part)
            out.append(part)
    return out


def fill(u_ref, parts, plane=0, offset=0, stride=None):
    rows, width = parts[0].shape
    stride = width if stride is None else stride
    for t, part in enumerate(parts):
        lane = t * stride + offset
        u_ref[plane : plane + rows, lane : lane + width] = part.astype(BF)


def clear_rims(u_ref, plane):
    rows, lanes = u_ref.shape
    zero = jnp.zeros((plane, lanes), BF)
    u_ref[0:plane, :] = zero
    u_ref[rows - plane : rows, :] = zero


def moved(field, ox, oy):
    nx, ny, nz, width = field.shape
    if ox:
        rim = jnp.zeros((1, ny, nz, width), F32)
        field = jnp.concatenate([field[1:], rim] if ox > 0 else [rim, field[:-1]], 0)
    if oy:
        rim = jnp.zeros((nx, 1, nz, width), F32)
        field = jnp.concatenate([field[:, 1:], rim] if oy > 0 else [rim, field[:, :-1]], 1)
    return field


def grouped(width, extent, product):
    total = None
    for first in range(0, 9, 2):
        groups = [first, first + 1] if first < 8 else [first]
        both = product(groups)
        for i, g in enumerate(groups):
            part = both[:, i * width : (i + 1) * width].reshape(extent + (width,))
            part = moved(part, g // 3 - 1, g % 3 - 1)
            total = part if total is None else total + part
    return total.reshape(-1, width)


def conv_z(uz, w_ref, extent):
    depth = w_ref.shape[0] // 9

    def product(groups):
        side = [w_ref[g * depth : (g + 1) * depth, :] for g in groups]
        return dot(uz, side[0] if len(side) == 1 else jnp.concatenate(side, 1))

    return grouped(w_ref.shape[1], extent, product)


def conv_z_back(uz, w_ref, extent):
    width = w_ref.shape[0] // 27

    def product(groups):
        side = []
        for g in groups:
            taps = [(8 - g) * 3 + 2 - t for t in range(3)]
            side.append(jnp.concatenate([w_ref[p * width : (p + 1) * width, :] for p in taps], 1))
        return dot_t(uz, side[0] if len(side) == 1 else jnp.concatenate(side, 0))

    return grouped(width, extent, product)


def conv(u_ref, w_ref, rows, plane):
    depth = u_ref.shape[1]
    total = None
    for ox in range(3):
        part = dot(u_ref[ox * plane : ox * plane + rows, :], w_ref[ox * depth : (ox + 1) * depth, :])
        total = part if total is None else total + part
    return total


def conv_back(u_ref, w_ref, rows, plane):
    width = w_ref.shape[0] // 27
    total = None
    for ox in range(3):
        taps = [(2 - ox) * 9 + 8 - t for t in range(9)]
        flipped = jnp.concatenate([w_ref[tap * width : (tap + 1) * width, :] for tap in taps], axis=1)
        part = dot_t(u_ref[ox * plane : ox * plane + rows, :], flipped)
        total = part if total is None else total + part
    return total


def own_columns(field, count, position):
    shape = (count, field.shape[1])
    wanted = lax.broadcasted_iota(jnp.int32, shape, 0) + position * count
    pick = (lax.broadcasted_iota(jnp.int32, shape, 1) == wanted).astype(F32).astype(BF)
    return dot_t(pick, field)


def tap_grad(grad, field, extent):
    nx, ny, nz = extent
    count, rows = grad.shape
    place = lax.broadcasted_iota(jnp.int32, grad.shape, 1)
    at = (lax.div(place, ny * nz), lax.rem(lax.div(place, nz), ny), lax.rem(place, nz))
    parts = []
    for ox in (-1, 0, 1):
        for oy in (-1, 0, 1):
            for oz in (-1, 0, 1):
                by = ((ox * ny) + oy) * nz + oz
                part = pltpu.roll(grad, by % rows, 1) if by else grad
                inside = None
                for index, size, o in zip(at, extent, (ox, oy, oz)):
                    if o:
                        here = index != (0 if o > 0 else size - 1)
                        inside = here if inside is None else inside & here
                parts.append(part if inside is None else jnp.where(inside, part, 0.0))
    return dot(jnp.concatenate(parts, 0).astype(BF), field)


def emit(pack_ref, spot, grad, taps=1):
    count, width = grad.shape[0] // taps, grad.shape[1]
    at = spot
    if width == LANES:
        pack_ref[at : at + taps * count, :] = grad.astype(BF)
        return
    for tap in range(taps):
        for v in range(0, width, LANES):
            pack_ref[at : at + count, :] = grad[tap * count : (tap + 1) * count, v : v + LANES].astype(BF)
            at += count


def to_blocks(shuffle, field, d_ref, pairs, plane):
    width = field.shape[1]
    for i in range(pairs):
        mixed = dot(shuffle, field[i * 8 * plane : (i + 1) * 8 * plane]).astype(BF)
        for t in range(8):
            d_ref[i * plane : (i + 1) * plane, t * width : (t + 1) * width] = mixed[
                t * plane : (t + 1) * plane
            ]


def from_blocks(unshuffle, flat, pairs, plane, width):
    parts = []
    for i in range(pairs):
        rows = flat[i * plane : (i + 1) * plane]
        stacked = jnp.concatenate([rows[:, t * width : (t + 1) * width] for t in range(8)], axis=0)
        parts.append(dot(unshuffle, stacked))
    return jnp.concatenate(parts, axis=0)


def upper_kernel(
    geo,
    place_ref,
    near_ref,
    far_ref,
    shuffle_ref,
    unshuffle_ref,
    w_first,
    w_enc,
    w_down,
    w_bottom,
    w_up,
    w_join,
    decoded_ref,
    keep_ref,
    send_ref,
    vol_ref,
    z1_ref,
    h1_ref,
    z2_ref,
    d_ref,
    z3_ref,
    t4_ref,
    skip_back_ref,
    blocks,
    uv,
    u1,
    uj,
    ut,
    uc,
    joined,
    lb_ref,
    out_map,
    pack,
):
    (n, sx, ny, nz, c0, c1, c2, masks, spots) = geo
    position = place_ref[0]
    plane, nx = ny * nz, sx * n
    rows = nx * plane
    cplane, cx = plane // 4, nx // 2
    crows = cx * cplane
    fine, coarse = (nx, ny, nz), (cx, ny // 2, nz // 2)
    half = n // 2 if n > 1 else 1
    for m, mask in enumerate(masks):
        source = near_ref if m < half else far_ref
        blocks[lax.bitwise_xor(position, mask)] = source[m % half]

    lane = lax.broadcasted_iota(jnp.int32, (plane, LANES), 1)
    vol_rows = sx // 2 * plane
    planes = []
    for j in range(n):
        for i in range(sx // 2):
            pair = blocks[j, i * plane : (i + 1) * plane, :].astype(F32)
            turned = pltpu.roll(pair, c0, 1)
            planes.append(jnp.where(lane < c0, pair, turned))
            planes.append(jnp.where(lane < c0, turned, pair))
    twice = jnp.concatenate(planes, 0)
    vol_ref[...] = twice.astype(BF)
    before, middle, after = z_windows(twice, nz)
    lane = lax.broadcasted_iota(jnp.int32, (rows, LANES), 1)
    uv[:, 0:LANES] = jnp.where(lane < c0, before, middle).astype(BF)
    uv[:, LANES:] = after.astype(BF)
    z1 = conv_z(uv[:, 0 : 3 * c0], w_first, fine)
    z1_ref[...] = z1
    h1 = silu(z1)
    h1_ref[...] = h1
    fill(u1, z_windows(h1.astype(F32), nz))
    z2 = conv_z(u1[...], w_enc, fine)
    z2_ref[...] = z2
    skip = silu(z2)
    joined[:, c1:] = skip
    fill(uj, z_windows(skip.astype(F32), nz), 0, c1, 2 * c1)
    to_blocks(shuffle_ref[...], skip, d_ref, cx, cplane)
    z3 = dot(d_ref[...], w_down[...])
    z3_ref[...] = z3
    g1 = silu(z3)
    clear_rims(uc, cplane)
    fill(uc, yz_windows(g1.astype(F32), *coarse[1:]), cplane)
    z4 = conv(uc, w_bottom, crows, cplane)
    g2 = silu(z4)
    lifted = from_blocks(unshuffle_ref[...], dot(g2, w_up[...]).astype(BF), cx, cplane, c1)
    joined[:, 0:c1] = lifted.astype(BF)
    fill(uj, z_windows(lifted, nz), 0, 0, 2 * c1)
    z7 = conv_z(uj[...], w_join, fine)
    out_map[...] = silu(z7)
    kept = sx * plane
    decoded_ref[...] = out_map[pl.ds(pl.multiple_of(position * kept, kept), kept), :]

    cot = jnp.concatenate([blocks[j, vol_rows:, :] for j in range(n)], 0).astype(F32)
    t7 = (cot * slope(z7)).astype(BF)
    clear_rims(ut, plane)
    fill(ut, yz_windows(t7.astype(F32), ny, nz), plane)
    emit(pack, spots["join"], tap_grad(own_columns(t7, c1 // n, position), joined[...], fine), 27)
    b7 = conv_back(ut, w_join, rows, plane)
    skip_back_ref[...] = b7[:, c1:]

    to_blocks(shuffle_ref[...], b7[:, :c1].astype(BF), lb_ref, cx, cplane)
    emit(pack, spots["up"], dot(own_columns(lb_ref[...], 8 * c1 // n, position).astype(BF), g2))
    e3 = dot_t(lb_ref[...], w_up[...]).astype(BF).astype(F32)
    t4 = (e3 * slope(z4)).astype(BF)
    t4_ref[...] = t4
    emit(pack, spots["bottom"], tap_grad(own_columns(t4, c2 // n, position), g1, coarse), 27)
    core = place_ref[1]
    size = keep_ref.shape[0]
    keep_ref[...] = pack[pl.ds(pl.multiple_of(core * size, size), size), :]
    send_ref[...] = pack[pl.ds(pl.multiple_of((1 - core) * size, size), size), :]


def lower_kernel(
    geo,
    place_ref,
    unshuffle_ref,
    w_enc,
    w_down,
    w_bottom,
    vol_ref,
    z1_ref,
    h1_ref,
    z2_ref,
    d_ref,
    z3_ref,
    t4_ref,
    skip_back_ref,
    pack,
    utc,
    ut,
):
    (n, sx, ny, nz, c0, c1, c2, masks, spots) = geo
    position = place_ref[0]
    plane, nx = ny * nz, sx * n
    cplane, cx = plane // 4, nx // 2
    crows = cx * cplane
    fine, coarse = (nx, ny, nz), (cx, ny // 2, nz // 2)
    clear_rims(utc, cplane)
    fill(utc, yz_windows(t4_ref[...].astype(F32), *coarse[1:]), cplane)
    e4 = conv_back(utc, w_bottom, crows, cplane).astype(BF).astype(F32)
    t3 = (e4 * slope(z3_ref[...])).astype(BF)
    emit(pack, spots["down"], dot(own_columns(t3, c2 // n, position).astype(BF), d_ref[...]))
    e5 = dot_t(t3, w_down[...])
    high = e5.astype(BF)
    low = (e5 - high.astype(F32)).astype(BF)
    e5 = from_blocks(unshuffle_ref[...], high, cx, cplane, c1) + from_blocks(
        unshuffle_ref[...], low, cx, cplane, c1
    )
    t2 = ((e5 + skip_back_ref[...]) * slope(z2_ref[...])).astype(BF)
    fill(ut, z_windows(t2.astype(F32), nz))
    emit(pack, spots["enc"], tap_grad(own_columns(t2, c1 // n, position), h1_ref[...], fine), 27)
    e6 = conv_z_back(ut[...], w_enc, fine).astype(BF).astype(F32)
    t1 = (e6 * slope(z1_ref[...])).astype(BF)
    count = c1 // n
    taps = tap_grad(own_columns(t1, count, position), vol_ref[...], fine)
    lane = lax.broadcasted_iota(jnp.int32, (count, LANES), 1)
    at = spots["first"]
    for tap in range(0, 27, 2):
        a = taps[tap * count : (tap + 1) * count]
        b = taps[(tap + 1) * count : (tap + 2) * count] if tap < 26 else a
        pack[at : at + count, :] = jnp.where(lane < c0, a, b).astype(BF)
        at += count


def unpack(source, spot, out, factor):
    count, width = out.shape
    at = spot
    for v in range(0, width, LANES):
        take = min(LANES, width - v)
        out[:, v : v + take] = (source(at, count) * factor)[:, :take]
        at += count


def finish_first(factor, spots, place_ref, mine_ref, other_ref, bottom_ref, up_ref, join_ref, both):
    core = place_ref[1]
    both[core] = mine_ref[...]
    both[1 - core] = other_ref[...]
    size = mine_ref.shape[0]

    def source(at, count):
        if (at + count - 1) // size == at // size:
            return both[at // size, at % size : at % size + count, :].astype(F32)
        cut = size - at % size
        return jnp.concatenate(
            [both[0, size - cut : size, :].astype(F32), both[1, 0 : count - cut, :].astype(F32)], 0
        )

    unpack(source, spots["bottom"], bottom_ref, factor)
    unpack(source, spots["join"], join_ref, factor)
    rows, width = up_ref.shape[1], up_ref.shape[0]
    for v in range(0, width, LANES):
        up_ref[v : v + LANES, :] = (source(spots["up"] + v // LANES * rows, rows) * factor).T


def finish_second(factor, spots, a_ref, b_ref, first_ref, enc_ref, down_ref):
    def source(at, count):
        return a_ref[at : at + count, :].astype(F32) + b_ref[at : at + count, :].astype(F32)

    unpack(source, spots["first"], first_ref, factor)
    unpack(source, spots["enc"], enc_ref, factor)
    unpack(source, spots["down"], down_ref, factor)


def exchange(array, axis, mask):
    devices = lax.axis_size(axis)
    return lax.ppermute(array, axis, [(i, i ^ mask) for i in range(devices)])


def add(a, b):
    return (a.astype(F32) + b.astype(F32)).astype(BF)


def one_hot_shuffle(ny, nz):
    plane = ny * nz
    shuffle = np.zeros((2 * plane, 2 * plane), np.float32)
    row = 0
    for ox in range(2):
        for oy in range(2):
            for oz in range(2):
                for y in range(ny // 2):
                    for z in range(nz // 2):
                        shuffle[row, ox * plane + (2 * y + oy) * nz + 2 * z + oz] = 1.0
                        row += 1
    return shuffle


def call(kernel, outs, scratch, scalars, flops=0, vmem=30):
    whole = pl.BlockSpec(memory_space=pltpu.VMEM)

    def run(*args):
        specs = [pl.BlockSpec(memory_space=pltpu.SMEM)] * scalars + [whole] * (len(args) - scalars)
        return pl.pallas_call(
            kernel,
            out_shape=tuple(jax.ShapeDtypeStruct(s, d) for s, d in outs),
            in_specs=specs,
            out_specs=tuple(whole for _ in outs),
            scratch_shapes=[pltpu.VMEM(s, d) for s, d in scratch],
            compiler_params=pltpu.CompilerParams(vmem_limit_bytes=vmem * MIB),
            cost_estimate=pl.CostEstimate(flops=flops, bytes_accessed=2 * MIB, transcendentals=0),
        )(*args)

    return run


def body(volume, w_first, w_enc, w_down, w_bottom, w_up, w_join, cotangent):
    n = lax.axis_size("space")
    crops = lax.axis_size("section")
    _, sx, ny, nz, c0 = volume.shape
    c1, c2 = w_enc.shape[1], w_bottom.shape[1]
    plane, nx = ny * nz, sx * n
    rows = nx * plane
    cplane, crows = plane // 4, rows // 8
    vol = volume.reshape(sx // 2, 2, plane, c0).transpose(0, 2, 1, 3).reshape(sx // 2 * plane, 2 * c0)
    near = jnp.concatenate([vol, cotangent.reshape(sx * plane, c1)], 0)[None]
    masks, step = [0], n // 2
    far = near
    while step:
        masks = masks + [m ^ step for m in masks]
        far = exchange(near, "space", step)
        step //= 2
        if step:
            near = jnp.concatenate([near, far], 0)

    fine_own, wide_own = c1 // n, c2 // n
    shapes = {
        "first": (fine_own, 27 * c0),
        "enc": (fine_own, 27 * c1),
        "down": (wide_own, 8 * c1),
        "bottom": (wide_own, 27 * c2),
        "up": (8 * c1 // n, c2),
        "join": (fine_own, 54 * c1),
    }

    def layout(names):
        spots, at = {}, 0
        for name in names:
            spots[name] = at
            count, width = shapes[name]
            at += count * -(-width // LANES)
        return spots, -(-at // 32) * 32

    upper_spots, upper_rows = layout(("bottom", "up", "join"))
    lower_spots, lower_rows = layout(("down", "enc", "first"))
    geo = (n, sx, ny, nz, c0, c1, c2, tuple(masks))
    shuffle = one_hot_shuffle(ny, nz)
    unshuffle = jnp.asarray(shuffle.T, BF)
    shuffle = jnp.asarray(shuffle, BF)
    section = lax.axis_index("section")
    place = jnp.stack([lax.axis_index("space"), section % 2]).astype(jnp.int32)
    size = upper_rows // 2
    decoded, keep, send, vol2, z1, h1, z2, blocks, z3, t4, skip_back = call(
        functools.partial(upper_kernel, geo + (upper_spots,)),
        [
            ((sx * plane, c1), BF),
            ((size, LANES), BF),
            ((size, LANES), BF),
            ((rows, 2 * c0), BF),
            ((rows, c1), F32),
            ((rows, c1), BF),
            ((rows, c1), F32),
            ((crows, 8 * c1), BF),
            ((crows, c2), F32),
            ((crows, c2), BF),
            ((rows, c1), F32),
        ],
        [
            ((n,) + near.shape[1:], BF),
            ((rows, 2 * LANES), BF),
            ((rows, 3 * c1), BF),
            ((rows, 6 * c1), BF),
            ((rows + 2 * plane, 9 * c1), BF),
            ((crows + 2 * cplane, 9 * c2), BF),
            ((rows, 2 * c1), BF),
            ((crows, 8 * c1), BF),
            ((rows, c1), BF),
            ((upper_rows, LANES), BF),
        ],
        1,
        flops=10**10,
    )(place, near, far, shuffle, unshuffle, w_first, w_enc, w_down, w_bottom, w_up, w_join)
    total = add(keep, exchange(send, "section", 1))
    mask = 2
    while mask < crops:
        total = add(total, exchange(total, "section", mask))
        mask *= 2
    other = exchange(total, "section", 1)

    (pack,) = call(
        functools.partial(lower_kernel, geo + (lower_spots,)),
        [((lower_rows, LANES), BF)],
        [((crows + 2 * cplane, 9 * c2), BF), ((rows, 3 * c1), BF)],
        1,
        flops=6 * 10**9,
    )(place, unshuffle, w_enc, w_down, w_bottom, vol2, z1, h1, z2, blocks, z3, t4, skip_back)
    mask = 1
    pack_other = exchange(pack, "section", mask)
    while 2 * mask < crops:
        pack = add(pack, pack_other)
        mask *= 2
        pack_other = exchange(pack, "section", mask)

    factor = 1.0 / math.sqrt(crops * rows)
    grad_bottom, grad_up, grad_join = call(
        functools.partial(finish_first, factor, upper_spots),
        [(shapes["bottom"], F32), (shapes["up"][::-1], F32), (shapes["join"], F32)],
        [((2, size, LANES), BF)],
        1,
    )(place, total, other)
    grad_first, grad_enc, grad_down = call(
        functools.partial(finish_second, factor, lower_spots),
        [(shapes[name], F32) for name in ("first", "enc", "down")],
        [],
        0,
    )(pack, pack_other)
    return (
        decoded.reshape((1, sx, ny, nz, c1)),
        grad_first.T,
        grad_enc.T,
        grad_down.T,
        grad_bottom.T,
        grad_up,
        grad_join.T,
    )


def solution(mesh):
    field = P("section", "space", None, None, None)
    split = P(None, "space")
    return jax.shard_map(
        body,
        mesh=mesh,
        in_specs=(field,) + (P(),) * 6 + (field,),
        out_specs=(field,) + (split,) * 6,
        check_vma=False,
    )
```

```python
import functools
import math

import jax
import jax.numpy as jnp
from jax import lax
from jax.experimental import pallas as pl
from jax.experimental.pallas import tpu as pltpu
from jax.sharding import PartitionSpec as P

BF = jnp.bfloat16
F32 = jnp.float32
LANES = 128
MIB = 1024 * 1024
VMEM = pltpu.MemorySpace.VMEM
SMEM = pltpu.MemorySpace.SMEM
HBM = pltpu.MemorySpace.HBM


def dot(a, b):
    return jnp.dot(a, b, preferred_element_type=F32)


def dot_t(a, b):
    return lax.dot_general(a, b, (((1,), (1,)), ((), ())), preferred_element_type=F32)


def sigmoid(z):
    return 1.0 / (1.0 + jnp.exp(-z))


def silu(z):
    return (z * sigmoid(z)).astype(BF)


def slope(z):
    s = sigmoid(z)
    return s * (1.0 + z * (1.0 - s))


def z_windows(field, size_z):
    rows = field.shape[0]
    at_z = lax.rem(lax.broadcasted_iota(jnp.int32, field.shape, 0), size_z)
    out = []
    for oz in (-1, 0, 1):
        part = field
        if oz:
            part = pltpu.roll(field, (-oz) % rows, 0)
            part = jnp.where(at_z == (size_z - 1 if oz > 0 else 0), 0.0, part)
        out.append(part)
    return out


def yz_windows(field, size_y, size_z):
    rows = field.shape[0]
    place = lax.broadcasted_iota(jnp.int32, field.shape, 0)
    at_y = lax.rem(lax.div(place, size_z), size_y)
    shifted = z_windows(field, size_z)
    out = []
    for oy in (-1, 0, 1):
        for part in shifted:
            if oy:
                part = pltpu.roll(part, (-oy * size_z) % rows, 0)
                part = jnp.where(at_y == (size_y - 1 if oy > 0 else 0), 0.0, part)
            out.append(part)
    return out


def fill(u_ref, parts, plane=0, offset=0, stride=None):
    rows, width = parts[0].shape
    stride = width if stride is None else stride
    for t, part in enumerate(parts):
        lane = t * stride + offset
        u_ref[plane : plane + rows, lane : lane + width] = part.astype(BF)


def clear_rims(u_ref, plane):
    rows, lanes = u_ref.shape
    zero = jnp.zeros((plane, lanes), BF)
    u_ref[0:plane, :] = zero
    u_ref[rows - plane : rows, :] = zero


def moved(field, ox, oy):
    nx, ny, nz, width = field.shape
    if ox:
        rim = jnp.zeros((1, ny, nz, width), F32)
        field = jnp.concatenate([field[1:], rim] if ox > 0 else [rim, field[:-1]], 0)
    if oy:
        rim = jnp.zeros((nx, 1, nz, width), F32)
        field = jnp.concatenate([field[:, 1:], rim] if oy > 0 else [rim, field[:, :-1]], 1)
    return field


def grouped(width, extent, product):
    total = None
    for first in range(0, 9, 2):
        groups = [first, first + 1] if first < 8 else [first]
        both = product(groups)
        for i, g in enumerate(groups):
            part = both[:, i * width : (i + 1) * width].reshape(extent + (width,))
            part = moved(part, g // 3 - 1, g % 3 - 1)
            total = part if total is None else total + part
    return total.reshape(-1, width)


def conv_z(uz, w_ref, extent):
    depth = w_ref.shape[0] // 9

    def product(groups):
        side = [w_ref[g * depth : (g + 1) * depth, :] for g in groups]
        return dot(uz, side[0] if len(side) == 1 else jnp.concatenate(side, 1))

    return grouped(w_ref.shape[1], extent, product)


def conv_z_back(uz, w_ref, extent):
    width = w_ref.shape[0] // 27

    def product(groups):
        side = []
        for g in groups:
            taps = [(8 - g) * 3 + 2 - t for t in range(3)]
            side.append(jnp.concatenate([w_ref[p * width : (p + 1) * width, :] for p in taps], 1))
        return dot_t(uz, side[0] if len(side) == 1 else jnp.concatenate(side, 0))

    return grouped(width, extent, product)


def conv(u_ref, w_ref, rows, plane):
    depth = u_ref.shape[1]
    total = None
    for ox in range(3):
        part = dot(u_ref[ox * plane : ox * plane + rows, :], w_ref[ox * depth : (ox + 1) * depth, :])
        total = part if total is None else total + part
    return total


def conv_back(u_ref, w_ref, rows, plane):
    width = w_ref.shape[0] // 27
    total = None
    for ox in range(3):
        taps = [(2 - ox) * 9 + 8 - t for t in range(9)]
        flipped = jnp.concatenate([w_ref[tap * width : (tap + 1) * width, :] for tap in taps], axis=1)
        part = dot_t(u_ref[ox * plane : ox * plane + rows, :], flipped)
        total = part if total is None else total + part
    return total


def own_columns(field, count, position):
    shape = (count, field.shape[1])
    wanted = lax.broadcasted_iota(jnp.int32, shape, 0) + position * count
    pick = (lax.broadcasted_iota(jnp.int32, shape, 1) == wanted).astype(F32).astype(BF)
    return dot_t(pick, field)


def tap_grad(grad, field, extent):
    nx, ny, nz = extent
    count, rows = grad.shape
    place = lax.broadcasted_iota(jnp.int32, grad.shape, 1)
    at = (lax.div(place, ny * nz), lax.rem(lax.div(place, nz), ny), lax.rem(place, nz))
    parts = []
    for ox in (-1, 0, 1):
        for oy in (-1, 0, 1):
            for oz in (-1, 0, 1):
                by = ((ox * ny) + oy) * nz + oz
                part = pltpu.roll(grad, by % rows, 1) if by else grad
                inside = None
                for index, size, o in zip(at, extent, (ox, oy, oz)):
                    if o:
                        here = index != (0 if o > 0 else size - 1)
                        inside = here if inside is None else inside & here
                parts.append(part if inside is None else jnp.where(inside, part, 0.0))
    return dot(jnp.concatenate(parts, 0).astype(BF), field)


def emit(pack_ref, spot, grad, taps=1):
    count, width = grad.shape[0] // taps, grad.shape[1]
    at = spot
    if width == LANES:
        pack_ref[at : at + taps * count, :] = grad.astype(BF)
        return
    for tap in range(taps):
        for v in range(0, width, LANES):
            pack_ref[at : at + count, :] = grad[tap * count : (tap + 1) * count, v : v + LANES].astype(BF)
            at += count


def one_hot(ny, nz, back):
    plane = ny * nz
    shape = (2 * plane, 2 * plane)
    row = lax.broadcasted_iota(jnp.int32, shape, 1 if back else 0)
    column = lax.broadcasted_iota(jnp.int32, shape, 0 if back else 1)
    tap, at = lax.div(row, plane // 4), lax.rem(row, plane // 4)
    ox, oy, oz = lax.div(tap, 4), lax.rem(lax.div(tap, 2), 2), lax.rem(tap, 2)
    y, z = lax.div(at, nz // 2), lax.rem(at, nz // 2)
    wanted = ox * plane + (2 * y + oy) * nz + 2 * z + oz
    return (column == wanted).astype(F32).astype(BF)


def to_blocks(shuffle, field, d_ref, pairs, plane):
    width = field.shape[1]
    for i in range(pairs):
        mixed = dot(shuffle, field[i * 8 * plane : (i + 1) * 8 * plane]).astype(BF)
        for t in range(8):
            d_ref[i * plane : (i + 1) * plane, t * width : (t + 1) * width] = mixed[
                t * plane : (t + 1) * plane
            ]


def from_blocks(unshuffle, flat, pairs, plane, width):
    parts = []
    for i in range(pairs):
        rows = flat[i * plane : (i + 1) * plane]
        stacked = jnp.concatenate([rows[:, t * width : (t + 1) * width] for t in range(8)], axis=0)
        parts.append(dot(unshuffle, stacked))
    return jnp.concatenate(parts, axis=0)


def join_kernel(sx, plane, volume_hbm, cotangent_hbm, out_ref, volume_ref, arrived):
    first = pltpu.make_async_copy(volume_hbm, volume_ref, arrived.at[0])
    second = pltpu.make_async_copy(cotangent_hbm, out_ref.at[0, sx // 2 * plane :], arrived.at[1])
    first.start()
    second.start()
    first.wait()
    for i in range(sx // 2):
        pair = [volume_ref[2 * i + k].astype(F32) for k in range(2)]
        out_ref[0, i * plane : (i + 1) * plane, :] = jnp.concatenate(pair, 1).astype(BF)
    second.wait()


def stage_kernel(place_ref, near_ref, sources, *refs):
    del place_ref, near_ref
    *held, arrived = refs
    copies = [pltpu.make_async_copy(a, b, arrived.at[i]) for i, (a, b) in enumerate(zip(sources, held))]
    for copy in copies:
        copy.start()
    for copy in copies:
        copy.wait()


def upper_kernel(
    geo,
    place_ref,
    gathered,
    weights,
    decoded_ref,
    keep_ref,
    send_ref,
    vol_ref,
    z1_ref,
    h1_ref,
    z2_ref,
    d_ref,
    z3_ref,
    t4_ref,
    skip_back_ref,
    blocks,
    uv,
    u1,
    uj,
    ut,
    uc,
    joined,
    lb_ref,
    out_map,
    pack,
):
    (n, sx, ny, nz, c0, c1, c2, masks, spots) = geo
    position = place_ref[0]
    w_first, w_enc, w_down, w_bottom, w_up, w_join = weights
    shuffle, unshuffle = one_hot(ny, nz, False), one_hot(ny, nz, True)
    plane, nx = ny * nz, sx * n
    rows = nx * plane
    cplane, cx = plane // 4, nx // 2
    crows = cx * cplane
    fine, coarse = (nx, ny, nz), (cx, ny // 2, nz // 2)
    for source, held in zip(gathered, masks):
        for m, mask in enumerate(held):
            blocks[lax.bitwise_xor(position, mask)] = source[m]

    lane = lax.broadcasted_iota(jnp.int32, (plane, LANES), 1)
    vol_rows = sx // 2 * plane
    planes = []
    for j in range(n):
        for i in range(sx // 2):
            pair = blocks[j, i * plane : (i + 1) * plane, :].astype(F32)
            turned = pltpu.roll(pair, c0, 1)
            planes.append(jnp.where(lane < c0, pair, turned))
            planes.append(jnp.where(lane < c0, turned, pair))
    twice = jnp.concatenate(planes, 0)
    vol_ref[...] = twice.astype(BF)
    before, middle, after = z_windows(twice, nz)
    lane = lax.broadcasted_iota(jnp.int32, (rows, LANES), 1)
    uv[:, 0:LANES] = jnp.where(lane < c0, before, middle).astype(BF)
    uv[:, LANES:] = after.astype(BF)
    z1 = conv_z(uv[:, 0 : 3 * c0], w_first, fine)
    z1_ref[...] = z1
    h1 = silu(z1)
    h1_ref[...] = h1
    fill(u1, z_windows(h1.astype(F32), nz))
    z2 = conv_z(u1[...], w_enc, fine)
    z2_ref[...] = z2
    skip = silu(z2)
    joined[:, c1:] = skip
    fill(uj, z_windows(skip.astype(F32), nz), 0, c1, 2 * c1)
    to_blocks(shuffle, skip, d_ref, cx, cplane)
    z3 = dot(d_ref[...], w_down[...])
    z3_ref[...] = z3
    g1 = silu(z3)
    clear_rims(uc, cplane)
    fill(uc, yz_windows(g1.astype(F32), *coarse[1:]), cplane)
    z4 = conv(uc, w_bottom, crows, cplane)
    g2 = silu(z4)
    lifted = from_blocks(unshuffle, dot(g2, w_up[...]).astype(BF), cx, cplane, c1)
    joined[:, 0:c1] = lifted.astype(BF)
    fill(uj, z_windows(lifted, nz), 0, 0, 2 * c1)
    z7 = conv_z(uj[...], w_join, fine)
    out_map[...] = silu(z7)
    kept = sx * plane
    decoded_ref[...] = out_map[pl.ds(pl.multiple_of(position * kept, kept), kept), :]

    cot = jnp.concatenate([blocks[j, vol_rows:, :] for j in range(n)], 0).astype(F32)
    t7 = (cot * slope(z7)).astype(BF)
    clear_rims(ut, plane)
    fill(ut, yz_windows(t7.astype(F32), ny, nz), plane)
    emit(pack, spots["join"], tap_grad(own_columns(t7, c1 // n, position), joined[...], fine), 27)
    b7 = conv_back(ut, w_join, rows, plane)
    skip_back_ref[...] = b7[:, c1:]

    to_blocks(shuffle, b7[:, :c1].astype(BF), lb_ref, cx, cplane)
    emit(pack, spots["up"], dot(own_columns(lb_ref[...], 8 * c1 // n, position).astype(BF), g2))
    e3 = dot_t(lb_ref[...], w_up[...]).astype(BF).astype(F32)
    t4 = (e3 * slope(z4)).astype(BF)
    t4_ref[...] = t4
    emit(pack, spots["bottom"], tap_grad(own_columns(t4, c2 // n, position), g1, coarse), 27)
    core = place_ref[1]
    size = keep_ref.shape[0]
    keep_ref[...] = pack[pl.ds(pl.multiple_of(core * size, size), size), :]
    send_ref[...] = pack[pl.ds(pl.multiple_of((1 - core) * size, size), size), :]


def lower_kernel(
    geo,
    place_ref,
    w_enc,
    w_down,
    w_bottom,
    vol_ref,
    z1_ref,
    h1_ref,
    z2_ref,
    d_ref,
    z3_ref,
    t4_ref,
    skip_back_ref,
    pack,
    utc,
    ut,
):
    (n, sx, ny, nz, c0, c1, c2, masks, spots) = geo
    position = place_ref[0]
    plane, nx = ny * nz, sx * n
    cplane, cx = plane // 4, nx // 2
    crows = cx * cplane
    fine, coarse = (nx, ny, nz), (cx, ny // 2, nz // 2)
    unshuffle = one_hot(ny, nz, True)
    clear_rims(utc, cplane)
    fill(utc, yz_windows(t4_ref[...].astype(F32), *coarse[1:]), cplane)
    e4 = conv_back(utc, w_bottom, crows, cplane).astype(BF).astype(F32)
    t3 = (e4 * slope(z3_ref[...])).astype(BF)
    emit(pack, spots["down"], dot(own_columns(t3, c2 // n, position).astype(BF), d_ref[...]))
    e5 = dot_t(t3, w_down[...])
    high = e5.astype(BF)
    low = (e5 - high.astype(F32)).astype(BF)
    e5 = from_blocks(unshuffle, high, cx, cplane, c1) + from_blocks(
        unshuffle, low, cx, cplane, c1
    )
    t2 = ((e5 + skip_back_ref[...]) * slope(z2_ref[...])).astype(BF)
    fill(ut, z_windows(t2.astype(F32), nz))
    emit(pack, spots["enc"], tap_grad(own_columns(t2, c1 // n, position), h1_ref[...], fine), 27)
    e6 = conv_z_back(ut[...], w_enc, fine).astype(BF).astype(F32)
    t1 = (e6 * slope(z1_ref[...])).astype(BF)
    count = c1 // n
    taps = tap_grad(own_columns(t1, count, position), vol_ref[...], fine)
    lane = lax.broadcasted_iota(jnp.int32, (count, LANES), 1)
    at = spots["first"]
    for tap in range(0, 27, 2):
        a = taps[tap * count : (tap + 1) * count]
        b = taps[(tap + 1) * count : (tap + 2) * count] if tap < 26 else a
        pack[at : at + count, :] = jnp.where(lane < c0, a, b).astype(BF)
        at += count


def unpack(source, spot, out, factor):
    count, width = out.shape
    at = spot
    for v in range(0, width, LANES):
        take = min(LANES, width - v)
        out[:, v : v + take] = (source(at, count) * factor)[:, :take]
        at += count


def finish_first(factor, spots, place_ref, mine_ref, other_ref, bottom_ref, up_ref, join_ref, token, both):
    token[...] = jnp.zeros(token.shape, F32)
    core = place_ref[1]
    both[core] = mine_ref[...]
    both[1 - core] = other_ref[...]
    size = mine_ref.shape[0]

    def source(at, count):
        if (at + count - 1) // size == at // size:
            return both[at // size, at % size : at % size + count, :].astype(F32)
        cut = size - at % size
        return jnp.concatenate(
            [both[0, size - cut : size, :].astype(F32), both[1, 0 : count - cut, :].astype(F32)], 0
        )

    unpack(source, spots["bottom"], bottom_ref, factor)
    unpack(source, spots["join"], join_ref, factor)
    rows, width = up_ref.shape[1], up_ref.shape[0]
    for v in range(0, width, LANES):
        up_ref[v : v + LANES, :] = (source(spots["up"] + v // LANES * rows, rows) * factor).T


def finish_second(factor, spots, earlier, a_ref, b_ref, first_ref, enc_ref, down_ref):
    del earlier

    def source(at, count):
        return a_ref[at : at + count, :].astype(F32) + b_ref[at : at + count, :].astype(F32)

    unpack(source, spots["first"], first_ref, factor)
    unpack(source, spots["enc"], enc_ref, factor)
    unpack(source, spots["down"], down_ref, factor)


def in_hbm(array):
    return pltpu.with_memory_space_constraint(array, HBM)


def exchange(array, axis, mask):
    devices = lax.axis_size(axis)
    return lax.ppermute(array, axis, [(i, i ^ mask) for i in range(devices)])


def add_kernel(a_ref, b_ref, out_ref):
    out_ref[...] = (a_ref[...].astype(F32) + b_ref[...].astype(F32)).astype(BF)


def add(a, b):
    return call(add_kernel, [(a.shape, BF)], [], (VMEM, VMEM), vmem=4)(a, b)[0]


def stack_kernel(a_ref, b_ref, out_ref):
    out_ref[0 : a_ref.shape[0]] = a_ref[...]
    out_ref[a_ref.shape[0] :] = b_ref[...]


def stack(a, b):
    shape = (a.shape[0] + b.shape[0],) + a.shape[1:]
    return call(stack_kernel, [(shape, BF)], [], (VMEM, VMEM), vmem=4)(a, b)[0]


def call(kernel, outs, scratch, spaces, flops=0, vmem=12):
    return pl.pallas_call(
        kernel,
        out_shape=tuple(jax.ShapeDtypeStruct(s, d) for s, d in outs),
        in_specs=jax.tree.map(lambda space: pl.BlockSpec(memory_space=space), spaces),
        out_specs=tuple(pl.BlockSpec(memory_space=VMEM) for _ in outs),
        scratch_shapes=scratch,
        compiler_params=pltpu.CompilerParams(vmem_limit_bytes=vmem * MIB),
        cost_estimate=pl.CostEstimate(flops=flops, bytes_accessed=2 * MIB, transcendentals=0),
    )


def body(volume, w_first, w_enc, w_down, w_bottom, w_up, w_join, cotangent):
    n = lax.axis_size("space")
    crops = lax.axis_size("section")
    _, sx, ny, nz, c0 = volume.shape
    c1, c2 = w_enc.shape[1], w_bottom.shape[1]
    plane, nx = ny * nz, sx * n
    rows = nx * plane
    cplane, crows = plane // 4, rows // 8
    section = lax.axis_index("section")
    place = jnp.stack([lax.axis_index("space"), section % 2]).astype(jnp.int32)
    own_rows = sx * plane // 2 + sx * plane
    (near,) = call(
        functools.partial(join_kernel, sx, plane),
        [((1, own_rows, LANES), BF)],
        [pltpu.VMEM((sx, plane, c0), BF), pltpu.SemaphoreType.DMA((2,))],
        (HBM, HBM),
        vmem=4,
    )(in_hbm(volume.reshape(sx, plane, c0)), in_hbm(cotangent.reshape(sx * plane, c1)))
    weights = [w_first, w_enc, w_down, w_bottom, w_up, w_join]
    stage = call(
        stage_kernel,
        [(w.shape, BF) for w in weights],
        [pltpu.SemaphoreType.DMA((len(weights),))],
        (SMEM, VMEM, [HBM] * len(weights)),
        flops=2 * 10**9,
        vmem=12,
    )
    weights = list(stage(place, near, [in_hbm(w) for w in weights]))
    held, step = [0], n // 2
    while step > 2:
        held = held + [m ^ step for m in held]
        near = stack(near, exchange(near, "space", step))
        step //= 2
    last = range(1, min(n, 4))
    gathered = [near] + [exchange(near, "space", mask) for mask in last]
    masks = tuple(tuple(m ^ mask for m in held) for mask in (0, *last))

    fine_own, wide_own = c1 // n, c2 // n
    shapes = {
        "first": (fine_own, 27 * c0),
        "enc": (fine_own, 27 * c1),
        "down": (wide_own, 8 * c1),
        "bottom": (wide_own, 27 * c2),
        "up": (8 * c1 // n, c2),
        "join": (fine_own, 54 * c1),
    }

    def layout(names):
        spots, at = {}, 0
        for name in names:
            spots[name] = at
            count, width = shapes[name]
            at += count * -(-width // LANES)
        return spots, -(-at // 32) * 32

    upper_spots, upper_rows = layout(("bottom", "up", "join"))
    lower_spots, lower_rows = layout(("down", "enc", "first"))
    geo = (n, sx, ny, nz, c0, c1, c2, masks)
    size = upper_rows // 2
    decoded, keep, send, vol2, z1, h1, z2, blocks, z3, t4, skip_back = call(
        functools.partial(upper_kernel, geo + (upper_spots,)),
        [
            ((sx * plane, c1), BF),
            ((size, LANES), BF),
            ((size, LANES), BF),
            ((rows, 2 * c0), BF),
            ((rows, c1), F32),
            ((rows, c1), BF),
            ((rows, c1), F32),
            ((crows, 8 * c1), BF),
            ((crows, c2), F32),
            ((crows, c2), BF),
            ((rows, c1), F32),
        ],
        [
            pltpu.VMEM((n, own_rows, LANES), BF),
            pltpu.VMEM((rows, 2 * LANES), BF),
            pltpu.VMEM((rows, 3 * c1), BF),
            pltpu.VMEM((rows, 6 * c1), BF),
            pltpu.VMEM((rows + 2 * plane, 9 * c1), BF),
            pltpu.VMEM((crows + 2 * cplane, 9 * c2), BF),
            pltpu.VMEM((rows, 2 * c1), BF),
            pltpu.VMEM((crows, 8 * c1), BF),
            pltpu.VMEM((rows, c1), BF),
            pltpu.VMEM((upper_rows, LANES), BF),
        ],
        (SMEM, [VMEM] * len(gathered), [VMEM] * len(weights)),
        flops=10**10,
        vmem=14,
    )(place, gathered, weights)
    total = add(keep, exchange(send, "section", 1))
    mask = 2
    while mask < crops:
        total = add(total, exchange(total, "section", mask))
        mask *= 2
    other = exchange(total, "section", 1)

    (pack,) = call(
        functools.partial(lower_kernel, geo + (lower_spots,)),
        [((lower_rows, LANES), BF)],
        [pltpu.VMEM((crows + 2 * cplane, 9 * c2), BF), pltpu.VMEM((rows, 3 * c1), BF)],
        (SMEM,) + (VMEM,) * 11,
        flops=6 * 10**9,
    )(place, *weights[1:4], vol2, z1, h1, z2, blocks, z3, t4, skip_back)
    mask = 1
    pack_other = exchange(pack, "section", mask)
    while 2 * mask < crops:
        pack = add(pack, pack_other)
        mask *= 2
        pack_other = exchange(pack, "section", mask)

    factor = 1.0 / math.sqrt(crops * rows)
    grad_bottom, grad_up, grad_join, token = call(
        functools.partial(finish_first, factor, upper_spots),
        [(shapes["bottom"], F32), (shapes["up"][::-1], F32), (shapes["join"], F32), ((8, LANES), F32)],
        [pltpu.VMEM((2, size, LANES), BF)],
        (SMEM, VMEM, VMEM),
        vmem=12,
    )(place, total, other)
    grad_first, grad_enc, grad_down = call(
        functools.partial(finish_second, factor, lower_spots),
        [(shapes[name], F32) for name in ("first", "enc", "down")],
        [],
        (VMEM, VMEM, VMEM),
        vmem=8,
    )(token, pack, pack_other)
    return (
        decoded.reshape((1, sx, ny, nz, c1)),
        grad_first.T,
        grad_enc.T,
        grad_down.T,
        grad_bottom.T,
        grad_up,
        grad_join.T,
    )


def solution(mesh):
    field = P("section", "space", None, None, None)
    split = P(None, "space")
    return jax.shard_map(
        body,
        mesh=mesh,
        in_specs=(field,) + (P(),) * 6 + (field,),
        out_specs=(field,) + (split,) * 6,
        check_vma=False,
    )
```

```python
import functools
import math

import jax
import jax.numpy as jnp
from jax import lax
from jax.experimental import pallas as pl
from jax.experimental.pallas import tpu as pltpu
from jax.sharding import PartitionSpec as P

BF = jnp.bfloat16
F32 = jnp.float32
LANES = 128
MIB = 1024 * 1024
VMEM = pltpu.MemorySpace.VMEM
HBM = pltpu.MemorySpace.HBM


def dot(a, b):
    return jnp.dot(a, b, preferred_element_type=F32)


def dot_t(a, b):
    return lax.dot_general(a, b, (((1,), (1,)), ((), ())), preferred_element_type=F32)


def sigmoid(z):
    return 1.0 / (1.0 + jnp.exp(-z))


def silu(z):
    return (z * sigmoid(z)).astype(BF)


def slope(z):
    s = sigmoid(z)
    return s * (1.0 + z * (1.0 - s))


def z_windows(field, size_z):
    rows = field.shape[0]
    at_z = lax.rem(lax.broadcasted_iota(jnp.int32, field.shape, 0), size_z)
    out = []
    for oz in (-1, 0, 1):
        part = field
        if oz:
            part = pltpu.roll(field, (-oz) % rows, 0)
            part = jnp.where(at_z == (size_z - 1 if oz > 0 else 0), 0.0, part)
        out.append(part)
    return out


def yz_windows(field, size_y, size_z):
    rows = field.shape[0]
    place = lax.broadcasted_iota(jnp.int32, field.shape, 0)
    at_y = lax.rem(lax.div(place, size_z), size_y)
    shifted = z_windows(field, size_z)
    out = []
    for oy in (-1, 0, 1):
        for part in shifted:
            if oy:
                part = pltpu.roll(part, (-oy * size_z) % rows, 0)
                part = jnp.where(at_y == (size_y - 1 if oy > 0 else 0), 0.0, part)
            out.append(part)
    return out


def fill(u_ref, parts, plane=0, offset=0, stride=None):
    rows, width = parts[0].shape
    stride = width if stride is None else stride
    for t, part in enumerate(parts):
        lane = t * stride + offset
        u_ref[plane : plane + rows, lane : lane + width] = part.astype(BF)


def clear_rims(u_ref, plane):
    rows, lanes = u_ref.shape
    zero = jnp.zeros((plane, lanes), BF)
    u_ref[0:plane, :] = zero
    u_ref[rows - plane : rows, :] = zero


def moved(field, ox, oy):
    nx, ny, nz, width = field.shape
    if ox:
        rim = jnp.zeros((1, ny, nz, width), F32)
        field = jnp.concatenate([field[1:], rim] if ox > 0 else [rim, field[:-1]], 0)
    if oy:
        rim = jnp.zeros((nx, 1, nz, width), F32)
        field = jnp.concatenate([field[:, 1:], rim] if oy > 0 else [rim, field[:, :-1]], 1)
    return field


def grouped(width, extent, product):
    total = None
    for first in range(0, 9, 2):
        groups = [first, first + 1] if first < 8 else [first]
        both = product(groups)
        for i, g in enumerate(groups):
            part = both[:, i * width : (i + 1) * width].reshape(extent + (width,))
            part = moved(part, g // 3 - 1, g % 3 - 1)
            total = part if total is None else total + part
    return total.reshape(-1, width)


def conv_z(uz, w_ref, extent):
    depth = w_ref.shape[0] // 9

    def product(groups):
        side = [w_ref[g * depth : (g + 1) * depth, :] for g in groups]
        return dot(uz, side[0] if len(side) == 1 else jnp.concatenate(side, 1))

    return grouped(w_ref.shape[1], extent, product)


def conv_z_back(uz, w_ref, extent, low=0, high=None):
    every = w_ref.shape[0] // 27
    high = every if high is None else high
    width = high - low

    def product(groups):
        side = []
        for g in groups:
            taps = [(8 - g) * 3 + 2 - t for t in range(3)]
            side.append(jnp.concatenate([w_ref[p * every + low : p * every + high, :] for p in taps], 1))
        return dot_t(uz, side[0] if len(side) == 1 else jnp.concatenate(side, 0))

    return grouped(width, extent, product)


def conv(u_ref, w_ref, rows, plane):
    depth = u_ref.shape[1]
    total = None
    for ox in range(3):
        part = dot(u_ref[ox * plane : ox * plane + rows, :], w_ref[ox * depth : (ox + 1) * depth, :])
        total = part if total is None else total + part
    return total


def conv_back(u_ref, w_ref, rows, plane):
    width = w_ref.shape[0] // 27
    total = None
    for ox in range(3):
        taps = [(2 - ox) * 9 + 8 - t for t in range(9)]
        flipped = jnp.concatenate([w_ref[tap * width : (tap + 1) * width, :] for tap in taps], axis=1)
        part = dot_t(u_ref[ox * plane : ox * plane + rows, :], flipped)
        total = part if total is None else total + part
    return total


def own_columns(field, count, position):
    shape = (count, field.shape[1])
    wanted = lax.broadcasted_iota(jnp.int32, shape, 0) + position * count
    pick = (lax.broadcasted_iota(jnp.int32, shape, 1) == wanted).astype(F32).astype(BF)
    return dot_t(pick, field)


def tap_shifts(grad, extent):
    nx, ny, nz = extent
    count, rows = grad.shape
    place = lax.broadcasted_iota(jnp.int32, grad.shape, 1)
    at = (lax.div(place, ny * nz), lax.rem(lax.div(place, nz), ny), lax.rem(place, nz))
    parts = []
    for ox in (-1, 0, 1):
        for oy in (-1, 0, 1):
            for oz in (-1, 0, 1):
                by = ((ox * ny) + oy) * nz + oz
                part = pltpu.roll(grad, by % rows, 1) if by else grad
                inside = None
                for index, size, o in zip(at, extent, (ox, oy, oz)):
                    if o:
                        here = index != (0 if o > 0 else size - 1)
                        inside = here if inside is None else inside & here
                parts.append(part if inside is None else jnp.where(inside, part, 0.0))
    return jnp.concatenate(parts, 0).astype(BF)


def tap_grad(grad, field, extent):
    return dot(tap_shifts(grad, extent), field)


def split(pack, keep_ref, send_ref, core):
    size = send_ref.shape[0]
    keep_ref[0:size, :] = pack[pl.ds(pl.multiple_of(core * size, size), size), :]
    send_ref[...] = pack[pl.ds(pl.multiple_of((1 - core) * size, size), size), :]


def emit(pack_ref, spot, grad, taps=1):
    count, width = grad.shape[0] // taps, grad.shape[1]
    at = spot
    if width == LANES:
        pack_ref[at : at + taps * count, :] = grad.astype(BF)
        return
    for tap in range(taps):
        for v in range(0, width, LANES):
            pack_ref[at : at + count, :] = grad[tap * count : (tap + 1) * count, v : v + LANES].astype(BF)
            at += count


def one_hot(ny, nz, back):
    plane = ny * nz
    shape = (2 * plane, 2 * plane)
    row = lax.broadcasted_iota(jnp.int32, shape, 1 if back else 0)
    column = lax.broadcasted_iota(jnp.int32, shape, 0 if back else 1)
    tap, at = lax.div(row, plane // 4), lax.rem(row, plane // 4)
    ox, oy, oz = lax.div(tap, 4), lax.rem(lax.div(tap, 2), 2), lax.rem(tap, 2)
    y, z = lax.div(at, nz // 2), lax.rem(at, nz // 2)
    wanted = ox * plane + (2 * y + oy) * nz + 2 * z + oz
    return (column == wanted).astype(F32).astype(BF)


def to_blocks(shuffle, field, d_ref, pairs, plane):
    width = field.shape[1]
    for i in range(pairs):
        mixed = dot(shuffle, field[i * 8 * plane : (i + 1) * 8 * plane]).astype(BF)
        for t in range(8):
            d_ref[i * plane : (i + 1) * plane, t * width : (t + 1) * width] = mixed[
                t * plane : (t + 1) * plane
            ]


def from_blocks(unshuffle, flat, pairs, plane, width):
    parts = []
    for i in range(pairs):
        rows = flat[i * plane : (i + 1) * plane]
        stacked = jnp.concatenate([rows[:, t * width : (t + 1) * width] for t in range(8)], axis=0)
        parts.append(dot(unshuffle, stacked))
    return jnp.concatenate(parts, axis=0)


def join_kernel(sx, plane, volume_hbm, cotangent_hbm, out_ref, volume_ref, arrived):
    first = pltpu.make_async_copy(volume_hbm, volume_ref, arrived.at[0])
    second = pltpu.make_async_copy(cotangent_hbm, out_ref.at[0, sx // 2 * plane :], arrived.at[1])
    first.start()
    second.start()
    first.wait()
    for i in range(sx // 2):
        pair = [volume_ref[2 * i + k].astype(F32) for k in range(2)]
        out_ref[0, i * plane : (i + 1) * plane, :] = jnp.concatenate(pair, 1).astype(BF)
    second.wait()


def stage_kernel(near_ref, sources, *refs):
    del near_ref
    *held, arrived = refs
    copies = [pltpu.make_async_copy(a, b, arrived.at[i]) for i, (a, b) in enumerate(zip(sources, held))]
    for copy in copies:
        copy.start()
    for copy in copies:
        copy.wait()


def upper_kernel(
    geo,
    gathered,
    weights,
    decoded_ref,
    keep_ref,
    send_ref,
    vol_ref,
    z1_ref,
    h1_ref,
    z2_ref,
    d_ref,
    z3_ref,
    t4_ref,
    ut,
    blocks,
    uv,
    u1,
    uj,
    uc,
    joined,
    lb_ref,
    out_map,
    pack,
):
    (n, sx, ny, nz, c0, c1, c2, masks, spots) = geo
    position = lax.axis_index("space")
    w_first, w_enc, w_down, w_bottom, w_up, w_join = weights
    shuffle, unshuffle = one_hot(ny, nz, False), one_hot(ny, nz, True)
    plane, nx = ny * nz, sx * n
    rows = nx * plane
    cplane, cx = plane // 4, nx // 2
    crows = cx * cplane
    fine, coarse = (nx, ny, nz), (cx, ny // 2, nz // 2)
    for source, held in zip(gathered, masks):
        for m, mask in enumerate(held):
            blocks[lax.bitwise_xor(position, mask)] = source[m]

    lane = lax.broadcasted_iota(jnp.int32, (plane, LANES), 1)
    vol_rows = sx // 2 * plane
    planes = []
    for j in range(n):
        for i in range(sx // 2):
            pair = blocks[j, i * plane : (i + 1) * plane, :].astype(F32)
            turned = pltpu.roll(pair, c0, 1)
            planes.append(jnp.where(lane < c0, pair, turned))
            planes.append(jnp.where(lane < c0, turned, pair))
    twice = jnp.concatenate(planes, 0)
    vol_ref[...] = twice.astype(BF)
    before, middle, after = z_windows(twice, nz)
    lane = lax.broadcasted_iota(jnp.int32, (rows, LANES), 1)
    uv[:, 0:LANES] = jnp.where(lane < c0, before, middle).astype(BF)
    uv[:, LANES:] = after.astype(BF)
    z1 = conv_z(uv[:, 0 : 3 * c0], w_first, fine)
    z1_ref[...] = z1
    h1 = silu(z1)
    h1_ref[...] = h1
    fill(u1, z_windows(h1.astype(F32), nz))
    z2 = conv_z(u1[...], w_enc, fine)
    z2_ref[...] = z2
    skip = silu(z2)
    joined[:, c1:] = skip
    fill(uj, z_windows(skip.astype(F32), nz), 0, c1, 2 * c1)
    to_blocks(shuffle, skip, d_ref, cx, cplane)
    z3 = dot(d_ref[...], w_down[...])
    z3_ref[...] = z3
    g1 = silu(z3)
    clear_rims(uc, cplane)
    fill(uc, yz_windows(g1.astype(F32), *coarse[1:]), cplane)
    z4 = conv(uc, w_bottom, crows, cplane)
    g2 = silu(z4)
    lifted = from_blocks(unshuffle, dot(g2, w_up[...]).astype(BF), cx, cplane, c1)
    joined[:, 0:c1] = lifted.astype(BF)
    fill(uj, z_windows(lifted, nz), 0, 0, 2 * c1)
    z7 = conv_z(uj[...], w_join, fine)
    out_map[...] = silu(z7)
    kept = sx * plane
    decoded_ref[...] = out_map[pl.ds(pl.multiple_of(position * kept, kept), kept), :]

    cot = jnp.concatenate([blocks[j, vol_rows:, :] for j in range(n)], 0).astype(F32)
    t7 = (cot * slope(z7)).astype(BF)
    fill(ut, z_windows(t7.astype(F32), nz))
    emit(pack, spots["join"], tap_grad(own_columns(t7, c1 // n, position), joined[...], fine), 27)
    e_lift = conv_z_back(ut[...], w_join, fine, 0, c1).astype(BF)
    to_blocks(shuffle, e_lift, lb_ref, cx, cplane)
    emit(pack, spots["up"], dot(own_columns(lb_ref[...], 8 * c1 // n, position).astype(BF), g2))
    e3 = dot_t(lb_ref[...], w_up[...]).astype(BF).astype(F32)
    t4 = (e3 * slope(z4)).astype(BF)
    t4_ref[...] = t4
    split(pack, keep_ref, send_ref, lax.rem(lax.axis_index("section"), 2))
    at = send_ref.shape[0]
    for v in range(0, c2, LANES):
        keep_ref[at : at + crows, :] = g1[:, v : v + LANES]
        at += crows
    mine = own_columns(t4, c2 // n, position).astype(BF)
    for v in range(0, crows, LANES):
        keep_ref[at : at + c2 // n, :] = mine[:, v : v + LANES]
        at += c2 // n


def skip_kernel(extent, c1, ut, w_join, out_ref):
    out_ref[...] = conv_z_back(ut[...], w_join, extent, c1, 2 * c1)


def lower_kernel(
    geo,
    w_enc,
    w_down,
    w_bottom,
    vol_ref,
    z1_ref,
    h1_ref,
    z2_ref,
    d_ref,
    z3_ref,
    t4_ref,
    skip_back_ref,
    keep_ref,
    send_ref,
    utc,
    ut,
    pack,
):
    (n, sx, ny, nz, c0, c1, c2, masks, spots) = geo
    position = lax.axis_index("space")
    plane, nx = ny * nz, sx * n
    cplane, cx = plane // 4, nx // 2
    crows = cx * cplane
    fine, coarse = (nx, ny, nz), (cx, ny // 2, nz // 2)
    unshuffle = one_hot(ny, nz, True)
    clear_rims(utc, cplane)
    fill(utc, yz_windows(t4_ref[...].astype(F32), *coarse[1:]), cplane)
    e4 = conv_back(utc, w_bottom, crows, cplane).astype(BF).astype(F32)
    t3 = (e4 * slope(z3_ref[...])).astype(BF)
    emit(pack, spots["down"], dot(own_columns(t3, c2 // n, position).astype(BF), d_ref[...]))
    e5 = dot_t(t3, w_down[...])
    high = e5.astype(BF)
    low = (e5 - high.astype(F32)).astype(BF)
    e5 = from_blocks(unshuffle, high, cx, cplane, c1) + from_blocks(
        unshuffle, low, cx, cplane, c1
    )
    t2 = ((e5 + skip_back_ref[...]) * slope(z2_ref[...])).astype(BF)
    fill(ut, z_windows(t2.astype(F32), nz))
    emit(pack, spots["enc"], tap_grad(own_columns(t2, c1 // n, position), h1_ref[...], fine), 27)
    e6 = conv_z_back(ut[...], w_enc, fine).astype(BF).astype(F32)
    t1 = (e6 * slope(z1_ref[...])).astype(BF)
    count = c1 // n
    taps = tap_grad(own_columns(t1, count, position), vol_ref[...], fine)
    lane = lax.broadcasted_iota(jnp.int32, (count, LANES), 1)
    at = spots["first"]
    for tap in range(0, 27, 2):
        a = taps[tap * count : (tap + 1) * count]
        b = taps[(tap + 1) * count : (tap + 2) * count] if tap < 26 else a
        pack[at : at + count, :] = jnp.where(lane < c0, a, b).astype(BF)
        at += count
    split(pack, keep_ref, send_ref, lax.rem(lax.axis_index("section"), 2))


def unpack(source, spot, out, factor):
    count, width = out.shape
    at = spot
    for v in range(0, width, LANES):
        take = min(LANES, width - v)
        out[:, v : v + take] = (source(at, count) * factor)[:, :take]
        at += count


def halves(both, mine_ref, other_ref, core):
    size = both.shape[1]
    both[core] = mine_ref[0:size, :]
    both[1 - core] = other_ref[0:size, :]

    def source(at, count):
        if (at + count - 1) // size == at // size:
            return both[at // size, at % size : at % size + count, :].astype(F32)
        cut = size - at % size
        return jnp.concatenate(
            [both[0, size - cut : size, :].astype(F32), both[1, 0 : count - cut, :].astype(F32)], 0
        )

    return source


def finish_first(
    factor, spots, extent, mine_ref, other_ref, bottom_ref, up_ref, join_ref, token, both, acts
):
    token[...] = jnp.zeros(token.shape, F32)
    section = lax.axis_index("section")
    size = both.shape[1]
    source = halves(both, mine_ref, other_ref, lax.rem(section, 2))
    unpack(source, spots["join"], join_ref, factor)
    rows, width = up_ref.shape[1], up_ref.shape[0]
    for v in range(0, width, LANES):
        up_ref[v : v + LANES, :] = (source(spots["up"] + v // LANES * rows, rows) * factor).T

    crops, each = acts.shape[0], acts.shape[1]
    for j in range(crops // 2):
        part = slice(size + j * each, size + (j + 1) * each)
        acts[lax.bitwise_xor(section, 2 * j)] = mine_ref[part, :]
        acts[lax.bitwise_xor(section, 2 * j + 1)] = other_ref[part, :]
    voxels = extent[0] * extent[1] * extent[2]
    count, wide = bottom_ref.shape[0], bottom_ref.shape[1] // 27
    shifted, fields = [], []
    for crop in range(crops):
        at = wide // LANES * voxels
        fields.append(
            jnp.concatenate([acts[crop, v : v + voxels, :] for v in range(0, at, voxels)], 1)
        )
        own = [acts[crop, v : v + count, :] for v in range(at, each, count)]
        shifted.append(tap_shifts(jnp.concatenate(own, 1).astype(F32), extent))
    grad = dot(jnp.concatenate(shifted, 1), jnp.concatenate(fields, 0)) * factor
    for tap in range(27):
        bottom_ref[:, tap * wide : (tap + 1) * wide] = grad[tap * count : (tap + 1) * count]


def finish_second(
    factor, spots, mine_ref, other_ref, first_ref, enc_ref, down_ref, both
):
    source = halves(both, mine_ref, other_ref, lax.rem(lax.axis_index("section"), 2))
    unpack(source, spots["first"], first_ref, factor)
    unpack(source, spots["enc"], enc_ref, factor)
    unpack(source, spots["down"], down_ref, factor)


def in_hbm(array):
    return pltpu.with_memory_space_constraint(array, HBM)


def exchange(array, axis, mask):
    devices = lax.axis_size(axis)
    return lax.ppermute(array, axis, [(i, i ^ mask) for i in range(devices)])


def merge_kernel(size, a_ref, b_ref, *refs):
    out_ref = refs[-1]
    out_ref[0:size, :] = (a_ref[0:size, :].astype(F32) + b_ref[0:size, :].astype(F32)).astype(BF)
    at = size
    for ref in (a_ref, b_ref):
        rest = ref.shape[0] - size
        if rest:
            out_ref[at : at + rest, :] = ref[size:, :]
            at += rest


def merge(a, b, size, *after):
    shape = (a.shape[0] + b.shape[0] - size, LANES)
    kernel = functools.partial(merge_kernel, size)
    return call(kernel, [(shape, BF)], [], (VMEM,) * (2 + len(after)), vmem=4)(a, b, *after)[0]


def between_cores(keep, send, *after):
    return merge(keep, exchange(send, "section", 1), send.shape[0], *after)


def between_chips(total, size, crops, *after):
    mask = 2
    while mask < crops:
        mask *= 2
        last = after if mask >= crops else ()
        total = merge(total, exchange(total, "section", mask // 2), size, *last)
    return total, exchange(total, "section", 1)


def in_hbm(array):
    return pltpu.with_memory_space_constraint(array, HBM)


def exchange(array, axis, mask):
    devices = lax.axis_size(axis)
    return lax.ppermute(array, axis, [(i, i ^ mask) for i in range(devices)])


def merge_kernel(size, a_ref, b_ref, *refs):
    out_ref = refs[-1]
    out_ref[0:size, :] = (a_ref[0:size, :].astype(F32) + b_ref[0:size, :].astype(F32)).astype(BF)
    at = size
    for ref in (a_ref, b_ref):
        rest = ref.shape[0] - size
        if rest:
            out_ref[at : at + rest, :] = ref[size:, :]
            at += rest


def merge(a, b, size, *after):
    shape = (a.shape[0] + b.shape[0] - size, LANES)
    kernel = functools.partial(merge_kernel, size)
    return call(kernel, [(shape, BF)], [], (VMEM,) * (2 + len(after)), vmem=4)(a, b, *after)[0]


def reduced(keep, send, crops, after=()):
    size = send.shape[0]
    total = merge(keep, exchange(send, "section", 1), size)
    mask = 2
    while mask < crops:
        mask *= 2
        total = merge(total, exchange(total, "section", mask // 2), size, *(after if mask >= crops else ()))
    return total, exchange(total, "section", 1)


def stack_kernel(a_ref, b_ref, out_ref):
    out_ref[0 : a_ref.shape[0]] = a_ref[...]
    out_ref[a_ref.shape[0] :] = b_ref[...]


def stack(a, b):
    shape = (a.shape[0] + b.shape[0],) + a.shape[1:]
    return call(stack_kernel, [(shape, BF)], [], (VMEM, VMEM), vmem=4)(a, b)[0]


def call(kernel, outs, scratch, spaces, flops=0, vmem=12):
    return pl.pallas_call(
        kernel,
        out_shape=tuple(jax.ShapeDtypeStruct(s, d) for s, d in outs),
        in_specs=jax.tree.map(lambda space: pl.BlockSpec(memory_space=space), spaces),
        out_specs=tuple(pl.BlockSpec(memory_space=VMEM) for _ in outs),
        scratch_shapes=scratch,
        compiler_params=pltpu.CompilerParams(vmem_limit_bytes=vmem * MIB),
        cost_estimate=pl.CostEstimate(flops=flops, bytes_accessed=2 * MIB, transcendentals=0),
    )


def body(volume, w_first, w_enc, w_down, w_bottom, w_up, w_join, cotangent):
    n = lax.axis_size("space")
    crops = lax.axis_size("section")
    _, sx, ny, nz, c0 = volume.shape
    c1, c2 = w_enc.shape[1], w_bottom.shape[1]
    plane, nx = ny * nz, sx * n
    rows = nx * plane
    cplane, crows = plane // 4, rows // 8
    own_rows = sx * plane // 2 + sx * plane
    (near,) = call(
        functools.partial(join_kernel, sx, plane),
        [((1, own_rows, LANES), BF)],
        [pltpu.VMEM((sx, plane, c0), BF), pltpu.SemaphoreType.DMA((2,))],
        (HBM, HBM),
        vmem=4,
    )(in_hbm(volume.reshape(sx, plane, c0)), in_hbm(cotangent.reshape(sx * plane, c1)))
    weights = [w_first, w_enc, w_down, w_bottom, w_up, w_join]
    stage = call(
        stage_kernel,
        [(w.shape, BF) for w in weights],
        [pltpu.SemaphoreType.DMA((len(weights),))],
        (VMEM, [HBM] * len(weights)),
        flops=2 * 10**9,
        vmem=12,
    )
    weights = list(stage(near, [in_hbm(w) for w in weights]))
    held, step = [0], n // 2
    while step > 2:
        held = held + [m ^ step for m in held]
        near = stack(near, exchange(near, "space", step))
        step //= 2
    last = range(1, min(n, 4))
    gathered = [near] + [exchange(near, "space", mask) for mask in last]
    masks = tuple(tuple(m ^ mask for m in held) for mask in (0, *last))

    fine_own, wide_own = c1 // n, c2 // n
    shapes = {
        "first": (fine_own, 27 * c0),
        "enc": (fine_own, 27 * c1),
        "down": (wide_own, 8 * c1),
        "bottom": (wide_own, 27 * c2),
        "up": (8 * c1 // n, c2),
        "join": (fine_own, 54 * c1),
    }

    def layout(names):
        spots, at = {}, 0
        for name in names:
            spots[name] = at
            count, width = shapes[name]
            at += count * -(-width // LANES)
        return spots, -(-at // 32) * 32

    upper_spots, upper_rows = layout(("up", "join"))
    lower_spots, lower_rows = layout(("down", "enc", "first"))
    geo = (n, sx, ny, nz, c0, c1, c2, masks)
    fine, coarse = (nx, ny, nz), (nx // 2, ny // 2, nz // 2)
    size = upper_rows // 2
    act_rows = c2 // LANES * crows + crows // LANES * wide_own
    decoded, keep, send, vol2, z1, h1, z2, blocks, z3, t4, ut = call(
        functools.partial(upper_kernel, geo + (upper_spots,)),
        [
            ((sx * plane, c1), BF),
            ((size + act_rows, LANES), BF),
            ((size, LANES), BF),
            ((rows, 2 * c0), BF),
            ((rows, c1), F32),
            ((rows, c1), BF),
            ((rows, c1), F32),
            ((crows, 8 * c1), BF),
            ((crows, c2), F32),
            ((crows, c2), BF),
            ((rows, 3 * c1), BF),
        ],
        [
            pltpu.VMEM((n, own_rows, LANES), BF),
            pltpu.VMEM((rows, 2 * LANES), BF),
            pltpu.VMEM((rows, 3 * c1), BF),
            pltpu.VMEM((rows, 6 * c1), BF),
            pltpu.VMEM((crows + 2 * cplane, 9 * c2), BF),
            pltpu.VMEM((rows, 2 * c1), BF),
            pltpu.VMEM((crows, 8 * c1), BF),
            pltpu.VMEM((rows, c1), BF),
            pltpu.VMEM((upper_rows, LANES), BF),
        ],
        ([VMEM] * len(gathered), [VMEM] * len(weights)),
        flops=10**10,
        vmem=14,
    )(gathered, weights)
    (skip_back,) = call(
        functools.partial(skip_kernel, fine, c1),
        [((rows, c1), F32)],
        [],
        (VMEM, VMEM),
        flops=10**9,
    )(ut, weights[5])
    total = between_cores(keep, send, skip_back)

    low_size = lower_rows // 2
    low_keep, low_send = call(
        functools.partial(lower_kernel, geo + (lower_spots,)),
        [((low_size, LANES), BF), ((low_size, LANES), BF)],
        [
            pltpu.VMEM((crows + 2 * cplane, 9 * c2), BF),
            pltpu.VMEM((rows, 3 * c1), BF),
            pltpu.VMEM((lower_rows, LANES), BF),
        ],
        (VMEM,) * 11,
        flops=6 * 10**9,
    )(*weights[1:4], vol2, z1, h1, z2, blocks, z3, t4, skip_back)
    total, other = between_chips(total, size, crops, low_send)

    factor = 1.0 / math.sqrt(crops * rows)
    grad_bottom, grad_up, grad_join, token = call(
        functools.partial(finish_first, factor, upper_spots, coarse),
        [
            (shapes["bottom"], F32),
            (shapes["up"][::-1], F32),
            (shapes["join"], F32),
            ((8, LANES), F32),
        ],
        [pltpu.VMEM((2, size, LANES), BF), pltpu.VMEM((crops, act_rows, LANES), BF)],
        (VMEM, VMEM),
        vmem=12,
    )(total, other)
    low_total = between_cores(low_keep, low_send)
    low_total, low_other = between_chips(low_total, low_size, crops, token)
    grad_first, grad_enc, grad_down = call(
        functools.partial(finish_second, factor, lower_spots),
        [(shapes[name], F32) for name in ("first", "enc", "down")],
        [pltpu.VMEM((2, low_size, LANES), BF)],
        (VMEM, VMEM),
        vmem=8,
    )(low_total, low_other)
    return (
        decoded.reshape((1, sx, ny, nz, c1)),
        grad_first.T,
        grad_enc.T,
        grad_down.T,
        grad_bottom.T,
        grad_up,
        grad_join.T,
    )


def solution(mesh):
    field = P("section", "space", None, None, None)
    split = P(None, "space")
    return jax.shard_map(
        body,
        mesh=mesh,
        in_specs=(field,) + (P(),) * 6 + (field,),
        out_specs=(field,) + (split,) * 6,
        check_vma=False,
    )
```

```python
import functools
import math

import jax
import jax.numpy as jnp
from jax import lax
from jax.experimental import pallas as pl
from jax.experimental.pallas import tpu as pltpu
from jax.sharding import PartitionSpec as P

BF = jnp.bfloat16
F32 = jnp.float32
LANES = 128
MIB = 1024 * 1024
VMEM = pltpu.MemorySpace.VMEM
HBM = pltpu.MemorySpace.HBM


def dot(a, b):
    return jnp.dot(a, b, preferred_element_type=F32)


def dot_t(a, b):
    return lax.dot_general(a, b, (((1,), (1,)), ((), ())), preferred_element_type=F32)


def sigmoid(z):
    return 1.0 / (1.0 + jnp.exp(-z))


def silu(z):
    return (z * sigmoid(z)).astype(BF)


def slope(z):
    s = sigmoid(z)
    return s * (1.0 + z * (1.0 - s))


def z_windows(field, size_z):
    rows = field.shape[0]
    at_z = lax.rem(lax.broadcasted_iota(jnp.int32, field.shape, 0), size_z)
    out = []
    for oz in (-1, 0, 1):
        part = field
        if oz:
            part = pltpu.roll(field, (-oz) % rows, 0)
            part = jnp.where(at_z == (size_z - 1 if oz > 0 else 0), 0.0, part)
        out.append(part)
    return out


def yz_windows(field, size_y, size_z):
    rows = field.shape[0]
    place = lax.broadcasted_iota(jnp.int32, field.shape, 0)
    at_y = lax.rem(lax.div(place, size_z), size_y)
    shifted = z_windows(field, size_z)
    out = []
    for oy in (-1, 0, 1):
        for part in shifted:
            if oy:
                part = pltpu.roll(part, (-oy * size_z) % rows, 0)
                part = jnp.where(at_y == (size_y - 1 if oy > 0 else 0), 0.0, part)
            out.append(part)
    return out


def fill(u_ref, parts, plane=0, offset=0, stride=None):
    rows, width = parts[0].shape
    stride = width if stride is None else stride
    for t, part in enumerate(parts):
        lane = t * stride + offset
        u_ref[plane : plane + rows, lane : lane + width] = part.astype(BF)


def clear_rims(u_ref, plane):
    rows, lanes = u_ref.shape
    zero = jnp.zeros((plane, lanes), BF)
    u_ref[0:plane, :] = zero
    u_ref[rows - plane : rows, :] = zero


def moved(field, ox, oy):
    nx, ny, nz, width = field.shape
    if ox:
        rim = jnp.zeros((1, ny, nz, width), F32)
        field = jnp.concatenate([field[1:], rim] if ox > 0 else [rim, field[:-1]], 0)
    if oy:
        rim = jnp.zeros((nx, 1, nz, width), F32)
        field = jnp.concatenate([field[:, 1:], rim] if oy > 0 else [rim, field[:, :-1]], 1)
    return field


def grouped(width, extent, product):
    total = None
    for first in range(0, 9, 2):
        groups = [first, first + 1] if first < 8 else [first]
        both = product(groups)
        for i, g in enumerate(groups):
            part = both[:, i * width : (i + 1) * width].reshape(extent + (width,))
            part = moved(part, g // 3 - 1, g % 3 - 1)
            total = part if total is None else total + part
    return total.reshape(-1, width)


def conv_z(uz, w_ref, extent):
    depth = w_ref.shape[0] // 9

    def product(groups):
        side = [w_ref[g * depth : (g + 1) * depth, :] for g in groups]
        return dot(uz, side[0] if len(side) == 1 else jnp.concatenate(side, 1))

    return grouped(w_ref.shape[1], extent, product)


def conv_z_back(uz, w_ref, extent, low=0, high=None):
    every = w_ref.shape[0] // 27
    high = every if high is None else high
    width = high - low

    def product(groups):
        side = []
        for g in groups:
            taps = [(8 - g) * 3 + 2 - t for t in range(3)]
            side.append(jnp.concatenate([w_ref[p * every + low : p * every + high, :] for p in taps], 1))
        return dot_t(uz, side[0] if len(side) == 1 else jnp.concatenate(side, 0))

    return grouped(width, extent, product)


def conv(u_ref, w_ref, rows, plane):
    depth = u_ref.shape[1]
    total = None
    for ox in range(3):
        part = dot(u_ref[ox * plane : ox * plane + rows, :], w_ref[ox * depth : (ox + 1) * depth, :])
        total = part if total is None else total + part
    return total


def own_columns(field, count, position):
    shape = (count, field.shape[1])
    wanted = lax.broadcasted_iota(jnp.int32, shape, 0) + position * count
    pick = (lax.broadcasted_iota(jnp.int32, shape, 1) == wanted).astype(F32).astype(BF)
    return dot_t(pick, field)


def tap_shifts(grad, extent):
    nx, ny, nz = extent
    count, rows = grad.shape
    place = lax.broadcasted_iota(jnp.int32, grad.shape, 1)
    at = (lax.div(place, ny * nz), lax.rem(lax.div(place, nz), ny), lax.rem(place, nz))
    parts = []
    for ox in (-1, 0, 1):
        for oy in (-1, 0, 1):
            for oz in (-1, 0, 1):
                by = ((ox * ny) + oy) * nz + oz
                part = pltpu.roll(grad, by % rows, 1) if by else grad
                inside = None
                for index, size, o in zip(at, extent, (ox, oy, oz)):
                    if o:
                        here = index != (0 if o > 0 else size - 1)
                        inside = here if inside is None else inside & here
                parts.append(part if inside is None else jnp.where(inside, part, 0.0))
    return jnp.concatenate(parts, 0).astype(BF)


def tap_grad(grad, field, extent):
    return dot(tap_shifts(grad, extent), field)


def split(pack, keep_ref, send_ref, core):
    size = send_ref.shape[0]
    keep_ref[0:size, :] = pack[pl.ds(pl.multiple_of(core * size, size), size), :]
    send_ref[...] = pack[pl.ds(pl.multiple_of((1 - core) * size, size), size), :]


def emit(pack_ref, spot, grad, taps=1):
    count, width = grad.shape[0] // taps, grad.shape[1]
    at = spot
    if width == LANES:
        pack_ref[at : at + taps * count, :] = grad.astype(BF)
        return
    for tap in range(taps):
        for v in range(0, width, LANES):
            pack_ref[at : at + count, :] = grad[tap * count : (tap + 1) * count, v : v + LANES].astype(BF)
            at += count


def one_hot(ny, nz, back):
    plane = ny * nz
    shape = (2 * plane, 2 * plane)
    row = lax.broadcasted_iota(jnp.int32, shape, 1 if back else 0)
    column = lax.broadcasted_iota(jnp.int32, shape, 0 if back else 1)
    tap, at = lax.div(row, plane // 4), lax.rem(row, plane // 4)
    ox, oy, oz = lax.div(tap, 4), lax.rem(lax.div(tap, 2), 2), lax.rem(tap, 2)
    y, z = lax.div(at, nz // 2), lax.rem(at, nz // 2)
    wanted = ox * plane + (2 * y + oy) * nz + 2 * z + oz
    return (column == wanted).astype(F32).astype(BF)


def to_blocks(shuffle, field, d_ref, pairs, plane):
    width = field.shape[1]
    for i in range(pairs):
        mixed = dot(shuffle, field[i * 8 * plane : (i + 1) * 8 * plane]).astype(BF)
        for t in range(8):
            d_ref[i * plane : (i + 1) * plane, t * width : (t + 1) * width] = mixed[
                t * plane : (t + 1) * plane
            ]


def from_blocks(unshuffle, flat, pairs, plane, width):
    parts = []
    for i in range(pairs):
        rows = flat[i * plane : (i + 1) * plane]
        stacked = jnp.concatenate([rows[:, t * width : (t + 1) * width] for t in range(8)], axis=0)
        parts.append(dot(unshuffle, stacked))
    return jnp.concatenate(parts, axis=0)


def join_kernel(sx, plane, volume_hbm, cotangent_hbm, out_ref, volume_ref, arrived):
    first = pltpu.make_async_copy(volume_hbm, volume_ref, arrived.at[0])
    second = pltpu.make_async_copy(cotangent_hbm, out_ref.at[0, sx // 2 * plane :], arrived.at[1])
    first.start()
    second.start()
    first.wait()
    for i in range(sx // 2):
        pair = [volume_ref[2 * i + k].astype(F32) for k in range(2)]
        out_ref[0, i * plane : (i + 1) * plane, :] = jnp.concatenate(pair, 1).astype(BF)
    second.wait()


def stage_kernel(near_ref, sources, *refs):
    del near_ref
    *held, arrived = refs
    copies = [pltpu.make_async_copy(a, b, arrived.at[i]) for i, (a, b) in enumerate(zip(sources, held))]
    for copy in copies:
        copy.start()
    for copy in copies:
        copy.wait()


def flip_kernel(near_ref, source, held, flipped, arrived):
    del near_ref
    width = source.shape[0] // 27
    parts = [slice(i * 9 * width, (i + 1) * 9 * width) for i in range(3)]
    copies = [
        pltpu.make_async_copy(source.at[part], held.at[part], arrived.at[i]) for i, part in enumerate(parts)
    ]
    for copy in copies:
        copy.start()
    for i, copy in enumerate(copies):
        copy.wait()
        for tap in range(9 * i, 9 * i + 9):
            to = 26 - tap
            flipped[to * width : (to + 1) * width, :] = held[tap * width : (tap + 1) * width, :].T


def upper_kernel(
    geo,
    gathered,
    weights,
    decoded_ref,
    keep_ref,
    send_ref,
    vol_ref,
    z1_ref,
    h1_ref,
    z2_ref,
    d_ref,
    z3_ref,
    t4_ref,
    ut,
    blocks,
    uv,
    u1,
    uj,
    uc,
    joined,
    lb_ref,
    out_map,
    pack,
):
    (n, sx, ny, nz, c0, c1, c2, masks, spots) = geo
    position = lax.axis_index("space")
    w_first, w_enc, w_down, w_bottom, w_up, w_join = weights
    shuffle, unshuffle = one_hot(ny, nz, False), one_hot(ny, nz, True)
    plane, nx = ny * nz, sx * n
    rows = nx * plane
    cplane, cx = plane // 4, nx // 2
    crows = cx * cplane
    fine, coarse = (nx, ny, nz), (cx, ny // 2, nz // 2)
    for source, held in zip(gathered, masks):
        for m, mask in enumerate(held):
            blocks[lax.bitwise_xor(position, mask)] = source[m]

    lane = lax.broadcasted_iota(jnp.int32, (plane, LANES), 1)
    vol_rows = sx // 2 * plane
    planes = []
    for j in range(n):
        for i in range(sx // 2):
            pair = blocks[j, i * plane : (i + 1) * plane, :].astype(F32)
            turned = pltpu.roll(pair, c0, 1)
            planes.append(jnp.where(lane < c0, pair, turned))
            planes.append(jnp.where(lane < c0, turned, pair))
    twice = jnp.concatenate(planes, 0)
    vol_ref[...] = twice.astype(BF)
    before, middle, after = z_windows(twice, nz)
    lane = lax.broadcasted_iota(jnp.int32, (rows, LANES), 1)
    uv[:, 0:LANES] = jnp.where(lane < c0, before, middle).astype(BF)
    uv[:, LANES:] = after.astype(BF)
    z1 = conv_z(uv[:, 0 : 3 * c0], w_first, fine)
    z1_ref[...] = z1
    h1 = silu(z1)
    h1_ref[...] = h1
    fill(u1, z_windows(h1.astype(F32), nz))
    z2 = conv_z(u1[...], w_enc, fine)
    z2_ref[...] = z2
    skip = silu(z2)
    joined[:, c1:] = skip
    fill(uj, z_windows(skip.astype(F32), nz), 0, c1, 2 * c1)
    to_blocks(shuffle, skip, d_ref, cx, cplane)
    z3 = dot(d_ref[...], w_down[...])
    z3_ref[...] = z3
    g1 = silu(z3)
    clear_rims(uc, cplane)
    fill(uc, yz_windows(g1.astype(F32), *coarse[1:]), cplane)
    z4 = conv(uc, w_bottom, crows, cplane)
    g2 = silu(z4)
    lifted = from_blocks(unshuffle, dot(g2, w_up[...]).astype(BF), cx, cplane, c1)
    joined[:, 0:c1] = lifted.astype(BF)
    fill(uj, z_windows(lifted, nz), 0, 0, 2 * c1)
    z7 = conv_z(uj[...], w_join, fine)
    out_map[...] = silu(z7)
    kept = sx * plane
    decoded_ref[...] = out_map[pl.ds(pl.multiple_of(position * kept, kept), kept), :]

    cot = jnp.concatenate([blocks[j, vol_rows:, :] for j in range(n)], 0).astype(F32)
    t7 = (cot * slope(z7)).astype(BF)
    fill(ut, z_windows(t7.astype(F32), nz))
    e_lift = conv_z_back(ut[...], w_join, fine, 0, c1).astype(BF)
    to_blocks(shuffle, e_lift, lb_ref, cx, cplane)
    e3 = dot_t(lb_ref[...], w_up[...]).astype(BF).astype(F32)
    t4 = (e3 * slope(z4)).astype(BF)
    t4_ref[...] = t4
    emit(pack, spots["up"], dot(own_columns(lb_ref[...], 8 * c1 // n, position).astype(BF), g2))
    emit(pack, spots["join"], tap_grad(own_columns(t7, c1 // n, position), joined[...], fine), 27)
    split(pack, keep_ref, send_ref, lax.rem(lax.axis_index("section"), 2))
    at = send_ref.shape[0]
    for v in range(0, c2, LANES):
        keep_ref[at : at + crows, :] = g1[:, v : v + LANES]
        at += crows
    mine = own_columns(t4, c2 // n, position).astype(BF)
    for v in range(0, crows, LANES):
        keep_ref[at : at + c2 // n, :] = mine[:, v : v + LANES]
        at += c2 // n


def skip_kernel(extent, c1, ut, w_join, out_ref):
    out_ref[...] = conv_z_back(ut[...], w_join, extent, c1, 2 * c1)


def lower_kernel(
    geo,
    w_enc,
    w_down,
    back_bottom,
    z1_ref,
    z2_ref,
    d_ref,
    z3_ref,
    t4_ref,
    skip_back_ref,
    pack,
    t2_ref,
    t1_ref,
    utc,
    ut,
):
    (n, sx, ny, nz, c0, c1, c2, masks, spots) = geo
    position = lax.axis_index("space")
    plane, nx = ny * nz, sx * n
    cplane, cx = plane // 4, nx // 2
    crows = cx * cplane
    fine, coarse = (nx, ny, nz), (cx, ny // 2, nz // 2)
    unshuffle = one_hot(ny, nz, True)
    clear_rims(utc, cplane)
    fill(utc, yz_windows(t4_ref[...].astype(F32), *coarse[1:]), cplane)
    e4 = conv(utc, back_bottom, crows, cplane).astype(BF).astype(F32)
    t3 = (e4 * slope(z3_ref[...])).astype(BF)
    emit(pack, spots["down"], dot(own_columns(t3, c2 // n, position).astype(BF), d_ref[...]))
    e5 = dot_t(t3, w_down[...])
    high = e5.astype(BF)
    low = (e5 - high.astype(F32)).astype(BF)
    e5 = from_blocks(unshuffle, high, cx, cplane, c1) + from_blocks(
        unshuffle, low, cx, cplane, c1
    )
    t2 = ((e5 + skip_back_ref[...]) * slope(z2_ref[...])).astype(BF)
    fill(ut, z_windows(t2.astype(F32), nz))
    t2_ref[...] = t2
    e6 = conv_z_back(ut[...], w_enc, fine).astype(BF).astype(F32)
    t1_ref[...] = (e6 * slope(z1_ref[...])).astype(BF)


def first_kernel(geo, down_ref, t2_ref, t1_ref, h1_ref, vol_ref, keep_ref, send_ref, pack):
    (n, sx, ny, nz, c0, c1, c2, masks, spots) = geo
    position = lax.axis_index("space")
    fine = (sx * n, ny, nz)
    count = c1 // n
    pack[0 : down_ref.shape[0], :] = down_ref[...]
    emit(pack, spots["enc"], tap_grad(own_columns(t2_ref[...], count, position), h1_ref[...], fine), 27)
    taps = tap_grad(own_columns(t1_ref[...], count, position), vol_ref[...], fine)
    lane = lax.broadcasted_iota(jnp.int32, (count, LANES), 1)
    at = spots["first"]
    for tap in range(0, 27, 2):
        a = taps[tap * count : (tap + 1) * count]
        b = taps[(tap + 1) * count : (tap + 2) * count] if tap < 26 else a
        pack[at : at + count, :] = jnp.where(lane < c0, a, b).astype(BF)
        at += count
    split(pack, keep_ref, send_ref, lax.rem(lax.axis_index("section"), 2))


def unpack(source, spot, out, factor):
    count, width = out.shape
    at = spot
    for v in range(0, width, LANES):
        take = min(LANES, width - v)
        out[:, v : v + take] = (source(at, count) * factor)[:, :take]
        at += count


def halves(both, mine_ref, other_ref, core):
    size = both.shape[1]
    both[core] = mine_ref[0:size, :]
    both[1 - core] = other_ref[0:size, :]

    def source(at, count):
        if (at + count - 1) // size == at // size:
            return both[at // size, at % size : at % size + count, :].astype(F32)
        cut = size - at % size
        return jnp.concatenate(
            [both[0, size - cut : size, :].astype(F32), both[1, 0 : count - cut, :].astype(F32)], 0
        )

    return source


def finish_first(
    factor, spots, extent, mine_ref, other_ref, bottom_ref, up_ref, join_ref, token, both, acts
):
    token[...] = jnp.zeros(token.shape, F32)
    section = lax.axis_index("section")
    size = both.shape[1]
    source = halves(both, mine_ref, other_ref, lax.rem(section, 2))
    unpack(source, spots["join"], join_ref, factor)
    rows, width = up_ref.shape[1], up_ref.shape[0]
    for v in range(0, width, LANES):
        up_ref[v : v + LANES, :] = (source(spots["up"] + v // LANES * rows, rows) * factor).T

    crops, each = acts.shape[0], acts.shape[1]
    for j in range(crops // 2):
        part = slice(size + j * each, size + (j + 1) * each)
        acts[lax.bitwise_xor(section, 2 * j)] = mine_ref[part, :]
        acts[lax.bitwise_xor(section, 2 * j + 1)] = other_ref[part, :]
    voxels = extent[0] * extent[1] * extent[2]
    count, wide = bottom_ref.shape[0], bottom_ref.shape[1] // 27
    shifted, fields = [], []
    for crop in range(crops):
        at = wide // LANES * voxels
        fields.append(
            jnp.concatenate([acts[crop, v : v + voxels, :] for v in range(0, at, voxels)], 1)
        )
        own = [acts[crop, v : v + count, :] for v in range(at, each, count)]
        shifted.append(tap_shifts(jnp.concatenate(own, 1).astype(F32), extent))
    grad = dot(jnp.concatenate(shifted, 1), jnp.concatenate(fields, 0)) * factor
    for tap in range(27):
        bottom_ref[:, tap * wide : (tap + 1) * wide] = grad[tap * count : (tap + 1) * count]


def finish_second(factor, spots, mine_ref, other_ref, first_ref, enc_ref, down_ref, both):
    source = halves(both, mine_ref, other_ref, lax.rem(lax.axis_index("section"), 2))
    unpack(source, spots["down"], down_ref, factor)
    unpack(source, spots["first"], first_ref, factor)
    unpack(source, spots["enc"], enc_ref, factor)


def merge_kernel(size, a_ref, b_ref, *refs):
    out_ref = refs[-1]
    out_ref[0:size, :] = (a_ref[0:size, :].astype(F32) + b_ref[0:size, :].astype(F32)).astype(BF)
    at = size
    for ref in (a_ref, b_ref):
        rest = ref.shape[0] - size
        if rest:
            out_ref[at : at + rest, :] = ref[size:, :]
            at += rest


def merge(a, b, size, *after):
    shape = (a.shape[0] + b.shape[0] - size, LANES)
    kernel = functools.partial(merge_kernel, size)
    return call(kernel, [(shape, BF)], [], (VMEM,) * (2 + len(after)), vmem=4)(a, b, *after)[0]


def between_cores(keep, send, *after):
    return merge(keep, exchange(send, "section", 1), send.shape[0], *after)


def between_chips(total, size, crops, *after):
    mask = 2
    while mask < crops:
        mask *= 2
        last = after if mask >= crops else ()
        total = merge(total, exchange(total, "section", mask // 2), size, *last)
    return total, exchange(total, "section", 1)


def in_hbm(array):
    return pltpu.with_memory_space_constraint(array, HBM)


def exchange(array, axis, mask):
    devices = lax.axis_size(axis)
    return lax.ppermute(array, axis, [(i, i ^ mask) for i in range(devices)])


def merge_kernel(size, a_ref, b_ref, *refs):
    out_ref = refs[-1]
    out_ref[0:size, :] = (a_ref[0:size, :].astype(F32) + b_ref[0:size, :].astype(F32)).astype(BF)
    at = size
    for ref in (a_ref, b_ref):
        rest = ref.shape[0] - size
        if rest:
            out_ref[at : at + rest, :] = ref[size:, :]
            at += rest


def merge(a, b, size, *after):
    shape = (a.shape[0] + b.shape[0] - size, LANES)
    kernel = functools.partial(merge_kernel, size)
    return call(kernel, [(shape, BF)], [], (VMEM,) * (2 + len(after)), vmem=4)(a, b, *after)[0]


def reduced(keep, send, crops, after=()):
    size = send.shape[0]
    total = merge(keep, exchange(send, "section", 1), size)
    mask = 2
    while mask < crops:
        mask *= 2
        total = merge(total, exchange(total, "section", mask // 2), size, *(after if mask >= crops else ()))
    return total, exchange(total, "section", 1)


def stack_kernel(a_ref, b_ref, *refs):
    out_ref = refs[-1]
    out_ref[0 : a_ref.shape[0]] = a_ref[...]
    out_ref[a_ref.shape[0] :] = b_ref[...]


def stack(a, b, *after):
    shape = (a.shape[0] + b.shape[0],) + a.shape[1:]
    return call(stack_kernel, [(shape, BF)], [], (VMEM,) * (2 + len(after)), vmem=4)(a, b, *after)[0]


def call(kernel, outs, scratch, spaces, flops=0, vmem=12):
    return pl.pallas_call(
        kernel,
        out_shape=tuple(jax.ShapeDtypeStruct(s, d) for s, d in outs),
        in_specs=jax.tree.map(lambda space: pl.BlockSpec(memory_space=space), spaces),
        out_specs=tuple(pl.BlockSpec(memory_space=VMEM) for _ in outs),
        scratch_shapes=scratch,
        compiler_params=pltpu.CompilerParams(vmem_limit_bytes=vmem * MIB),
        cost_estimate=pl.CostEstimate(flops=flops, bytes_accessed=2 * MIB, transcendentals=0),
    )


def body(volume, w_first, w_enc, w_down, w_bottom, w_up, w_join, cotangent):
    n = lax.axis_size("space")
    crops = lax.axis_size("section")
    _, sx, ny, nz, c0 = volume.shape
    c1, c2 = w_enc.shape[1], w_bottom.shape[1]
    plane, nx = ny * nz, sx * n
    rows = nx * plane
    cplane, crows = plane // 4, rows // 8
    own_rows = sx * plane // 2 + sx * plane
    (near,) = call(
        functools.partial(join_kernel, sx, plane),
        [((1, own_rows, LANES), BF)],
        [pltpu.VMEM((sx, plane, c0), BF), pltpu.SemaphoreType.DMA((2,))],
        (HBM, HBM),
        vmem=4,
    )(in_hbm(volume.reshape(sx, plane, c0)), in_hbm(cotangent.reshape(sx * plane, c1)))
    held_bottom, back_bottom = call(
        flip_kernel,
        [(w_bottom.shape, BF)] * 2,
        [pltpu.SemaphoreType.DMA((3,))],
        (VMEM, HBM),
        flops=10**9,
    )(near, in_hbm(w_bottom))
    held, step = [0], n // 2
    while step > 2:
        held = held + [m ^ step for m in held]
        near = stack(near, exchange(near, "space", step), back_bottom)
        step //= 2
    weights = [w_first, w_enc, w_down, w_up, w_join]
    weights = call(
        stage_kernel,
        [(w.shape, BF) for w in weights],
        [pltpu.SemaphoreType.DMA((len(weights),))],
        (VMEM, [HBM] * len(weights)),
        flops=10**9,
    )(near, [in_hbm(w) for w in weights])
    weights = [*weights[:3], held_bottom, *weights[3:]]
    last = range(1, min(n, 4))
    gathered = [near] + [exchange(near, "space", mask) for mask in last]
    masks = tuple(tuple(m ^ mask for m in held) for mask in (0, *last))

    fine_own, wide_own = c1 // n, c2 // n
    shapes = {
        "first": (fine_own, 27 * c0),
        "enc": (fine_own, 27 * c1),
        "down": (wide_own, 8 * c1),
        "bottom": (wide_own, 27 * c2),
        "up": (8 * c1 // n, c2),
        "join": (fine_own, 54 * c1),
    }

    def layout(names):
        spots, at = {}, 0
        for name in names:
            spots[name] = at
            count, width = shapes[name]
            at += count * -(-width // LANES)
        return spots, -(-at // 32) * 32

    upper_spots, upper_rows = layout(("up", "join"))
    lower_spots, lower_rows = layout(("down", "enc", "first"))
    geo = (n, sx, ny, nz, c0, c1, c2, masks)
    fine, coarse = (nx, ny, nz), (nx // 2, ny // 2, nz // 2)
    size = upper_rows // 2
    act_rows = c2 // LANES * crows + crows // LANES * wide_own
    decoded, keep, send, vol2, z1, h1, z2, blocks, z3, t4, ut = call(
        functools.partial(upper_kernel, geo + (upper_spots,)),
        [
            ((sx * plane, c1), BF),
            ((size + act_rows, LANES), BF),
            ((size, LANES), BF),
            ((rows, 2 * c0), BF),
            ((rows, c1), F32),
            ((rows, c1), BF),
            ((rows, c1), F32),
            ((crows, 8 * c1), BF),
            ((crows, c2), F32),
            ((crows, c2), BF),
            ((rows, 3 * c1), BF),
        ],
        [
            pltpu.VMEM((n, own_rows, LANES), BF),
            pltpu.VMEM((rows, 2 * LANES), BF),
            pltpu.VMEM((rows, 3 * c1), BF),
            pltpu.VMEM((rows, 6 * c1), BF),
            pltpu.VMEM((crows + 2 * cplane, 9 * c2), BF),
            pltpu.VMEM((rows, 2 * c1), BF),
            pltpu.VMEM((crows, 8 * c1), BF),
            pltpu.VMEM((rows, c1), BF),
            pltpu.VMEM((upper_rows, LANES), BF),
        ],
        ([VMEM] * len(gathered), [VMEM] * len(weights)),
        flops=10**10,
        vmem=14,
    )(gathered, weights)
    (skip_back,) = call(
        functools.partial(skip_kernel, fine, c1),
        [((rows, c1), F32)],
        [],
        (VMEM, VMEM),
        flops=10**9,
    )(ut, weights[5])
    total = between_cores(keep, send, skip_back)

    low_size = lower_rows // 2
    down, t2, t1 = call(
        functools.partial(lower_kernel, geo + (lower_spots,)),
        [((lower_spots["enc"], LANES), BF), ((rows, c1), BF), ((rows, c1), BF)],
        [pltpu.VMEM((crows + 2 * cplane, 9 * c2), BF), pltpu.VMEM((rows, 3 * c1), BF)],
        (VMEM,) * 9,
        flops=6 * 10**9,
    )(weights[1], weights[2], back_bottom, z1, z2, blocks, z3, t4, skip_back)
    low_keep, low_send = call(
        functools.partial(first_kernel, geo + (lower_spots,)),
        [((low_size, LANES), BF), ((low_size, LANES), BF)],
        [pltpu.VMEM((lower_rows, LANES), BF)],
        (VMEM,) * 5,
        flops=10**9,
    )(down, t2, t1, h1, vol2)
    low_total = between_cores(low_keep, low_send)
    total, other = between_chips(total, size, crops, low_total)
    factor = 1.0 / math.sqrt(crops * rows)
    grad_bottom, grad_up, grad_join, token = call(
        functools.partial(finish_first, factor, upper_spots, coarse),
        [
            (shapes["bottom"], F32),
            (shapes["up"][::-1], F32),
            (shapes["join"], F32),
            ((8, LANES), F32),
        ],
        [pltpu.VMEM((2, size, LANES), BF), pltpu.VMEM((crops, act_rows, LANES), BF)],
        (VMEM, VMEM),
        vmem=12,
    )(total, other)
    low_total, low_other = between_chips(low_total, low_size, crops, token)
    grad_first, grad_enc, grad_down = call(
        functools.partial(finish_second, factor, lower_spots),
        [(shapes[name], F32) for name in ("first", "enc", "down")],
        [pltpu.VMEM((2, low_size, LANES), BF)],
        (VMEM, VMEM),
        vmem=8,
    )(low_total, low_other)
    return (
        decoded.reshape((1, sx, ny, nz, c1)),
        grad_first.T,
        grad_enc.T,
        grad_down.T,
        grad_bottom.T,
        grad_up,
        grad_join.T,
    )


def solution(mesh):
    field = P("section", "space", None, None, None)
    split = P(None, "space")
    return jax.shard_map(
        body,
        mesh=mesh,
        in_specs=(field,) + (P(),) * 6 + (field,),
        out_specs=(field,) + (split,) * 6,
        check_vma=False,
    )
```

```python
import functools
import math

import jax
import jax.numpy as jnp
from jax import lax
from jax.experimental import pallas as pl
from jax.experimental.pallas import tpu as pltpu
from jax.sharding import PartitionSpec as P

BF = jnp.bfloat16
F32 = jnp.float32
LANES = 128
MIB = 1024 * 1024
VMEM = pltpu.MemorySpace.VMEM
HBM = pltpu.MemorySpace.HBM


def dot(a, b):
    return jnp.dot(a, b, preferred_element_type=F32)


def dot_t(a, b):
    return lax.dot_general(a, b, (((1,), (1,)), ((), ())), preferred_element_type=F32)


def sigmoid(z):
    return jax.nn.sigmoid(z)


def silu(z):
    return (z * sigmoid(z)).astype(BF)


def slope(z):
    s = sigmoid(z)
    return s * (1.0 + z * (1.0 - s))


def mod(index, size):
    return index & (size - 1) if size & (size - 1) == 0 else lax.rem(index, size)


def over(index, size):
    if size & (size - 1) == 0:
        return lax.shift_right_logical(index, size.bit_length() - 1)
    return lax.div(index, size)


def z_windows(field, size_z):
    rows = field.shape[0]
    at_z = mod(lax.broadcasted_iota(jnp.int32, field.shape, 0), size_z)
    out = []
    for oz in (-1, 0, 1):
        part = field
        if oz:
            part = pltpu.roll(field, (-oz) % rows, 0)
            part = jnp.where(at_z == (size_z - 1 if oz > 0 else 0), 0.0, part)
        out.append(part)
    return out


def yz_windows(field, size_y, size_z):
    rows = field.shape[0]
    place = lax.broadcasted_iota(jnp.int32, field.shape, 0)
    at_y = mod(over(place, size_z), size_y)
    shifted = z_windows(field, size_z)
    out = []
    for oy in (-1, 0, 1):
        for part in shifted:
            if oy:
                part = pltpu.roll(part, (-oy * size_z) % rows, 0)
                part = jnp.where(at_y == (size_y - 1 if oy > 0 else 0), 0.0, part)
            out.append(part)
    return out


def fill(u_ref, parts, plane=0, offset=0, stride=None):
    rows, width = parts[0].shape
    stride = width if stride is None else stride
    for t, part in enumerate(parts):
        lane = t * stride + offset
        u_ref[plane : plane + rows, lane : lane + width] = part.astype(BF)


def clear_rims(u_ref, plane):
    rows, lanes = u_ref.shape
    zero = jnp.zeros((plane, lanes), BF)
    u_ref[0:plane, :] = zero
    u_ref[rows - plane : rows, :] = zero


def moved(field, ox, oy):
    nx, ny, nz, width = field.shape
    if ox:
        rim = jnp.zeros((1, ny, nz, width), F32)
        field = jnp.concatenate([field[1:], rim] if ox > 0 else [rim, field[:-1]], 0)
    if oy:
        rim = jnp.zeros((nx, 1, nz, width), F32)
        field = jnp.concatenate([field[:, 1:], rim] if oy > 0 else [rim, field[:, :-1]], 1)
    return field


def grouped(width, extent, product):
    total = None
    for first in range(0, 9, 2):
        groups = [first, first + 1] if first < 8 else [first]
        both = product(groups)
        for i, g in enumerate(groups):
            part = both[:, i * width : (i + 1) * width].reshape(extent + (width,))
            part = moved(part, g // 3 - 1, g % 3 - 1)
            total = part if total is None else total + part
    return total.reshape(-1, width)


def conv_z(uz, w_ref, extent):
    depth = w_ref.shape[0] // 9

    def product(groups):
        side = [w_ref[g * depth : (g + 1) * depth, :] for g in groups]
        return dot(uz, side[0] if len(side) == 1 else jnp.concatenate(side, 1))

    return grouped(w_ref.shape[1], extent, product)


def conv_z_back(uz, w_ref, extent, low=0, high=None):
    every = w_ref.shape[0] // 27
    high = every if high is None else high
    width = high - low

    def product(groups):
        side = []
        for g in groups:
            taps = [(8 - g) * 3 + 2 - t for t in range(3)]
            side.append(jnp.concatenate([w_ref[p * every + low : p * every + high, :] for p in taps], 1))
        return dot_t(uz, side[0] if len(side) == 1 else jnp.concatenate(side, 0))

    return grouped(width, extent, product)


def conv(u_ref, w_ref, rows, plane):
    depth = u_ref.shape[1]
    total = None
    for ox in range(3):
        part = dot(u_ref[ox * plane : ox * plane + rows, :], w_ref[ox * depth : (ox + 1) * depth, :])
        total = part if total is None else total + part
    return total


def own_columns(field, count, position):
    shape = (count, field.shape[1])
    wanted = lax.broadcasted_iota(jnp.int32, shape, 0) + position * count
    pick = (lax.broadcasted_iota(jnp.int32, shape, 1) == wanted).astype(F32).astype(BF)
    return dot_t(pick, field)


def tap_shifts(grad, extent):
    nx, ny, nz = extent
    count, rows = grad.shape
    place = lax.broadcasted_iota(jnp.int32, grad.shape, 1)
    at = (over(place, ny * nz), mod(over(place, nz), ny), mod(place, nz))
    parts = []
    for ox in (-1, 0, 1):
        for oy in (-1, 0, 1):
            for oz in (-1, 0, 1):
                by = ((ox * ny) + oy) * nz + oz
                part = pltpu.roll(grad, by % rows, 1) if by else grad
                inside = None
                for index, size, o in zip(at, extent, (ox, oy, oz)):
                    if o:
                        here = index != (0 if o > 0 else size - 1)
                        inside = here if inside is None else inside & here
                parts.append(part if inside is None else jnp.where(inside, part, 0.0))
    return jnp.concatenate(parts, 0).astype(BF)


def tap_grad(grad, field, extent):
    return dot(tap_shifts(grad, extent), field)


def split(pack, keep_ref, send_ref, core):
    size = send_ref.shape[0]
    keep_ref[0:size, :] = pack[pl.ds(pl.multiple_of(core * size, size), size), :]
    send_ref[...] = pack[pl.ds(pl.multiple_of((1 - core) * size, size), size), :]


def emit(pack_ref, spot, grad, taps=1):
    count, width = grad.shape[0] // taps, grad.shape[1]
    at = spot
    if width == LANES:
        pack_ref[at : at + taps * count, :] = grad.astype(BF)
        return
    for tap in range(taps):
        for v in range(0, width, LANES):
            pack_ref[at : at + count, :] = grad[tap * count : (tap + 1) * count, v : v + LANES].astype(BF)
            at += count


def one_hot(ny, nz, back):
    plane = ny * nz
    shape = (2 * plane, 2 * plane)
    row = lax.broadcasted_iota(jnp.int32, shape, 1 if back else 0)
    column = lax.broadcasted_iota(jnp.int32, shape, 0 if back else 1)
    tap, at = over(row, plane // 4), mod(row, plane // 4)
    ox, oy, oz = over(tap, 4), mod(over(tap, 2), 2), mod(tap, 2)
    y, z = over(at, nz // 2), mod(at, nz // 2)
    wanted = ox * plane + (2 * y + oy) * nz + 2 * z + oz
    return (column == wanted).astype(F32).astype(BF)


def to_blocks(shuffle, field, d_ref, pairs, plane):
    width = field.shape[1]
    for i in range(pairs):
        mixed = dot(shuffle, field[i * 8 * plane : (i + 1) * 8 * plane]).astype(BF)
        for t in range(8):
            d_ref[i * plane : (i + 1) * plane, t * width : (t + 1) * width] = mixed[
                t * plane : (t + 1) * plane
            ]


def from_blocks(unshuffle, flat, pairs, plane, width):
    parts = []
    for i in range(pairs):
        rows = flat[i * plane : (i + 1) * plane]
        stacked = jnp.concatenate([rows[:, t * width : (t + 1) * width] for t in range(8)], axis=0)
        parts.append(dot(unshuffle, stacked))
    return jnp.concatenate(parts, axis=0)


def join_kernel(sx, plane, volume_hbm, cotangent_hbm, out_ref, volume_ref, arrived):
    first = pltpu.make_async_copy(volume_hbm, volume_ref, arrived.at[0])
    second = pltpu.make_async_copy(cotangent_hbm, out_ref.at[0, sx // 2 * plane :], arrived.at[1])
    first.start()
    second.start()
    first.wait()
    for i in range(sx // 2):
        pair = [volume_ref[2 * i + k].astype(F32) for k in range(2)]
        out_ref[0, i * plane : (i + 1) * plane, :] = jnp.concatenate(pair, 1).astype(BF)
    second.wait()


def stage_kernel(near_ref, sources, *refs):
    del near_ref
    *held, arrived = refs
    copies = [pltpu.make_async_copy(a, b, arrived.at[i]) for i, (a, b) in enumerate(zip(sources, held))]
    for copy in copies:
        copy.start()
    for copy in copies:
        copy.wait()


def flip_kernel(near_ref, source, held, flipped, arrived):
    del near_ref
    width = source.shape[0] // 27
    parts = [slice(i * 9 * width, (i + 1) * 9 * width) for i in range(3)]
    copies = [
        pltpu.make_async_copy(source.at[part], held.at[part], arrived.at[i]) for i, part in enumerate(parts)
    ]
    for copy in copies:
        copy.start()
    for i, copy in enumerate(copies):
        copy.wait()
        for tap in range(9 * i, 9 * i + 9):
            to = 26 - tap
            flipped[to * width : (to + 1) * width, :] = held[tap * width : (tap + 1) * width, :].T


def upper_kernel(
    geo,
    gathered,
    weights,
    own_ref,
    keep_ref,
    send_ref,
    vol_ref,
    z1_ref,
    h1_ref,
    z2_ref,
    d_ref,
    z3_ref,
    t4_ref,
    ut,
    blocks,
    uv,
    u1,
    uj,
    uc,
    joined,
    lb_ref,
    out_map,
    pack,
):
    (n, sx, ny, nz, c0, c1, c2, masks, spots) = geo
    position = lax.axis_index("space")
    w_first, w_enc, w_down, w_bottom, w_up, w_join = weights
    shuffle, unshuffle = one_hot(ny, nz, False), one_hot(ny, nz, True)
    plane, nx = ny * nz, sx * n
    rows = nx * plane
    cplane, cx = plane // 4, nx // 2
    crows = cx * cplane
    fine, coarse = (nx, ny, nz), (cx, ny // 2, nz // 2)
    for source, held in zip(gathered, masks):
        for m, mask in enumerate(held):
            blocks[lax.bitwise_xor(position, mask)] = source[m]

    lane = lax.broadcasted_iota(jnp.int32, (plane, LANES), 1)
    vol_rows = sx // 2 * plane
    planes = []
    for j in range(n):
        for i in range(sx // 2):
            pair = blocks[j, i * plane : (i + 1) * plane, :].astype(F32)
            turned = pltpu.roll(pair, c0, 1)
            planes.append(jnp.where(lane < c0, pair, turned))
            planes.append(jnp.where(lane < c0, turned, pair))
    twice = jnp.concatenate(planes, 0)
    vol_ref[...] = twice.astype(BF)
    before, middle, after = z_windows(twice, nz)
    lane = lax.broadcasted_iota(jnp.int32, (rows, LANES), 1)
    uv[:, 0:LANES] = jnp.where(lane < c0, before, middle).astype(BF)
    uv[:, LANES:] = after.astype(BF)
    z1 = conv_z(uv[:, 0 : 3 * c0], w_first, fine)
    z1_ref[...] = z1
    h1 = silu(z1)
    h1_ref[...] = h1
    fill(u1, z_windows(h1.astype(F32), nz))
    z2 = conv_z(u1[...], w_enc, fine)
    z2_ref[...] = z2
    skip = silu(z2)
    joined[:, c1:] = skip
    fill(uj, z_windows(skip.astype(F32), nz), 0, c1, 2 * c1)
    to_blocks(shuffle, skip, d_ref, cx, cplane)
    z3 = dot(d_ref[...], w_down[...])
    z3_ref[...] = z3
    g1 = silu(z3)
    clear_rims(uc, cplane)
    fill(uc, yz_windows(g1.astype(F32), *coarse[1:]), cplane)
    z4 = conv(uc, w_bottom, crows, cplane)
    g2 = silu(z4)
    lifted = from_blocks(unshuffle, dot(g2, w_up[...]).astype(BF), cx, cplane, c1)
    joined[:, 0:c1] = lifted.astype(BF)
    fill(uj, z_windows(lifted, nz), 0, 0, 2 * c1)
    z7 = conv_z(uj[...], w_join, fine)
    out_map[...] = silu(z7)
    kept = sx * plane
    own_ref[...] = out_map[pl.ds(pl.multiple_of(position * kept, kept), kept), :]

    cot = jnp.concatenate([blocks[j, vol_rows:, :] for j in range(n)], 0).astype(F32)
    t7 = (cot * slope(z7)).astype(BF)
    fill(ut, z_windows(t7.astype(F32), nz))
    e_lift = conv_z_back(ut[...], w_join, fine, 0, c1).astype(BF)
    to_blocks(shuffle, e_lift, lb_ref, cx, cplane)
    e3 = dot_t(lb_ref[...], w_up[...]).astype(BF).astype(F32)
    t4 = (e3 * slope(z4)).astype(BF)
    t4_ref[...] = t4
    emit(pack, spots["up"], dot(own_columns(lb_ref[...], 8 * c1 // n, position).astype(BF), g2))
    emit(pack, spots["join"], tap_grad(own_columns(t7, c1 // n, position), joined[...], fine), 27)
    split(pack, keep_ref, send_ref, lax.rem(lax.axis_index("section"), 2))
    at = send_ref.shape[0]
    for v in range(0, c2, LANES):
        keep_ref[at : at + crows, :] = g1[:, v : v + LANES]
        at += crows
    mine = own_columns(t4, c2 // n, position).astype(BF)
    for v in range(0, crows, LANES):
        keep_ref[at : at + c2 // n, :] = mine[:, v : v + LANES]
        at += c2 // n


def skip_kernel(extent, c1, ut, w_join, out_ref):
    out_ref[...] = conv_z_back(ut[...], w_join, extent, c1, 2 * c1)


def lower_kernel(
    geo,
    w_enc,
    w_down,
    back_bottom,
    z1_ref,
    z2_ref,
    d_ref,
    z3_ref,
    t4_ref,
    skip_back_ref,
    pack,
    t2_ref,
    t1_ref,
    utc,
    ut,
):
    (n, sx, ny, nz, c0, c1, c2, masks, spots) = geo
    position = lax.axis_index("space")
    plane, nx = ny * nz, sx * n
    cplane, cx = plane // 4, nx // 2
    crows = cx * cplane
    fine, coarse = (nx, ny, nz), (cx, ny // 2, nz // 2)
    unshuffle = one_hot(ny, nz, True)
    clear_rims(utc, cplane)
    fill(utc, yz_windows(t4_ref[...].astype(F32), *coarse[1:]), cplane)
    e4 = conv(utc, back_bottom, crows, cplane).astype(BF).astype(F32)
    t3 = (e4 * slope(z3_ref[...])).astype(BF)
    emit(pack, spots["down"], dot(own_columns(t3, c2 // n, position).astype(BF), d_ref[...]))
    e5 = dot_t(t3, w_down[...])
    high = e5.astype(BF)
    low = (e5 - high.astype(F32)).astype(BF)
    e5 = from_blocks(unshuffle, high, cx, cplane, c1) + from_blocks(
        unshuffle, low, cx, cplane, c1
    )
    t2 = ((e5 + skip_back_ref[...]) * slope(z2_ref[...])).astype(BF)
    fill(ut, z_windows(t2.astype(F32), nz))
    t2_ref[...] = t2
    e6 = conv_z_back(ut[...], w_enc, fine).astype(BF).astype(F32)
    t1_ref[...] = (e6 * slope(z1_ref[...])).astype(BF)


def first_kernel(geo, down_ref, t2_ref, t1_ref, h1_ref, vol_ref, keep_ref, send_ref, pack):
    (n, sx, ny, nz, c0, c1, c2, masks, spots) = geo
    position = lax.axis_index("space")
    fine = (sx * n, ny, nz)
    count = c1 // n
    pack[0 : down_ref.shape[0], :] = down_ref[...]
    emit(pack, spots["enc"], tap_grad(own_columns(t2_ref[...], count, position), h1_ref[...], fine), 27)
    taps = tap_grad(own_columns(t1_ref[...], count, position), vol_ref[...], fine)
    lane = lax.broadcasted_iota(jnp.int32, (count, LANES), 1)
    at = spots["first"]
    for tap in range(0, 27, 2):
        a = taps[tap * count : (tap + 1) * count]
        b = taps[(tap + 1) * count : (tap + 2) * count] if tap < 26 else a
        pack[at : at + count, :] = jnp.where(lane < c0, a, b).astype(BF)
        at += count
    split(pack, keep_ref, send_ref, lax.rem(lax.axis_index("section"), 2))


def unpack(source, spot, out, factor):
    count, width = out.shape
    at = spot
    for v in range(0, width, LANES):
        take = min(LANES, width - v)
        out[:, v : v + take] = (source(at, count) * factor)[:, :take]
        at += count


def halves(both, mine_ref, other_ref, core):
    size = both.shape[1]
    both[core] = mine_ref[0:size, :]
    both[1 - core] = other_ref[0:size, :]

    def source(at, count):
        if (at + count - 1) // size == at // size:
            return both[at // size, at % size : at % size + count, :].astype(F32)
        cut = size - at % size
        return jnp.concatenate(
            [both[0, size - cut : size, :].astype(F32), both[1, 0 : count - cut, :].astype(F32)], 0
        )

    return source


def finish_first(factor, spots, extent, *refs):
    own_ref, mine_ref, other_ref, decoded_ref, bottom_ref, up_ref, join_ref, token, both, acts = refs
    decoded_ref[...] = own_ref[...]
    token[...] = jnp.zeros(token.shape, F32)
    section = lax.axis_index("section")
    size = both.shape[1]
    source = halves(both, mine_ref, other_ref, lax.rem(section, 2))
    unpack(source, spots["join"], join_ref, factor)
    rows, width = up_ref.shape[1], up_ref.shape[0]
    for v in range(0, width, LANES):
        up_ref[v : v + LANES, :] = (source(spots["up"] + v // LANES * rows, rows) * factor).T

    crops, each = acts.shape[0], acts.shape[1]
    for j in range(crops // 2):
        part = slice(size + j * each, size + (j + 1) * each)
        acts[lax.bitwise_xor(section, 2 * j)] = mine_ref[part, :]
        acts[lax.bitwise_xor(section, 2 * j + 1)] = other_ref[part, :]
    voxels = extent[0] * extent[1] * extent[2]
    count, wide = bottom_ref.shape[0], bottom_ref.shape[1] // 27
    shifted, fields = [], []
    for crop in range(crops):
        at = wide // LANES * voxels
        fields.append(
            jnp.concatenate([acts[crop, v : v + voxels, :] for v in range(0, at, voxels)], 1)
        )
        own = [acts[crop, v : v + count, :] for v in range(at, each, count)]
        shifted.append(tap_shifts(jnp.concatenate(own, 1).astype(F32), extent))
    grad = dot(jnp.concatenate(shifted, 1), jnp.concatenate(fields, 0)) * factor
    for tap in range(27):
        bottom_ref[:, tap * wide : (tap + 1) * wide] = grad[tap * count : (tap + 1) * count]


def finish_second(factor, spots, mine_ref, other_ref, first_ref, enc_ref, down_ref, both):
    source = halves(both, mine_ref, other_ref, lax.rem(lax.axis_index("section"), 2))
    unpack(source, spots["down"], down_ref, factor)
    unpack(source, spots["first"], first_ref, factor)
    unpack(source, spots["enc"], enc_ref, factor)


def merge_kernel(size, a_ref, b_ref, *refs):
    out_ref = refs[-1]
    out_ref[0:size, :] = (a_ref[0:size, :].astype(F32) + b_ref[0:size, :].astype(F32)).astype(BF)
    at = size
    for ref in (a_ref, b_ref):
        rest = ref.shape[0] - size
        if rest:
            out_ref[at : at + rest, :] = ref[size:, :]
            at += rest


def merge(a, b, size, *after):
    shape = (a.shape[0] + b.shape[0] - size, LANES)
    kernel = functools.partial(merge_kernel, size)
    return call(kernel, [(shape, BF)], [], (VMEM,) * (2 + len(after)), vmem=4)(a, b, *after)[0]


def between_cores(keep, send, *after):
    return merge(keep, exchange(send, "section", 1), send.shape[0], *after)


def between_chips(total, size, crops, *after):
    mask = 2
    while mask < crops:
        mask *= 2
        last = after if mask >= crops else ()
        total = merge(total, exchange(total, "section", mask // 2), size, *last)
    return total, exchange(total, "section", 1)


def in_hbm(array):
    return pltpu.with_memory_space_constraint(array, HBM)


def exchange(array, axis, mask):
    devices = lax.axis_size(axis)
    return lax.ppermute(array, axis, [(i, i ^ mask) for i in range(devices)])


def merge_kernel(size, a_ref, b_ref, *refs):
    out_ref = refs[-1]
    out_ref[0:size, :] = (a_ref[0:size, :].astype(F32) + b_ref[0:size, :].astype(F32)).astype(BF)
    at = size
    for ref in (a_ref, b_ref):
        rest = ref.shape[0] - size
        if rest:
            out_ref[at : at + rest, :] = ref[size:, :]
            at += rest


def merge(a, b, size, *after):
    shape = (a.shape[0] + b.shape[0] - size, LANES)
    kernel = functools.partial(merge_kernel, size)
    return call(kernel, [(shape, BF)], [], (VMEM,) * (2 + len(after)), vmem=4)(a, b, *after)[0]


def reduced(keep, send, crops, after=()):
    size = send.shape[0]
    total = merge(keep, exchange(send, "section", 1), size)
    mask = 2
    while mask < crops:
        mask *= 2
        total = merge(total, exchange(total, "section", mask // 2), size, *(after if mask >= crops else ()))
    return total, exchange(total, "section", 1)


def stack_kernel(a_ref, b_ref, *refs):
    out_ref = refs[-1]
    out_ref[0 : a_ref.shape[0]] = a_ref[...]
    out_ref[a_ref.shape[0] :] = b_ref[...]


def stack(a, b, *after):
    shape = (a.shape[0] + b.shape[0],) + a.shape[1:]
    return call(stack_kernel, [(shape, BF)], [], (VMEM,) * (2 + len(after)), vmem=4)(a, b, *after)[0]


def call(kernel, outs, scratch, spaces, flops=0, vmem=12):
    return pl.pallas_call(
        kernel,
        out_shape=tuple(jax.ShapeDtypeStruct(s, d) for s, d in outs),
        in_specs=jax.tree.map(lambda space: pl.BlockSpec(memory_space=space), spaces),
        out_specs=tuple(pl.BlockSpec(memory_space=VMEM) for _ in outs),
        scratch_shapes=scratch,
        compiler_params=pltpu.CompilerParams(vmem_limit_bytes=vmem * MIB),
        cost_estimate=pl.CostEstimate(flops=flops, bytes_accessed=2 * MIB, transcendentals=0),
    )


def body(volume, w_first, w_enc, w_down, w_bottom, w_up, w_join, cotangent):
    n = lax.axis_size("space")
    crops = lax.axis_size("section")
    _, sx, ny, nz, c0 = volume.shape
    c1, c2 = w_enc.shape[1], w_bottom.shape[1]
    plane, nx = ny * nz, sx * n
    rows = nx * plane
    cplane, crows = plane // 4, rows // 8
    own_rows = sx * plane // 2 + sx * plane
    (near,) = call(
        functools.partial(join_kernel, sx, plane),
        [((1, own_rows, LANES), BF)],
        [pltpu.VMEM((sx, plane, c0), BF), pltpu.SemaphoreType.DMA((2,))],
        (HBM, HBM),
        vmem=4,
    )(in_hbm(volume.reshape(sx, plane, c0)), in_hbm(cotangent.reshape(sx * plane, c1)))
    held_bottom, back_bottom = call(
        flip_kernel,
        [(w_bottom.shape, BF)] * 2,
        [pltpu.SemaphoreType.DMA((3,))],
        (VMEM, HBM),
        flops=10**9,
    )(near, in_hbm(w_bottom))
    held, step = [0], n // 2
    while step > 2:
        held = held + [m ^ step for m in held]
        near = stack(near, exchange(near, "space", step), back_bottom)
        step //= 2
    weights = [w_first, w_enc, w_down, w_up, w_join]
    weights = call(
        stage_kernel,
        [(w.shape, BF) for w in weights],
        [pltpu.SemaphoreType.DMA((len(weights),))],
        (VMEM, [HBM] * len(weights)),
        flops=10**9,
    )(near, [in_hbm(w) for w in weights])
    weights = [*weights[:3], held_bottom, *weights[3:]]
    last = [m for m in (2, 3, 1) if m < n]
    gathered = [near] + [exchange(near, "space", mask) for mask in last]
    masks = tuple(tuple(m ^ mask for m in held) for mask in (0, *last))

    fine_own, wide_own = c1 // n, c2 // n
    shapes = {
        "first": (fine_own, 27 * c0),
        "enc": (fine_own, 27 * c1),
        "down": (wide_own, 8 * c1),
        "bottom": (wide_own, 27 * c2),
        "up": (8 * c1 // n, c2),
        "join": (fine_own, 54 * c1),
    }

    def layout(names):
        spots, at = {}, 0
        for name in names:
            spots[name] = at
            count, width = shapes[name]
            at += count * -(-width // LANES)
        return spots, -(-at // 32) * 32

    upper_spots, upper_rows = layout(("up", "join"))
    lower_spots, lower_rows = layout(("down", "enc", "first"))
    geo = (n, sx, ny, nz, c0, c1, c2, masks)
    fine, coarse = (nx, ny, nz), (nx // 2, ny // 2, nz // 2)
    size = upper_rows // 2
    act_rows = c2 // LANES * crows + crows // LANES * wide_own
    own, keep, send, vol2, z1, h1, z2, blocks, z3, t4, ut = call(
        functools.partial(upper_kernel, geo + (upper_spots,)),
        [
            ((sx * plane, c1), BF),
            ((size + act_rows, LANES), BF),
            ((size, LANES), BF),
            ((rows, 2 * c0), BF),
            ((rows, c1), F32),
            ((rows, c1), BF),
            ((rows, c1), F32),
            ((crows, 8 * c1), BF),
            ((crows, c2), F32),
            ((crows, c2), BF),
            ((rows, 3 * c1), BF),
        ],
        [
            pltpu.VMEM((n, own_rows, LANES), BF),
            pltpu.VMEM((rows, 2 * LANES), BF),
            pltpu.VMEM((rows, 3 * c1), BF),
            pltpu.VMEM((rows, 6 * c1), BF),
            pltpu.VMEM((crows + 2 * cplane, 9 * c2), BF),
            pltpu.VMEM((rows, 2 * c1), BF),
            pltpu.VMEM((crows, 8 * c1), BF),
            pltpu.VMEM((rows, c1), BF),
            pltpu.VMEM((upper_rows, LANES), BF),
        ],
        ([VMEM] * len(gathered), [VMEM] * len(weights)),
        flops=10**10,
        vmem=14,
    )(gathered, weights)
    (skip_back,) = call(
        functools.partial(skip_kernel, fine, c1),
        [((rows, c1), F32)],
        [],
        (VMEM, VMEM),
        flops=10**9,
    )(ut, weights[5])
    total = between_cores(keep, send, skip_back)

    low_size = lower_rows // 2
    down, t2, t1 = call(
        functools.partial(lower_kernel, geo + (lower_spots,)),
        [((lower_spots["enc"], LANES), BF), ((rows, c1), BF), ((rows, c1), BF)],
        [pltpu.VMEM((crows + 2 * cplane, 9 * c2), BF), pltpu.VMEM((rows, 3 * c1), BF)],
        (VMEM,) * 9,
        flops=6 * 10**9,
    )(weights[1], weights[2], back_bottom, z1, z2, blocks, z3, t4, skip_back)
    low_keep, low_send = call(
        functools.partial(first_kernel, geo + (lower_spots,)),
        [((low_size, LANES), BF), ((low_size, LANES), BF)],
        [pltpu.VMEM((lower_rows, LANES), BF)],
        (VMEM,) * 5,
        flops=10**9,
    )(down, t2, t1, h1, vol2)
    low_total = between_cores(low_keep, low_send)
    total, other = between_chips(total, size, crops, low_total)
    factor = 1.0 / math.sqrt(crops * rows)
    decoded, grad_bottom, grad_up, grad_join, token = call(
        functools.partial(finish_first, factor, upper_spots, coarse),
        [
            ((sx * plane, c1), BF),
            (shapes["bottom"], F32),
            (shapes["up"][::-1], F32),
            (shapes["join"], F32),
            ((8, LANES), F32),
        ],
        [pltpu.VMEM((2, size, LANES), BF), pltpu.VMEM((crops, act_rows, LANES), BF)],
        (VMEM, VMEM, VMEM),
        vmem=12,
    )(own, total, other)
    low_total, low_other = between_chips(low_total, low_size, crops, token)
    grad_first, grad_enc, grad_down = call(
        functools.partial(finish_second, factor, lower_spots),
        [(shapes[name], F32) for name in ("first", "enc", "down")],
        [pltpu.VMEM((2, low_size, LANES), BF)],
        (VMEM, VMEM),
        vmem=8,
    )(low_total, low_other)
    return (
        decoded.reshape((1, sx, ny, nz, c1)),
        grad_first.T,
        grad_enc.T,
        grad_down.T,
        grad_bottom.T,
        grad_up,
        grad_join.T,
    )


def solution(mesh):
    field = P("section", "space", None, None, None)
    split = P(None, "space")
    return jax.shard_map(
        body,
        mesh=mesh,
        in_specs=(field,) + (P(),) * 6 + (field,),
        out_specs=(field,) + (split,) * 6,
        check_vma=False,
    )
```

```python
import functools
import math

import jax
import jax.numpy as jnp
from jax import lax
from jax.experimental import pallas as pl
from jax.experimental.pallas import tpu as pltpu
from jax.sharding import PartitionSpec as P

BF = jnp.bfloat16
F32 = jnp.float32
LANES = 128
MIB = 1024 * 1024
VMEM = pltpu.MemorySpace.VMEM
HBM = pltpu.MemorySpace.HBM


def dot(a, b):
    return jnp.dot(a, b, preferred_element_type=F32)


def dot_t(a, b):
    return lax.dot_general(a, b, (((1,), (1,)), ((), ())), preferred_element_type=F32)


def sigmoid(z):
    return jax.nn.sigmoid(z)


def silu(z):
    return (z * sigmoid(z)).astype(BF)


def slope(z):
    s = sigmoid(z)
    return s * (1.0 + z * (1.0 - s))


def mod(index, size):
    return index & (size - 1) if size & (size - 1) == 0 else lax.rem(index, size)


def over(index, size):
    if size & (size - 1) == 0:
        return lax.shift_right_logical(index, size.bit_length() - 1)
    return lax.div(index, size)


def z_windows(field, size_z):
    rows = field.shape[0]
    at_z = mod(lax.broadcasted_iota(jnp.int32, field.shape, 0), size_z)
    out = []
    for oz in (-1, 0, 1):
        part = field
        if oz:
            part = pltpu.roll(field, (-oz) % rows, 0)
            part = jnp.where(at_z == (size_z - 1 if oz > 0 else 0), 0.0, part)
        out.append(part)
    return out


def yz_windows(field, size_y, size_z):
    rows = field.shape[0]
    place = lax.broadcasted_iota(jnp.int32, field.shape, 0)
    at_y = mod(over(place, size_z), size_y)
    shifted = z_windows(field, size_z)
    out = []
    for oy in (-1, 0, 1):
        for part in shifted:
            if oy:
                part = pltpu.roll(part, (-oy * size_z) % rows, 0)
                part = jnp.where(at_y == (size_y - 1 if oy > 0 else 0), 0.0, part)
            out.append(part)
    return out


def fill(u_ref, parts, plane=0, offset=0, stride=None):
    rows, width = parts[0].shape
    stride = width if stride is None else stride
    for t, part in enumerate(parts):
        lane = t * stride + offset
        u_ref[plane : plane + rows, lane : lane + width] = part.astype(BF)


def clear_rims(u_ref, plane):
    rows, lanes = u_ref.shape
    zero = jnp.zeros((plane, lanes), BF)
    u_ref[0:plane, :] = zero
    u_ref[rows - plane : rows, :] = zero


def moved(field, ox, oy):
    nx, ny, nz, width = field.shape
    if ox:
        rim = jnp.zeros((1, ny, nz, width), F32)
        field = jnp.concatenate([field[1:], rim] if ox > 0 else [rim, field[:-1]], 0)
    if oy:
        rim = jnp.zeros((nx, 1, nz, width), F32)
        field = jnp.concatenate([field[:, 1:], rim] if oy > 0 else [rim, field[:, :-1]], 1)
    return field


def grouped(width, extent, product):
    total = None
    for first in range(0, 9, 2):
        groups = [first, first + 1] if first < 8 else [first]
        both = product(groups)
        for i, g in enumerate(groups):
            part = both[:, i * width : (i + 1) * width].reshape(extent + (width,))
            part = moved(part, g // 3 - 1, g % 3 - 1)
            total = part if total is None else total + part
    return total.reshape(-1, width)


def conv_z(uz, w_ref, extent):
    depth = w_ref.shape[0] // 9

    def product(groups):
        side = [w_ref[g * depth : (g + 1) * depth, :] for g in groups]
        return dot(uz, side[0] if len(side) == 1 else jnp.concatenate(side, 1))

    return grouped(w_ref.shape[1], extent, product)


def conv_z_back(uz, w_ref, extent, low=0, high=None):
    every = w_ref.shape[0] // 27
    high = every if high is None else high
    width = high - low

    def product(groups):
        side = []
        for g in groups:
            taps = [(8 - g) * 3 + 2 - t for t in range(3)]
            side.append(jnp.concatenate([w_ref[p * every + low : p * every + high, :] for p in taps], 1))
        return dot_t(uz, side[0] if len(side) == 1 else jnp.concatenate(side, 0))

    return grouped(width, extent, product)


def conv(u_ref, w_ref, rows, plane):
    depth = u_ref.shape[1]
    total = None
    for ox in range(3):
        part = dot(u_ref[ox * plane : ox * plane + rows, :], w_ref[ox * depth : (ox + 1) * depth, :])
        total = part if total is None else total + part
    return total


def own_columns(field, count, position):
    shape = (count, field.shape[1])
    wanted = lax.broadcasted_iota(jnp.int32, shape, 0) + position * count
    pick = (lax.broadcasted_iota(jnp.int32, shape, 1) == wanted).astype(F32).astype(BF)
    return dot_t(pick, field)


def tap_shifts(grad, extent, depths=(-1, 0, 1)):
    nx, ny, nz = extent
    count, rows = grad.shape
    place = lax.broadcasted_iota(jnp.int32, grad.shape, 1)
    at = (over(place, ny * nz), mod(over(place, nz), ny), mod(place, nz))
    parts = []
    for ox in (-1, 0, 1):
        for oy in (-1, 0, 1):
            for oz in depths:
                by = ((ox * ny) + oy) * nz + oz
                part = pltpu.roll(grad, by % rows, 1) if by else grad
                inside = None
                for index, size, o in zip(at, extent, (ox, oy, oz)):
                    if o:
                        here = index != (0 if o > 0 else size - 1)
                        inside = here if inside is None else inside & here
                parts.append(part if inside is None else jnp.where(inside, part, 0.0))
    return jnp.concatenate(parts, 0).astype(BF)


def tap_grad(grad, field, extent):
    return dot(tap_shifts(grad, extent), field)


def split(pack, keep_ref, send_ref, core):
    size = send_ref.shape[0]
    keep_ref[0:size, :] = pack[pl.ds(pl.multiple_of(core * size, size), size), :]
    send_ref[...] = pack[pl.ds(pl.multiple_of((1 - core) * size, size), size), :]


def emit(pack_ref, spot, grad, taps=1):
    count, width = grad.shape[0] // taps, grad.shape[1]
    at = spot
    if width == LANES:
        pack_ref[at : at + taps * count, :] = grad.astype(BF)
        return
    for tap in range(taps):
        for v in range(0, width, LANES):
            pack_ref[at : at + count, :] = grad[tap * count : (tap + 1) * count, v : v + LANES].astype(BF)
            at += count


def one_hot(ny, nz, back):
    plane = ny * nz
    shape = (2 * plane, 2 * plane)
    row = lax.broadcasted_iota(jnp.int32, shape, 1 if back else 0)
    column = lax.broadcasted_iota(jnp.int32, shape, 0 if back else 1)
    tap, at = over(row, plane // 4), mod(row, plane // 4)
    ox, oy, oz = over(tap, 4), mod(over(tap, 2), 2), mod(tap, 2)
    y, z = over(at, nz // 2), mod(at, nz // 2)
    wanted = ox * plane + (2 * y + oy) * nz + 2 * z + oz
    return (column == wanted).astype(F32).astype(BF)


def to_blocks(shuffle, field, d_ref, pairs, plane):
    width = field.shape[1]
    for i in range(pairs):
        mixed = dot(shuffle, field[i * 8 * plane : (i + 1) * 8 * plane]).astype(BF)
        for t in range(8):
            d_ref[i * plane : (i + 1) * plane, t * width : (t + 1) * width] = mixed[
                t * plane : (t + 1) * plane
            ]


def from_blocks(unshuffle, flat, pairs, plane, width):
    parts = []
    for i in range(pairs):
        rows = flat[i * plane : (i + 1) * plane]
        stacked = jnp.concatenate([rows[:, t * width : (t + 1) * width] for t in range(8)], axis=0)
        parts.append(dot(unshuffle, stacked))
    return jnp.concatenate(parts, axis=0)


def join_kernel(sx, plane, volume_hbm, cotangent_hbm, out_ref, volume_ref, arrived):
    first = pltpu.make_async_copy(volume_hbm, volume_ref, arrived.at[0])
    second = pltpu.make_async_copy(cotangent_hbm, out_ref.at[0, sx // 2 * plane :], arrived.at[1])
    first.start()
    second.start()
    first.wait()
    for i in range(sx // 2):
        pair = [volume_ref[2 * i + k].astype(F32) for k in range(2)]
        out_ref[0, i * plane : (i + 1) * plane, :] = jnp.concatenate(pair, 1).astype(BF)
    second.wait()


def stage_kernel(near_ref, sources, *refs):
    del near_ref
    *held, arrived = refs
    copies = [pltpu.make_async_copy(a, b, arrived.at[i]) for i, (a, b) in enumerate(zip(sources, held))]
    for copy in copies:
        copy.start()
    for copy in copies:
        copy.wait()


def flip_kernel(near_ref, source, held, flipped, arrived):
    del near_ref
    width = source.shape[0] // 27
    parts = [slice(i * 9 * width, (i + 1) * 9 * width) for i in range(3)]
    copies = [
        pltpu.make_async_copy(source.at[part], held.at[part], arrived.at[i]) for i, part in enumerate(parts)
    ]
    for copy in copies:
        copy.start()
    for i, copy in enumerate(copies):
        copy.wait()
        for tap in range(9 * i, 9 * i + 9):
            to = 26 - tap
            flipped[to * width : (to + 1) * width, :] = held[tap * width : (tap + 1) * width, :].T


def upper_kernel(
    geo,
    gathered,
    weights,
    own_ref,
    keep_ref,
    send_ref,
    vol_ref,
    z1_ref,
    h1_ref,
    z2_ref,
    d_ref,
    z3_ref,
    t4_ref,
    ut,
    blocks,
    uv,
    u1,
    uj,
    uc,
    joined,
    lb_ref,
    out_map,
    pack,
):
    (n, sx, ny, nz, c0, c1, c2, masks, spots) = geo
    position = lax.axis_index("space")
    w_first, w_enc, w_down, w_bottom, w_up, w_join = weights
    shuffle, unshuffle = one_hot(ny, nz, False), one_hot(ny, nz, True)
    plane, nx = ny * nz, sx * n
    rows = nx * plane
    cplane, cx = plane // 4, nx // 2
    crows = cx * cplane
    fine, coarse = (nx, ny, nz), (cx, ny // 2, nz // 2)
    for source, held in zip(gathered, masks):
        for m, mask in enumerate(held):
            blocks[lax.bitwise_xor(position, mask)] = source[m]

    lane = lax.broadcasted_iota(jnp.int32, (plane, LANES), 1)
    vol_rows = sx // 2 * plane
    planes = []
    for j in range(n):
        for i in range(sx // 2):
            pair = blocks[j, i * plane : (i + 1) * plane, :].astype(F32)
            turned = pltpu.roll(pair, c0, 1)
            planes.append(jnp.where(lane < c0, pair, turned))
            planes.append(jnp.where(lane < c0, turned, pair))
    twice = jnp.concatenate(planes, 0)
    vol_ref[...] = twice.astype(BF)
    before, middle, after = z_windows(twice, nz)
    lane = lax.broadcasted_iota(jnp.int32, (rows, LANES), 1)
    uv[:, 0:LANES] = jnp.where(lane < c0, before, middle).astype(BF)
    uv[:, LANES:] = after.astype(BF)
    z1 = conv_z(uv[:, 0 : 3 * c0], w_first, fine)
    z1_ref[...] = z1
    h1 = silu(z1)
    h1_ref[...] = h1
    fill(u1, z_windows(h1.astype(F32), nz))
    z2 = conv_z(u1[...], w_enc, fine)
    z2_ref[...] = z2
    skip = silu(z2)
    joined[:, c1:] = skip
    fill(uj, z_windows(skip.astype(F32), nz), 0, c1, 2 * c1)
    to_blocks(shuffle, skip, d_ref, cx, cplane)
    z3 = dot(d_ref[...], w_down[...])
    z3_ref[...] = z3
    g1 = silu(z3)
    clear_rims(uc, cplane)
    fill(uc, yz_windows(g1.astype(F32), *coarse[1:]), cplane)
    z4 = conv(uc, w_bottom, crows, cplane)
    g2 = silu(z4)
    lifted = from_blocks(unshuffle, dot(g2, w_up[...]).astype(BF), cx, cplane, c1)
    joined[:, 0:c1] = lifted.astype(BF)
    fill(uj, z_windows(lifted, nz), 0, 0, 2 * c1)
    z7 = conv_z(uj[...], w_join, fine)
    out_map[...] = silu(z7)
    kept = sx * plane
    own_ref[...] = out_map[pl.ds(pl.multiple_of(position * kept, kept), kept), :]

    cot = jnp.concatenate([blocks[j, vol_rows:, :] for j in range(n)], 0).astype(F32)
    t7 = (cot * slope(z7)).astype(BF)
    fill(ut, z_windows(t7.astype(F32), nz))
    e_lift = conv_z_back(ut[...], w_join, fine, 0, c1).astype(BF)
    to_blocks(shuffle, e_lift, lb_ref, cx, cplane)
    e3 = dot_t(lb_ref[...], w_up[...]).astype(BF).astype(F32)
    t4 = (e3 * slope(z4)).astype(BF)
    t4_ref[...] = t4
    emit(pack, spots["up"], dot(own_columns(lb_ref[...], 8 * c1 // n, position).astype(BF), g2))
    taps = dot(tap_shifts(own_columns(t7, c1 // n, position), fine, (0,)), uj[...])
    emit(pack, spots["join"], taps, 9)
    split(pack, keep_ref, send_ref, lax.rem(lax.axis_index("section"), 2))
    at = send_ref.shape[0]
    for v in range(0, c2, LANES):
        keep_ref[at : at + crows, :] = g1[:, v : v + LANES]
        at += crows
    mine = own_columns(t4, c2 // n, position).astype(BF)
    for v in range(0, crows, LANES):
        keep_ref[at : at + c2 // n, :] = mine[:, v : v + LANES]
        at += c2 // n


def skip_kernel(extent, c1, ut, w_join, out_ref):
    out_ref[...] = conv_z_back(ut[...], w_join, extent, c1, 2 * c1)


def lower_kernel(
    geo,
    w_enc,
    w_down,
    back_bottom,
    z1_ref,
    z2_ref,
    d_ref,
    z3_ref,
    t4_ref,
    skip_back_ref,
    pack,
    t2_ref,
    t1_ref,
    utc,
    ut,
):
    (n, sx, ny, nz, c0, c1, c2, masks, spots) = geo
    position = lax.axis_index("space")
    plane, nx = ny * nz, sx * n
    cplane, cx = plane // 4, nx // 2
    crows = cx * cplane
    fine, coarse = (nx, ny, nz), (cx, ny // 2, nz // 2)
    unshuffle = one_hot(ny, nz, True)
    clear_rims(utc, cplane)
    fill(utc, yz_windows(t4_ref[...].astype(F32), *coarse[1:]), cplane)
    e4 = conv(utc, back_bottom, crows, cplane).astype(BF).astype(F32)
    t3 = (e4 * slope(z3_ref[...])).astype(BF)
    emit(pack, spots["down"], dot(own_columns(t3, c2 // n, position).astype(BF), d_ref[...]))
    e5 = dot_t(t3, w_down[...])
    high = e5.astype(BF)
    low = (e5 - high.astype(F32)).astype(BF)
    e5 = from_blocks(unshuffle, high, cx, cplane, c1) + from_blocks(
        unshuffle, low, cx, cplane, c1
    )
    t2 = ((e5 + skip_back_ref[...]) * slope(z2_ref[...])).astype(BF)
    fill(ut, z_windows(t2.astype(F32), nz))
    t2_ref[...] = t2
    e6 = conv_z_back(ut[...], w_enc, fine).astype(BF).astype(F32)
    t1_ref[...] = (e6 * slope(z1_ref[...])).astype(BF)


def first_kernel(geo, down_ref, t2_ref, t1_ref, h1_ref, vol_ref, keep_ref, send_ref, pack):
    (n, sx, ny, nz, c0, c1, c2, masks, spots) = geo
    position = lax.axis_index("space")
    fine = (sx * n, ny, nz)
    count = c1 // n
    pack[0 : down_ref.shape[0], :] = down_ref[...]
    emit(pack, spots["enc"], tap_grad(own_columns(t2_ref[...], count, position), h1_ref[...], fine), 27)
    taps = tap_grad(own_columns(t1_ref[...], count, position), vol_ref[...], fine)
    lane = lax.broadcasted_iota(jnp.int32, (count, LANES), 1)
    at = spots["first"]
    for tap in range(0, 27, 2):
        a = taps[tap * count : (tap + 1) * count]
        b = taps[(tap + 1) * count : (tap + 2) * count] if tap < 26 else a
        pack[at : at + count, :] = jnp.where(lane < c0, a, b).astype(BF)
        at += count
    split(pack, keep_ref, send_ref, lax.rem(lax.axis_index("section"), 2))


def unpack(source, spot, out, factor):
    count, width = out.shape
    at = spot
    for v in range(0, width, LANES):
        take = min(LANES, width - v)
        out[:, v : v + take] = (source(at, count) * factor)[:, :take]
        at += count


def halves(both, mine_ref, other_ref, core):
    size = both.shape[1]
    both[core] = mine_ref[0:size, :]
    both[1 - core] = other_ref[0:size, :]

    def source(at, count):
        if (at + count - 1) // size == at // size:
            return both[at // size, at % size : at % size + count, :].astype(F32)
        cut = size - at % size
        return jnp.concatenate(
            [both[0, size - cut : size, :].astype(F32), both[1, 0 : count - cut, :].astype(F32)], 0
        )

    return source


def finish_first(factor, spots, extent, *refs):
    own_ref, mine_ref, other_ref, decoded_ref, bottom_ref, up_ref, join_ref, token, both, acts = refs
    decoded_ref[...] = own_ref[...]
    token[...] = jnp.zeros(token.shape, F32)
    section = lax.axis_index("section")
    size = both.shape[1]
    source = halves(both, mine_ref, other_ref, lax.rem(section, 2))
    unpack(source, spots["join"], join_ref, factor)
    rows, width = up_ref.shape[1], up_ref.shape[0]
    for v in range(0, width, LANES):
        up_ref[v : v + LANES, :] = (source(spots["up"] + v // LANES * rows, rows) * factor).T

    crops, each = acts.shape[0], acts.shape[1]
    for j in range(crops // 2):
        part = slice(size + j * each, size + (j + 1) * each)
        acts[lax.bitwise_xor(section, 2 * j)] = mine_ref[part, :]
        acts[lax.bitwise_xor(section, 2 * j + 1)] = other_ref[part, :]
    voxels = extent[0] * extent[1] * extent[2]
    count, wide = bottom_ref.shape[0], bottom_ref.shape[1] // 27
    shifted, fields = [], []
    for crop in range(crops):
        at = wide // LANES * voxels
        fields.append(
            jnp.concatenate([acts[crop, v : v + voxels, :] for v in range(0, at, voxels)], 1)
        )
        own = [acts[crop, v : v + count, :] for v in range(at, each, count)]
        shifted.append(tap_shifts(jnp.concatenate(own, 1).astype(F32), extent))
    grad = dot(jnp.concatenate(shifted, 1), jnp.concatenate(fields, 0)) * factor
    for tap in range(27):
        bottom_ref[:, tap * wide : (tap + 1) * wide] = grad[tap * count : (tap + 1) * count]


def finish_second(factor, spots, mine_ref, other_ref, first_ref, enc_ref, down_ref, both):
    source = halves(both, mine_ref, other_ref, lax.rem(lax.axis_index("section"), 2))
    unpack(source, spots["down"], down_ref, factor)
    unpack(source, spots["first"], first_ref, factor)
    unpack(source, spots["enc"], enc_ref, factor)


def merge_kernel(size, a_ref, b_ref, *refs):
    out_ref = refs[-1]
    out_ref[0:size, :] = (a_ref[0:size, :].astype(F32) + b_ref[0:size, :].astype(F32)).astype(BF)
    at = size
    for ref in (a_ref, b_ref):
        rest = ref.shape[0] - size
        if rest:
            out_ref[at : at + rest, :] = ref[size:, :]
            at += rest


def merge(a, b, size, *after):
    shape = (a.shape[0] + b.shape[0] - size, LANES)
    kernel = functools.partial(merge_kernel, size)
    return call(kernel, [(shape, BF)], [], (VMEM,) * (2 + len(after)), vmem=4)(a, b, *after)[0]


def between_cores(keep, send, *after):
    return merge(keep, exchange(send, "section", 1), send.shape[0], *after)


def between_chips(total, size, crops, *after):
    mask = 2
    while mask < crops:
        mask *= 2
        last = after if mask >= crops else ()
        total = merge(total, exchange(total, "section", mask // 2), size, *last)
    return total, exchange(total, "section", 1)


def in_hbm(array):
    return pltpu.with_memory_space_constraint(array, HBM)


def exchange(array, axis, mask):
    devices = lax.axis_size(axis)
    return lax.ppermute(array, axis, [(i, i ^ mask) for i in range(devices)])


def merge_kernel(size, a_ref, b_ref, *refs):
    out_ref = refs[-1]
    out_ref[0:size, :] = (a_ref[0:size, :].astype(F32) + b_ref[0:size, :].astype(F32)).astype(BF)
    at = size
    for ref in (a_ref, b_ref):
        rest = ref.shape[0] - size
        if rest:
            out_ref[at : at + rest, :] = ref[size:, :]
            at += rest


def merge(a, b, size, *after):
    shape = (a.shape[0] + b.shape[0] - size, LANES)
    kernel = functools.partial(merge_kernel, size)
    return call(kernel, [(shape, BF)], [], (VMEM,) * (2 + len(after)), vmem=4)(a, b, *after)[0]


def reduced(keep, send, crops, after=()):
    size = send.shape[0]
    total = merge(keep, exchange(send, "section", 1), size)
    mask = 2
    while mask < crops:
        mask *= 2
        total = merge(total, exchange(total, "section", mask // 2), size, *(after if mask >= crops else ()))
    return total, exchange(total, "section", 1)


def stack_kernel(a_ref, b_ref, *refs):
    out_ref = refs[-1]
    out_ref[0 : a_ref.shape[0]] = a_ref[...]
    out_ref[a_ref.shape[0] :] = b_ref[...]


def stack(a, b, *after):
    shape = (a.shape[0] + b.shape[0],) + a.shape[1:]
    return call(stack_kernel, [(shape, BF)], [], (VMEM,) * (2 + len(after)), vmem=4)(a, b, *after)[0]


def call(kernel, outs, scratch, spaces, flops=0, vmem=12):
    return pl.pallas_call(
        kernel,
        out_shape=tuple(jax.ShapeDtypeStruct(s, d) for s, d in outs),
        in_specs=jax.tree.map(lambda space: pl.BlockSpec(memory_space=space), spaces),
        out_specs=tuple(pl.BlockSpec(memory_space=VMEM) for _ in outs),
        scratch_shapes=scratch,
        compiler_params=pltpu.CompilerParams(vmem_limit_bytes=vmem * MIB),
        cost_estimate=pl.CostEstimate(flops=flops, bytes_accessed=2 * MIB, transcendentals=0),
    )


def body(volume, w_first, w_enc, w_down, w_bottom, w_up, w_join, cotangent):
    n = lax.axis_size("space")
    crops = lax.axis_size("section")
    _, sx, ny, nz, c0 = volume.shape
    c1, c2 = w_enc.shape[1], w_bottom.shape[1]
    plane, nx = ny * nz, sx * n
    rows = nx * plane
    cplane, crows = plane // 4, rows // 8
    own_rows = sx * plane // 2 + sx * plane
    (near,) = call(
        functools.partial(join_kernel, sx, plane),
        [((1, own_rows, LANES), BF)],
        [pltpu.VMEM((sx, plane, c0), BF), pltpu.SemaphoreType.DMA((2,))],
        (HBM, HBM),
        vmem=4,
    )(in_hbm(volume.reshape(sx, plane, c0)), in_hbm(cotangent.reshape(sx * plane, c1)))
    held_bottom, back_bottom = call(
        flip_kernel,
        [(w_bottom.shape, BF)] * 2,
        [pltpu.SemaphoreType.DMA((3,))],
        (VMEM, HBM),
        flops=10**9,
    )(near, in_hbm(w_bottom))
    held, step = [0], n // 2
    while step > 2:
        held = held + [m ^ step for m in held]
        near = stack(near, exchange(near, "space", step), back_bottom)
        step //= 2
    weights = [w_first, w_enc, w_down, w_up, w_join]
    weights = call(
        stage_kernel,
        [(w.shape, BF) for w in weights],
        [pltpu.SemaphoreType.DMA((len(weights),))],
        (VMEM, [HBM] * len(weights)),
        flops=10**9,
    )(near, [in_hbm(w) for w in weights])
    weights = [*weights[:3], held_bottom, *weights[3:]]
    last = [m for m in (2, 3, 1) if m < n]
    gathered = [near] + [exchange(near, "space", mask) for mask in last]
    masks = tuple(tuple(m ^ mask for m in held) for mask in (0, *last))

    fine_own, wide_own = c1 // n, c2 // n
    shapes = {
        "first": (fine_own, 27 * c0),
        "enc": (fine_own, 27 * c1),
        "down": (wide_own, 8 * c1),
        "bottom": (wide_own, 27 * c2),
        "up": (8 * c1 // n, c2),
        "join": (fine_own, 54 * c1),
    }

    def layout(names):
        spots, at = {}, 0
        for name in names:
            spots[name] = at
            count, width = shapes[name]
            at += count * -(-width // LANES)
        return spots, -(-at // 32) * 32

    upper_spots, upper_rows = layout(("up", "join"))
    lower_spots, lower_rows = layout(("down", "enc", "first"))
    geo = (n, sx, ny, nz, c0, c1, c2, masks)
    fine, coarse = (nx, ny, nz), (nx // 2, ny // 2, nz // 2)
    size = upper_rows // 2
    act_rows = c2 // LANES * crows + crows // LANES * wide_own
    own, keep, send, vol2, z1, h1, z2, blocks, z3, t4, ut = call(
        functools.partial(upper_kernel, geo + (upper_spots,)),
        [
            ((sx * plane, c1), BF),
            ((size + act_rows, LANES), BF),
            ((size, LANES), BF),
            ((rows, 2 * c0), BF),
            ((rows, c1), F32),
            ((rows, c1), BF),
            ((rows, c1), F32),
            ((crows, 8 * c1), BF),
            ((crows, c2), F32),
            ((crows, c2), BF),
            ((rows, 3 * c1), BF),
        ],
        [
            pltpu.VMEM((n, own_rows, LANES), BF),
            pltpu.VMEM((rows, 2 * LANES), BF),
            pltpu.VMEM((rows, 3 * c1), BF),
            pltpu.VMEM((rows, 6 * c1), BF),
            pltpu.VMEM((crows + 2 * cplane, 9 * c2), BF),
            pltpu.VMEM((rows, 2 * c1), BF),
            pltpu.VMEM((crows, 8 * c1), BF),
            pltpu.VMEM((rows, c1), BF),
            pltpu.VMEM((upper_rows, LANES), BF),
        ],
        ([VMEM] * len(gathered), [VMEM] * len(weights)),
        flops=10**10,
        vmem=14,
    )(gathered, weights)
    (skip_back,) = call(
        functools.partial(skip_kernel, fine, c1),
        [((rows, c1), F32)],
        [],
        (VMEM, VMEM),
        flops=10**9,
    )(ut, weights[5])
    total = between_cores(keep, send, skip_back)

    low_size = lower_rows // 2
    down, t2, t1 = call(
        functools.partial(lower_kernel, geo + (lower_spots,)),
        [((lower_spots["enc"], LANES), BF), ((rows, c1), BF), ((rows, c1), BF)],
        [pltpu.VMEM((crows + 2 * cplane, 9 * c2), BF), pltpu.VMEM((rows, 3 * c1), BF)],
        (VMEM,) * 9,
        flops=6 * 10**9,
    )(weights[1], weights[2], back_bottom, z1, z2, blocks, z3, t4, skip_back)
    low_keep, low_send = call(
        functools.partial(first_kernel, geo + (lower_spots,)),
        [((low_size, LANES), BF), ((low_size, LANES), BF)],
        [pltpu.VMEM((lower_rows, LANES), BF)],
        (VMEM,) * 5,
        flops=10**9,
    )(down, t2, t1, h1, vol2)
    low_total = between_cores(low_keep, low_send)
    total, other = between_chips(total, size, crops, low_total)
    factor = 1.0 / math.sqrt(crops * rows)
    decoded, grad_bottom, grad_up, grad_join, token = call(
        functools.partial(finish_first, factor, upper_spots, coarse),
        [
            ((sx * plane, c1), BF),
            (shapes["bottom"], F32),
            (shapes["up"][::-1], F32),
            (shapes["join"], F32),
            ((8, LANES), F32),
        ],
        [pltpu.VMEM((2, size, LANES), BF), pltpu.VMEM((crops, act_rows, LANES), BF)],
        (VMEM, VMEM, VMEM),
        vmem=12,
    )(own, total, other)
    low_total, low_other = between_chips(low_total, low_size, crops, token)
    grad_first, grad_enc, grad_down = call(
        functools.partial(finish_second, factor, lower_spots),
        [(shapes[name], F32) for name in ("first", "enc", "down")],
        [pltpu.VMEM((2, low_size, LANES), BF)],
        (VMEM, VMEM),
        vmem=8,
    )(low_total, low_other)
    return (
        decoded.reshape((1, sx, ny, nz, c1)),
        grad_first.T,
        grad_enc.T,
        grad_down.T,
        grad_bottom.T,
        grad_up,
        grad_join.T,
    )


def solution(mesh):
    field = P("section", "space", None, None, None)
    split = P(None, "space")
    return jax.shard_map(
        body,
        mesh=mesh,
        in_specs=(field,) + (P(),) * 6 + (field,),
        out_specs=(field,) + (split,) * 6,
        check_vma=False,
    )
```

```python
import functools
import math

import jax
import jax.numpy as jnp
from jax import lax
from jax.experimental import pallas as pl
from jax.experimental.pallas import tpu as pltpu
from jax.sharding import PartitionSpec as P

BF = jnp.bfloat16
F32 = jnp.float32
LANES = 128
MIB = 1024 * 1024
VMEM = pltpu.MemorySpace.VMEM
HBM = pltpu.MemorySpace.HBM


def dot(a, b):
    return jnp.dot(a, b, preferred_element_type=F32)


def dot_t(a, b):
    return lax.dot_general(a, b, (((1,), (1,)), ((), ())), preferred_element_type=F32)


def sigmoid(z):
    return jax.nn.sigmoid(z)


def silu(z):
    return (z * sigmoid(z)).astype(BF)


def slope(z):
    s = sigmoid(z)
    return s * (1.0 + z * (1.0 - s))


def mod(index, size):
    return index & (size - 1) if size & (size - 1) == 0 else lax.rem(index, size)


def over(index, size):
    if size & (size - 1) == 0:
        return lax.shift_right_logical(index, size.bit_length() - 1)
    return lax.div(index, size)


def z_windows(field, size_z):
    rows = field.shape[0]
    at_z = mod(lax.broadcasted_iota(jnp.int32, field.shape, 0), size_z)
    out = []
    for oz in (-1, 0, 1):
        part = field
        if oz:
            part = pltpu.roll(field, (-oz) % rows, 0)
            part = jnp.where(at_z == (size_z - 1 if oz > 0 else 0), 0.0, part)
        out.append(part)
    return out


def yz_windows(field, size_y, size_z):
    rows = field.shape[0]
    place = lax.broadcasted_iota(jnp.int32, field.shape, 0)
    at_y = mod(over(place, size_z), size_y)
    shifted = z_windows(field, size_z)
    out = []
    for oy in (-1, 0, 1):
        for part in shifted:
            if oy:
                part = pltpu.roll(part, (-oy * size_z) % rows, 0)
                part = jnp.where(at_y == (size_y - 1 if oy > 0 else 0), 0.0, part)
            out.append(part)
    return out


def fill(u_ref, parts, plane=0, offset=0, stride=None):
    rows, width = parts[0].shape
    stride = width if stride is None else stride
    for t, part in enumerate(parts):
        lane = t * stride + offset
        u_ref[plane : plane + rows, lane : lane + width] = part.astype(BF)


def clear_rims(u_ref, plane):
    rows, lanes = u_ref.shape
    zero = jnp.zeros((plane, lanes), BF)
    u_ref[0:plane, :] = zero
    u_ref[rows - plane : rows, :] = zero


def moved(field, ox, oy):
    nx, ny, nz, width = field.shape
    if ox:
        rim = jnp.zeros((1, ny, nz, width), F32)
        field = jnp.concatenate([field[1:], rim] if ox > 0 else [rim, field[:-1]], 0)
    if oy:
        rim = jnp.zeros((nx, 1, nz, width), F32)
        field = jnp.concatenate([field[:, 1:], rim] if oy > 0 else [rim, field[:, :-1]], 1)
    return field


def grouped(width, extent, product):
    total = None
    for first in range(0, 9, 2):
        groups = [first, first + 1] if first < 8 else [first]
        both = product(groups)
        for i, g in enumerate(groups):
            part = both[:, i * width : (i + 1) * width].reshape(extent + (width,))
            part = moved(part, g // 3 - 1, g % 3 - 1)
            total = part if total is None else total + part
    return total.reshape(-1, width)


def conv_z(uz, w_ref, extent):
    depth = w_ref.shape[0] // 9

    def product(groups):
        side = [w_ref[g * depth : (g + 1) * depth, :] for g in groups]
        return dot(uz, side[0] if len(side) == 1 else jnp.concatenate(side, 1))

    return grouped(w_ref.shape[1], extent, product)


def conv_z_back(uz, w_ref, extent, low=0, high=None):
    every = w_ref.shape[0] // 27
    high = every if high is None else high
    width = high - low

    def product(groups):
        side = []
        for g in groups:
            taps = [(8 - g) * 3 + 2 - t for t in range(3)]
            side.append(jnp.concatenate([w_ref[p * every + low : p * every + high, :] for p in taps], 1))
        return dot_t(uz, side[0] if len(side) == 1 else jnp.concatenate(side, 0))

    return grouped(width, extent, product)


def conv(u_ref, w_ref, rows, plane):
    depth = u_ref.shape[1]
    total = None
    for ox in range(3):
        part = dot(u_ref[ox * plane : ox * plane + rows, :], w_ref[ox * depth : (ox + 1) * depth, :])
        total = part if total is None else total + part
    return total


def own_columns(field, count, position):
    shape = (count, field.shape[1])
    wanted = lax.broadcasted_iota(jnp.int32, shape, 0) + position * count
    pick = (lax.broadcasted_iota(jnp.int32, shape, 1) == wanted).astype(F32).astype(BF)
    return dot_t(pick, field)


def tap_shifts(grad, extent, depths=(-1, 0, 1)):
    nx, ny, nz = extent
    count, rows = grad.shape
    place = lax.broadcasted_iota(jnp.int32, grad.shape, 1)
    at = (over(place, ny * nz), mod(over(place, nz), ny), mod(place, nz))
    parts = []
    for ox in (-1, 0, 1):
        for oy in (-1, 0, 1):
            for oz in depths:
                by = ((ox * ny) + oy) * nz + oz
                part = pltpu.roll(grad, by % rows, 1) if by else grad
                inside = None
                for index, size, o in zip(at, extent, (ox, oy, oz)):
                    if o:
                        here = index != (0 if o > 0 else size - 1)
                        inside = here if inside is None else inside & here
                parts.append(part if inside is None else jnp.where(inside, part, 0.0))
    return jnp.concatenate(parts, 0).astype(BF)


def tap_grad(grad, field, extent):
    return dot(tap_shifts(grad, extent), field)


def split(pack, keep_ref, send_ref, core):
    size = send_ref.shape[0]
    keep_ref[0:size, :] = pack[pl.ds(pl.multiple_of(core * size, size), size), :]
    send_ref[...] = pack[pl.ds(pl.multiple_of((1 - core) * size, size), size), :]


def emit(pack_ref, spot, grad, taps=1):
    count, width = grad.shape[0] // taps, grad.shape[1]
    at = spot
    if width == LANES:
        pack_ref[at : at + taps * count, :] = grad.astype(BF)
        return
    for tap in range(taps):
        for v in range(0, width, LANES):
            pack_ref[at : at + count, :] = grad[tap * count : (tap + 1) * count, v : v + LANES].astype(BF)
            at += count


def one_hot(ny, nz, back):
    plane = ny * nz
    shape = (2 * plane, 2 * plane)
    row = lax.broadcasted_iota(jnp.int32, shape, 1 if back else 0)
    column = lax.broadcasted_iota(jnp.int32, shape, 0 if back else 1)
    tap, at = over(row, plane // 4), mod(row, plane // 4)
    ox, oy, oz = over(tap, 4), mod(over(tap, 2), 2), mod(tap, 2)
    y, z = over(at, nz // 2), mod(at, nz // 2)
    wanted = ox * plane + (2 * y + oy) * nz + 2 * z + oz
    return (column == wanted).astype(F32).astype(BF)


def to_blocks(shuffle, field, d_ref, pairs, plane):
    width = field.shape[1]
    for i in range(pairs):
        mixed = dot(shuffle, field[i * 8 * plane : (i + 1) * 8 * plane]).astype(BF)
        for t in range(8):
            d_ref[i * plane : (i + 1) * plane, t * width : (t + 1) * width] = mixed[
                t * plane : (t + 1) * plane
            ]


def from_blocks(unshuffle, flat, pairs, plane, width):
    parts = []
    for i in range(pairs):
        rows = flat[i * plane : (i + 1) * plane]
        stacked = jnp.concatenate([rows[:, t * width : (t + 1) * width] for t in range(8)], axis=0)
        parts.append(dot(unshuffle, stacked))
    return jnp.concatenate(parts, axis=0)


def join_kernel(sx, plane, volume_hbm, cotangent_hbm, out_ref, volume_ref, arrived):
    first = pltpu.make_async_copy(volume_hbm, volume_ref, arrived.at[0])
    second = pltpu.make_async_copy(cotangent_hbm, out_ref.at[0, sx // 2 * plane :], arrived.at[1])
    first.start()
    second.start()
    first.wait()
    for i in range(sx // 2):
        pair = [volume_ref[2 * i + k].astype(F32) for k in range(2)]
        out_ref[0, i * plane : (i + 1) * plane, :] = jnp.concatenate(pair, 1).astype(BF)
    second.wait()


def stage_kernel(near_ref, sources, *refs):
    del near_ref
    *held, arrived = refs
    copies = [pltpu.make_async_copy(a, b, arrived.at[i]) for i, (a, b) in enumerate(zip(sources, held))]
    for copy in copies:
        copy.start()
    for copy in copies:
        copy.wait()


def flip_kernel(near_ref, source, held, flipped, arrived):
    del near_ref
    width = source.shape[0] // 27
    parts = [slice(i * 9 * width, (i + 1) * 9 * width) for i in range(3)]
    copies = [
        pltpu.make_async_copy(source.at[part], held.at[part], arrived.at[i]) for i, part in enumerate(parts)
    ]
    for copy in copies:
        copy.start()
    for i, copy in enumerate(copies):
        copy.wait()
        for tap in range(9 * i, 9 * i + 9):
            to = 26 - tap
            flipped[to * width : (to + 1) * width, :] = held[tap * width : (tap + 1) * width, :].T


def upper_kernel(
    geo,
    gathered,
    weights,
    own_ref,
    keep_ref,
    send_ref,
    vol_ref,
    z1_ref,
    u1,
    z2_ref,
    d_ref,
    z3_ref,
    t4_ref,
    ut,
    blocks,
    uv,
    uj,
    uc,
    joined,
    lb_ref,
    out_map,
    pack,
):
    (n, sx, ny, nz, c0, c1, c2, masks, spots) = geo
    position = lax.axis_index("space")
    w_first, w_enc, w_down, w_bottom, w_up, w_join = weights
    shuffle, unshuffle = one_hot(ny, nz, False), one_hot(ny, nz, True)
    plane, nx = ny * nz, sx * n
    rows = nx * plane
    cplane, cx = plane // 4, nx // 2
    crows = cx * cplane
    fine, coarse = (nx, ny, nz), (cx, ny // 2, nz // 2)
    for source, held in zip(gathered, masks):
        for m, mask in enumerate(held):
            blocks[lax.bitwise_xor(position, mask)] = source[m]

    lane = lax.broadcasted_iota(jnp.int32, (plane, LANES), 1)
    vol_rows = sx // 2 * plane
    planes = []
    for j in range(n):
        for i in range(sx // 2):
            pair = blocks[j, i * plane : (i + 1) * plane, :].astype(F32)
            turned = pltpu.roll(pair, c0, 1)
            planes.append(jnp.where(lane < c0, pair, turned))
            planes.append(jnp.where(lane < c0, turned, pair))
    twice = jnp.concatenate(planes, 0)
    vol_ref[...] = twice.astype(BF)
    before, middle, after = z_windows(twice, nz)
    lane = lax.broadcasted_iota(jnp.int32, (rows, LANES), 1)
    uv[:, 0:LANES] = jnp.where(lane < c0, before, middle).astype(BF)
    uv[:, LANES:] = after.astype(BF)
    z1 = conv_z(uv[:, 0 : 3 * c0], w_first, fine)
    z1_ref[...] = z1
    h1 = silu(z1)
    fill(u1, z_windows(h1.astype(F32), nz))
    z2 = conv_z(u1[...], w_enc, fine)
    z2_ref[...] = z2
    skip = silu(z2)
    joined[:, c1:] = skip
    fill(uj, z_windows(skip.astype(F32), nz), 0, c1, 2 * c1)
    to_blocks(shuffle, skip, d_ref, cx, cplane)
    z3 = dot(d_ref[...], w_down[...])
    z3_ref[...] = z3
    g1 = silu(z3)
    clear_rims(uc, cplane)
    fill(uc, yz_windows(g1.astype(F32), *coarse[1:]), cplane)
    z4 = conv(uc, w_bottom, crows, cplane)
    g2 = silu(z4)
    lifted = from_blocks(unshuffle, dot(g2, w_up[...]).astype(BF), cx, cplane, c1)
    joined[:, 0:c1] = lifted.astype(BF)
    fill(uj, z_windows(lifted, nz), 0, 0, 2 * c1)
    z7 = conv_z(uj[...], w_join, fine)
    out_map[...] = silu(z7)
    kept = sx * plane
    own_ref[...] = out_map[pl.ds(pl.multiple_of(position * kept, kept), kept), :]

    cot = jnp.concatenate([blocks[j, vol_rows:, :] for j in range(n)], 0).astype(F32)
    t7 = (cot * slope(z7)).astype(BF)
    fill(ut, z_windows(t7.astype(F32), nz))
    e_lift = conv_z_back(ut[...], w_join, fine, 0, c1).astype(BF)
    to_blocks(shuffle, e_lift, lb_ref, cx, cplane)
    e3 = dot_t(lb_ref[...], w_up[...]).astype(BF).astype(F32)
    t4 = (e3 * slope(z4)).astype(BF)
    t4_ref[...] = t4
    emit(pack, spots["up"], dot(own_columns(lb_ref[...], 8 * c1 // n, position).astype(BF), g2))
    taps = dot(tap_shifts(own_columns(t7, c1 // n, position), fine, (0,)), uj[...])
    emit(pack, spots["join"], taps, 9)
    split(pack, keep_ref, send_ref, lax.rem(lax.axis_index("section"), 2))
    at = send_ref.shape[0]
    for v in range(0, c2, LANES):
        keep_ref[at : at + crows, :] = g1[:, v : v + LANES]
        at += crows
    mine = own_columns(t4, c2 // n, position).astype(BF)
    for v in range(0, crows, LANES):
        keep_ref[at : at + c2 // n, :] = mine[:, v : v + LANES]
        at += c2 // n


def skip_kernel(extent, c1, ut, w_join, out_ref):
    out_ref[...] = conv_z_back(ut[...], w_join, extent, c1, 2 * c1)


def lower_kernel(
    geo,
    w_enc,
    w_down,
    back_bottom,
    z1_ref,
    z2_ref,
    d_ref,
    z3_ref,
    t4_ref,
    skip_back_ref,
    pack,
    t2_ref,
    t1_ref,
    utc,
    ut,
):
    (n, sx, ny, nz, c0, c1, c2, masks, spots) = geo
    position = lax.axis_index("space")
    plane, nx = ny * nz, sx * n
    cplane, cx = plane // 4, nx // 2
    crows = cx * cplane
    fine, coarse = (nx, ny, nz), (cx, ny // 2, nz // 2)
    unshuffle = one_hot(ny, nz, True)
    clear_rims(utc, cplane)
    fill(utc, yz_windows(t4_ref[...].astype(F32), *coarse[1:]), cplane)
    e4 = conv(utc, back_bottom, crows, cplane).astype(BF).astype(F32)
    t3 = (e4 * slope(z3_ref[...])).astype(BF)
    emit(pack, spots["down"], dot(own_columns(t3, c2 // n, position).astype(BF), d_ref[...]))
    e5 = dot_t(t3, w_down[...])
    high = e5.astype(BF)
    low = (e5 - high.astype(F32)).astype(BF)
    e5 = from_blocks(unshuffle, high, cx, cplane, c1) + from_blocks(
        unshuffle, low, cx, cplane, c1
    )
    t2 = ((e5 + skip_back_ref[...]) * slope(z2_ref[...])).astype(BF)
    fill(ut, z_windows(t2.astype(F32), nz))
    t2_ref[...] = t2
    e6 = conv_z_back(ut[...], w_enc, fine).astype(BF).astype(F32)
    t1_ref[...] = (e6 * slope(z1_ref[...])).astype(BF)


def first_kernel(geo, down_ref, t2_ref, t1_ref, h1_ref, vol_ref, keep_ref, send_ref, pack):
    (n, sx, ny, nz, c0, c1, c2, masks, spots) = geo
    position = lax.axis_index("space")
    fine = (sx * n, ny, nz)
    count = c1 // n
    pack[0 : down_ref.shape[0], :] = down_ref[...]
    taps = dot(tap_shifts(own_columns(t2_ref[...], count, position), fine, (0,)), h1_ref[...])
    emit(pack, spots["enc"], taps, 9)
    taps = tap_grad(own_columns(t1_ref[...], count, position), vol_ref[...], fine)
    lane = lax.broadcasted_iota(jnp.int32, (count, LANES), 1)
    at = spots["first"]
    for tap in range(0, 27, 2):
        a = taps[tap * count : (tap + 1) * count]
        b = taps[(tap + 1) * count : (tap + 2) * count] if tap < 26 else a
        pack[at : at + count, :] = jnp.where(lane < c0, a, b).astype(BF)
        at += count
    split(pack, keep_ref, send_ref, lax.rem(lax.axis_index("section"), 2))


def unpack(source, spot, out, factor):
    count, width = out.shape
    at = spot
    for v in range(0, width, LANES):
        take = min(LANES, width - v)
        out[:, v : v + take] = (source(at, count) * factor)[:, :take]
        at += count


def halves(both, mine_ref, other_ref, core):
    size = both.shape[1]
    both[core] = mine_ref[0:size, :]
    both[1 - core] = other_ref[0:size, :]

    def source(at, count):
        if (at + count - 1) // size == at // size:
            return both[at // size, at % size : at % size + count, :].astype(F32)
        cut = size - at % size
        return jnp.concatenate(
            [both[0, size - cut : size, :].astype(F32), both[1, 0 : count - cut, :].astype(F32)], 0
        )

    return source


def finish_first(factor, spots, extent, *refs):
    own_ref, mine_ref, other_ref, decoded_ref, bottom_ref, up_ref, join_ref, token, both, acts = refs
    decoded_ref[...] = own_ref[...]
    token[...] = jnp.zeros(token.shape, F32)
    section = lax.axis_index("section")
    size = both.shape[1]
    source = halves(both, mine_ref, other_ref, lax.rem(section, 2))
    unpack(source, spots["join"], join_ref, factor)
    rows, width = up_ref.shape[1], up_ref.shape[0]
    for v in range(0, width, LANES):
        up_ref[v : v + LANES, :] = (source(spots["up"] + v // LANES * rows, rows) * factor).T

    crops, each = acts.shape[0], acts.shape[1]
    for j in range(crops // 2):
        part = slice(size + j * each, size + (j + 1) * each)
        acts[lax.bitwise_xor(section, 2 * j)] = mine_ref[part, :]
        acts[lax.bitwise_xor(section, 2 * j + 1)] = other_ref[part, :]
    voxels = extent[0] * extent[1] * extent[2]
    count, wide = bottom_ref.shape[0], bottom_ref.shape[1] // 27
    shifted, fields = [], []
    for crop in range(crops):
        at = wide // LANES * voxels
        fields.append(
            jnp.concatenate([acts[crop, v : v + voxels, :] for v in range(0, at, voxels)], 1)
        )
        own = [acts[crop, v : v + count, :] for v in range(at, each, count)]
        shifted.append(tap_shifts(jnp.concatenate(own, 1).astype(F32), extent))
    grad = dot(jnp.concatenate(shifted, 1), jnp.concatenate(fields, 0)) * factor
    for tap in range(27):
        bottom_ref[:, tap * wide : (tap + 1) * wide] = grad[tap * count : (tap + 1) * count]


def finish_second(factor, spots, mine_ref, other_ref, first_ref, enc_ref, down_ref, both):
    source = halves(both, mine_ref, other_ref, lax.rem(lax.axis_index("section"), 2))
    unpack(source, spots["down"], down_ref, factor)
    unpack(source, spots["first"], first_ref, factor)
    unpack(source, spots["enc"], enc_ref, factor)


def merge_kernel(size, a_ref, b_ref, *refs):
    out_ref = refs[-1]
    out_ref[0:size, :] = (a_ref[0:size, :].astype(F32) + b_ref[0:size, :].astype(F32)).astype(BF)
    at = size
    for ref in (a_ref, b_ref):
        rest = ref.shape[0] - size
        if rest:
            out_ref[at : at + rest, :] = ref[size:, :]
            at += rest


def merge(a, b, size, *after):
    shape = (a.shape[0] + b.shape[0] - size, LANES)
    kernel = functools.partial(merge_kernel, size)
    return call(kernel, [(shape, BF)], [], (VMEM,) * (2 + len(after)), vmem=4)(a, b, *after)[0]


def between_cores(keep, send, *after):
    return merge(keep, exchange(send, "section", 1), send.shape[0], *after)


def between_chips(total, size, crops, *after):
    mask = 2
    while mask < crops:
        mask *= 2
        last = after if mask >= crops else ()
        total = merge(total, exchange(total, "section", mask // 2), size, *last)
    return total, exchange(total, "section", 1)


def in_hbm(array):
    return pltpu.with_memory_space_constraint(array, HBM)


def exchange(array, axis, mask):
    devices = lax.axis_size(axis)
    return lax.ppermute(array, axis, [(i, i ^ mask) for i in range(devices)])


def merge_kernel(size, a_ref, b_ref, *refs):
    out_ref = refs[-1]
    out_ref[0:size, :] = (a_ref[0:size, :].astype(F32) + b_ref[0:size, :].astype(F32)).astype(BF)
    at = size
    for ref in (a_ref, b_ref):
        rest = ref.shape[0] - size
        if rest:
            out_ref[at : at + rest, :] = ref[size:, :]
            at += rest


def merge(a, b, size, *after):
    shape = (a.shape[0] + b.shape[0] - size, LANES)
    kernel = functools.partial(merge_kernel, size)
    return call(kernel, [(shape, BF)], [], (VMEM,) * (2 + len(after)), vmem=4)(a, b, *after)[0]


def reduced(keep, send, crops, after=()):
    size = send.shape[0]
    total = merge(keep, exchange(send, "section", 1), size)
    mask = 2
    while mask < crops:
        mask *= 2
        total = merge(total, exchange(total, "section", mask // 2), size, *(after if mask >= crops else ()))
    return total, exchange(total, "section", 1)


def stack_kernel(a_ref, b_ref, *refs):
    out_ref = refs[-1]
    out_ref[0 : a_ref.shape[0]] = a_ref[...]
    out_ref[a_ref.shape[0] :] = b_ref[...]


def stack(a, b, *after):
    shape = (a.shape[0] + b.shape[0],) + a.shape[1:]
    return call(stack_kernel, [(shape, BF)], [], (VMEM,) * (2 + len(after)), vmem=4)(a, b, *after)[0]


def call(kernel, outs, scratch, spaces, flops=0, vmem=12):
    return pl.pallas_call(
        kernel,
        out_shape=tuple(jax.ShapeDtypeStruct(s, d) for s, d in outs),
        in_specs=jax.tree.map(lambda space: pl.BlockSpec(memory_space=space), spaces),
        out_specs=tuple(pl.BlockSpec(memory_space=VMEM) for _ in outs),
        scratch_shapes=scratch,
        compiler_params=pltpu.CompilerParams(vmem_limit_bytes=vmem * MIB),
        cost_estimate=pl.CostEstimate(flops=flops, bytes_accessed=2 * MIB, transcendentals=0),
    )


def body(volume, w_first, w_enc, w_down, w_bottom, w_up, w_join, cotangent):
    n = lax.axis_size("space")
    crops = lax.axis_size("section")
    _, sx, ny, nz, c0 = volume.shape
    c1, c2 = w_enc.shape[1], w_bottom.shape[1]
    plane, nx = ny * nz, sx * n
    rows = nx * plane
    cplane, crows = plane // 4, rows // 8
    own_rows = sx * plane // 2 + sx * plane
    (near,) = call(
        functools.partial(join_kernel, sx, plane),
        [((1, own_rows, LANES), BF)],
        [pltpu.VMEM((sx, plane, c0), BF), pltpu.SemaphoreType.DMA((2,))],
        (HBM, HBM),
        vmem=4,
    )(in_hbm(volume.reshape(sx, plane, c0)), in_hbm(cotangent.reshape(sx * plane, c1)))
    held_bottom, back_bottom = call(
        flip_kernel,
        [(w_bottom.shape, BF)] * 2,
        [pltpu.SemaphoreType.DMA((3,))],
        (VMEM, HBM),
        flops=10**9,
    )(near, in_hbm(w_bottom))
    held, step = [0], n // 2
    while step > 2:
        held = held + [m ^ step for m in held]
        near = stack(near, exchange(near, "space", step), back_bottom)
        step //= 2
    weights = [w_first, w_enc, w_down, w_up, w_join]
    weights = call(
        stage_kernel,
        [(w.shape, BF) for w in weights],
        [pltpu.SemaphoreType.DMA((len(weights),))],
        (VMEM, [HBM] * len(weights)),
        flops=10**9,
    )(near, [in_hbm(w) for w in weights])
    weights = [*weights[:3], held_bottom, *weights[3:]]
    last = [m for m in (2, 3, 1) if m < n]
    gathered = [near] + [exchange(near, "space", mask) for mask in last]
    masks = tuple(tuple(m ^ mask for m in held) for mask in (0, *last))

    fine_own, wide_own = c1 // n, c2 // n
    shapes = {
        "first": (fine_own, 27 * c0),
        "enc": (fine_own, 27 * c1),
        "down": (wide_own, 8 * c1),
        "bottom": (wide_own, 27 * c2),
        "up": (8 * c1 // n, c2),
        "join": (fine_own, 54 * c1),
    }

    def layout(names):
        spots, at = {}, 0
        for name in names:
            spots[name] = at
            count, width = shapes[name]
            at += count * -(-width // LANES)
        return spots, -(-at // 32) * 32

    upper_spots, upper_rows = layout(("up", "join"))
    lower_spots, lower_rows = layout(("down", "enc", "first"))
    geo = (n, sx, ny, nz, c0, c1, c2, masks)
    fine, coarse = (nx, ny, nz), (nx // 2, ny // 2, nz // 2)
    size = upper_rows // 2
    act_rows = c2 // LANES * crows + crows // LANES * wide_own
    own, keep, send, vol2, z1, h1, z2, blocks, z3, t4, ut = call(
        functools.partial(upper_kernel, geo + (upper_spots,)),
        [
            ((sx * plane, c1), BF),
            ((size + act_rows, LANES), BF),
            ((size, LANES), BF),
            ((rows, 2 * c0), BF),
            ((rows, c1), F32),
            ((rows, 3 * c1), BF),
            ((rows, c1), F32),
            ((crows, 8 * c1), BF),
            ((crows, c2), F32),
            ((crows, c2), BF),
            ((rows, 3 * c1), BF),
        ],
        [
            pltpu.VMEM((n, own_rows, LANES), BF),
            pltpu.VMEM((rows, 2 * LANES), BF),
            pltpu.VMEM((rows, 6 * c1), BF),
            pltpu.VMEM((crows + 2 * cplane, 9 * c2), BF),
            pltpu.VMEM((rows, 2 * c1), BF),
            pltpu.VMEM((crows, 8 * c1), BF),
            pltpu.VMEM((rows, c1), BF),
            pltpu.VMEM((upper_rows, LANES), BF),
        ],
        ([VMEM] * len(gathered), [VMEM] * len(weights)),
        flops=10**10,
        vmem=14,
    )(gathered, weights)
    (skip_back,) = call(
        functools.partial(skip_kernel, fine, c1),
        [((rows, c1), F32)],
        [],
        (VMEM, VMEM),
        flops=10**9,
    )(ut, weights[5])
    total = between_cores(keep, send, skip_back)

    low_size = lower_rows // 2
    down, t2, t1 = call(
        functools.partial(lower_kernel, geo + (lower_spots,)),
        [((lower_spots["enc"], LANES), BF), ((rows, c1), BF), ((rows, c1), BF)],
        [pltpu.VMEM((crows + 2 * cplane, 9 * c2), BF), pltpu.VMEM((rows, 3 * c1), BF)],
        (VMEM,) * 9,
        flops=6 * 10**9,
    )(weights[1], weights[2], back_bottom, z1, z2, blocks, z3, t4, skip_back)
    low_keep, low_send = call(
        functools.partial(first_kernel, geo + (lower_spots,)),
        [((low_size, LANES), BF), ((low_size, LANES), BF)],
        [pltpu.VMEM((lower_rows, LANES), BF)],
        (VMEM,) * 5,
        flops=10**9,
    )(down, t2, t1, h1, vol2)
    low_total = between_cores(low_keep, low_send)
    total, other = between_chips(total, size, crops, low_total)
    factor = 1.0 / math.sqrt(crops * rows)
    decoded, grad_bottom, grad_up, grad_join, token = call(
        functools.partial(finish_first, factor, upper_spots, coarse),
        [
            ((sx * plane, c1), BF),
            (shapes["bottom"], F32),
            (shapes["up"][::-1], F32),
            (shapes["join"], F32),
            ((8, LANES), F32),
        ],
        [pltpu.VMEM((2, size, LANES), BF), pltpu.VMEM((crops, act_rows, LANES), BF)],
        (VMEM, VMEM, VMEM),
        vmem=12,
    )(own, total, other)
    low_total, low_other = between_chips(low_total, low_size, crops, token)
    grad_first, grad_enc, grad_down = call(
        functools.partial(finish_second, factor, lower_spots),
        [(shapes[name], F32) for name in ("first", "enc", "down")],
        [pltpu.VMEM((2, low_size, LANES), BF)],
        (VMEM, VMEM),
        vmem=8,
    )(low_total, low_other)
    return (
        decoded.reshape((1, sx, ny, nz, c1)),
        grad_first.T,
        grad_enc.T,
        grad_down.T,
        grad_bottom.T,
        grad_up,
        grad_join.T,
    )


def solution(mesh):
    field = P("section", "space", None, None, None)
    split = P(None, "space")
    return jax.shard_map(
        body,
        mesh=mesh,
        in_specs=(field,) + (P(),) * 6 + (field,),
        out_specs=(field,) + (split,) * 6,
        check_vma=False,
    )
```
